32 devices in a mesh: dp: 16 (over z, x, core), ctx: 2 (over y).
Axes of the slice: x: 2, y: 2, z: 4, core: 2. Of those that a mesh axis runs over, the one named last changes fastest.
Arguments:
- inputs: bfloat16 [18688, 1024], P(('dp', 'ctx')), may hold values from -6 to 6
- cotangent: bfloat16 [18688, 1024], P(('dp', 'ctx')), may hold values from -6 to 6
- segment: int32 [18688], P(('dp', 'ctx')), may hold values from -1 to 1, as said below
- w_qkv: bfloat16 [8192, 384], P(('dp', 'ctx')), may hold values from -0.1875 to 0.1875
- b_query: bfloat16 [1024], P(('dp', 'ctx')), may hold values from -4 to 4
- b_value: bfloat16 [1024], P(('dp', 'ctx')), may hold values from -0.4375 to 0.4375
- w_out: bfloat16 [8192, 128], P(('dp', 'ctx')), may hold values from -6 to 6
- b_out: bfloat16 [1024], P(('dp', 'ctx')), may hold values from -4 to 4
- norm1_gain: bfloat16 [1024], P(('dp', 'ctx')), may hold values from 0.5 to 1.5
- norm1_shift: bfloat16 [1024], P(('dp', 'ctx')), may hold values from -4 to 4
- norm2_gain: bfloat16 [1024], P(('dp', 'ctx')), may hold values from 0.5 to 1.5
- norm2_shift: bfloat16 [1024], P(('dp', 'ctx')), may hold values from -4 to 4
- w_up: bfloat16 [8192, 512], P(('dp', 'ctx')), may hold values from -0.1875 to 0.1875
- b_up: bfloat16 [4096], P(('dp', 'ctx')), may hold values from -4 to 4
- w_down: bfloat16 [32768, 128], P(('dp', 'ctx')), may hold values from -0.1875 to 0.1875
- b_down: bfloat16 [1024], P(('dp', 'ctx')), may hold values from -4 to 4
Outputs:
- outputs: bfloat16 [18688, 1024], P(('dp', 'ctx'))
- input_grad: float32 [18688, 1024], P(('dp', 'ctx'))
- grad_w_qkv: float32 [8192, 384], P(('dp', 'ctx'))
- grad_b_query: float32 [1024], P(('dp', 'ctx'))
- grad_b_value: float32 [1024], P(('dp', 'ctx'))
- grad_w_out: float32 [8192, 128], P(('dp', 'ctx'))
- grad_b_out: float32 [1024], P(('dp', 'ctx'))
- grad_norm1_gain: float32 [1024], P(('dp', 'ctx'))
- grad_norm1_shift: float32 [1024], P(('dp', 'ctx'))
- grad_norm2_gain: float32 [1024], P(('dp', 'ctx'))
- grad_norm2_shift: float32 [1024], P(('dp', 'ctx'))
- grad_w_up: float32 [8192, 512], P(('dp', 'ctx'))
- grad_b_up: float32 [4096], P(('dp', 'ctx'))
- grad_w_down: float32 [32768, 128], P(('dp', 'ctx'))
- grad_b_down: float32 [1024], P(('dp', 'ctx'))
The draws below stay inside these ranges and needn't reach their ends.
Inputs may be any that keep to these rules, and one draw needn't show every extreme that they name: `segment`: each block of 1168 consecutive token slots holds 2 images of 577 tokens each, numbered 0 to 1, their slots in a drawn order over the whole block; the remaining slots are padding with id -1.
All inputs are finite; a program needn't handle non-finite values.
Results may differ from the reference program's by a relative error of at most 0.024.
Values may be sent and summed in bfloat16 or wider, within the bound.
No kernel may reach another device: no remote copies, remote signals or barrier semaphores. Data moves between devices by JAX's collectives and lax.ppermute only.
A program may use at most 384 MiB of HBM per device.

```python
import math
import jax
import jax.numpy as jnp
from jax import lax

D = 1024
HD = 64
FF = 4096
SEQ = 577
IMAGES = 2
TOK_DEV = 584
GROUP = 1168
TOKENS = 18688
N_CTX = 2


def draw_segment(key, part):
    key = jax.random.fold_in(key, 7)
    group_count = TOKENS // GROUP
    images = jnp.repeat(jnp.arange(IMAGES, dtype=jnp.int32), SEQ)
    padding = jnp.full((GROUP - IMAGES * SEQ,), -1, dtype=jnp.int32)
    base = jnp.concatenate([images, padding])
    group_keys = jax.random.split(key, group_count)
    shuffled = jax.vmap(lambda one_key: jax.random.permutation(one_key, base))(group_keys)
    return shuffled.reshape(-1).astype(jnp.int32)


def levels(key, dims, cuts, least, largest):
    level, own = 1.0, jax.random.fold_in(key, 6)
    for position, blocks in cuts:
        heights = jnp.exp(jax.random.uniform(jax.random.fold_in(own, position), (blocks,), jnp.float32, least / len(cuts), largest / len(cuts)))
        level = level * jnp.repeat(heights, dims[position] // blocks).reshape([-1 if axis == position else 1 for axis in range(len(dims))])
    return level


def gaussian(stream_key, extent, width, most, shards=(), kind=jnp.bfloat16):
    values = jax.random.normal(stream_key, extent, jnp.float32) * width
    if len(shards) > 0:
        values = levels(stream_key, extent, shards, -0.22, 0.18) * values
    return jnp.clip(values, min=-most, max=most).astype(kind)


def setup_inputs(seed: int = 0) -> dict:
    seeds = jax.random.split(jax.random.key(seed), 17)
    inputs = gaussian(seeds[0], (TOKENS, D), 1.0, 6.0, ((0, 32),))
    cotangent = gaussian(seeds[1], (TOKENS, D), 1.0, 6.0, ((0, 32),))
    segment = draw_segment(jax.random.fold_in(seeds[16], 71), 0)
    w_qkv = gaussian(seeds[3], (8 * D, 3 * D // 8), D ** -0.5, 0.1875, ((0, 32),))
    b_query = gaussian(seeds[4], (D,), 0.3, 4.0, ((0, 32),))
    b_value = gaussian(seeds[5], (D,), 0.03, 0.4375, ((0, 32),))
    w_out = gaussian(seeds[6], (8 * D, D // 8), (max(D // SEQ, 1)) ** -0.5, 6.0, ((0, 32),))
    b_out = gaussian(seeds[7], (D,), 0.3, 4.0, ((0, 32),))
    norm1_gain = jnp.clip(1.0 + 0.1 * jax.random.normal(seeds[8], (D,), jnp.float32), 0.5, 1.5).astype(jnp.bfloat16)
    norm1_shift = gaussian(seeds[9], (D,), 0.3, 4.0, ((0, 32),))
    norm2_gain = jnp.clip(1.0 + 0.1 * jax.random.normal(seeds[10], (D,), jnp.float32), 0.5, 1.5).astype(jnp.bfloat16)
    norm2_shift = gaussian(seeds[11], (D,), 0.3, 4.0, ((0, 32),))
    w_up = gaussian(seeds[12], (8 * D, FF // 8), D ** -0.5, 0.1875, ((0, 32),))
    b_up = gaussian(seeds[13], (FF,), 0.3, 4.0, ((0, 32),))
    w_down = gaussian(seeds[14], (8 * FF, D // 8), (FF // 4) ** -0.5, 0.1875, ((0, 32),))
    b_down = gaussian(seeds[15], (D,), 0.3, 4.0, ((0, 32),))
    return dict(inputs=inputs, cotangent=cotangent, segment=segment, w_qkv=w_qkv, b_query=b_query, b_value=b_value, w_out=w_out, b_out=b_out, norm1_gain=norm1_gain, norm1_shift=norm1_shift, norm2_gain=norm2_gain, norm2_shift=norm2_shift, w_up=w_up, b_up=b_up, w_down=w_down, b_down=b_down)


EPSILON = 1e-06
HIGH = lax.Precision.HIGHEST

@jax.custom_vjp
def low(v):
    return lax.optimization_barrier(v.astype(jnp.bfloat16)).astype(jnp.float32)

@jax.custom_vjp
def low_back(v):
    return v

def low_keep(v):
    return (low(v), None)

def low_pass(kept, grad):
    return (grad,)

def back_keep(v):
    return (v, None)

def back_low(kept, grad):
    return (low(grad),)
low.defvjp(low_keep, low_pass)
low_back.defvjp(back_keep, back_low)

def matmul(left, right):
    return jnp.dot(left, right, precision=HIGH, preferred_element_type=jnp.float32)

def unfold(stored):
    return stored.reshape(stored.shape[0] // 8, stored.shape[1] * 8)

def refold(matrix):
    return matrix.reshape(matrix.shape[0] * 8, matrix.shape[1] // 8)

def layer_norm(value, gain, shift):
    center = value - lax.optimization_barrier(jnp.mean(value, axis=-1, keepdims=True))
    variance = lax.optimization_barrier(jnp.mean(center * center, axis=-1, keepdims=True))
    return center * lax.rsqrt(variance + EPSILON) * gain + shift

def layer(values_in, group_seg, w_qkv, b_query, b_value, w_out, b_out, norm1_gain, norm1_shift, norm2_gain, norm2_shift, w_up, b_up, w_down, b_down):
    token_count = values_in.shape[0]
    model_width = w_out.shape[0]
    head_count = model_width // HD
    normed1 = low(layer_norm(values_in, norm1_gain, norm1_shift))
    joined = matmul(normed1, w_qkv)
    queries = low(low_back(joined[:, :model_width] + b_query)).reshape(token_count, head_count, HD)
    key_rows = low(low_back(joined[:, model_width:2 * model_width])).reshape(token_count, head_count, HD)
    value_rows = low(low_back(joined[:, 2 * model_width:] + b_value)).reshape(token_count, head_count, HD)
    scores = low_back(jnp.einsum('qhd,khd->hqk', queries, key_rows, precision=HIGH) * (1.0 / math.sqrt(HD)))
    same_seg = group_seg[:, None] == group_seg[None, :]
    scores = jnp.where(same_seg[None], scores, -1e+30)
    probs_low = low(jax.nn.softmax(scores, axis=-1))
    mixed = jnp.einsum('hqk,khd->qhd', probs_low, value_rows, precision=HIGH).reshape(token_count, model_width)
    attended = low(low_back(mixed))
    branch = low_back(matmul(attended, w_out) + b_out)
    middle = values_in + branch
    normed2 = low(layer_norm(middle, norm2_gain, norm2_shift))
    hidden = low_back(matmul(normed2, w_up) + b_up)
    active = low(jax.nn.gelu(hidden, approximate=False))
    branch_two = low_back(matmul(active, w_down) + b_down)
    return middle + branch_two

def reference(inputs, cotangent, segment, w_qkv, b_query, b_value, w_out, b_out, norm1_gain, norm1_shift, norm2_gain, norm2_shift, w_up, b_up, w_down, b_down):
    params = (unfold(w_qkv.astype(jnp.float32)), b_query.astype(jnp.float32), b_value.astype(jnp.float32), unfold(w_out.astype(jnp.float32)), b_out.astype(jnp.float32), norm1_gain.astype(jnp.float32), norm1_shift.astype(jnp.float32), norm2_gain.astype(jnp.float32), norm2_shift.astype(jnp.float32), unfold(w_up.astype(jnp.float32)), b_up.astype(jnp.float32), unfold(w_down.astype(jnp.float32)), b_down.astype(jnp.float32))
    group_size = TOK_DEV * N_CTX
    group_count = inputs.shape[0] // group_size
    stacked = (inputs.astype(jnp.float32).reshape(group_count, group_size, D), cotangent.astype(jnp.float32).reshape(group_count, group_size, D), segment.reshape(group_count, group_size))

    def one_group(totals, item):
        group_in, group_cot, group_seg = item

        def forward(values_in, *weights):
            return layer(values_in, group_seg, *weights)
        result, pull = jax.vjp(forward, group_in, *params)
        valid = (group_seg >= 0).astype(jnp.float32)[:, None]
        grads = pull(group_cot * valid)
        totals = tuple((total + grad for total, grad in zip(totals, grads[1:])))
        return (totals, (result.astype(jnp.bfloat16), grads[0]))
    zeros = tuple((jnp.zeros_like(param) for param in params))
    totals, (results, input_grads) = lax.scan(one_group, zeros, stacked)
    return (results.reshape(-1, D), input_grads.reshape(-1, D), refold(totals[0]), totals[1], totals[2], refold(totals[3]), totals[4], totals[5], totals[6], totals[7], totals[8], refold(totals[9]), totals[10], refold(totals[11]), totals[12])
```

```python
import math

import jax
import jax.numpy as jnp
from jax import lax
from jax.experimental import pallas as pl
from jax.experimental.pallas import tpu as pltpu
from jax.sharding import PartitionSpec as P

HD = 64


EPSILON = 1e-06


def layer_norm(value, gain, shift):
    center = value - jnp.mean(value, axis=-1, keepdims=True)
    variance = jnp.mean(center * center, axis=-1, keepdims=True)
    return center * lax.rsqrt(variance + EPSILON) * gain + shift


def gelu_exact(value):
    return jax.nn.gelu(value, approximate=False)


def matmul(left, right):
    return jnp.dot(left, right, preferred_element_type=jnp.float32)


def unfold(stored):
    return stored.reshape(stored.shape[0] // 8, stored.shape[1] * 8)


def refold(matrix):
    return matrix.reshape(matrix.shape[0] * 8, matrix.shape[1] // 8)


def on_device(
    inputs,
    cotangent,
    segment,
    w_qkv,
    b_query,
    b_value,
    w_out,
    b_out,
    norm1_gain,
    norm1_shift,
    norm2_gain,
    norm2_shift,
    w_up,
    b_up,
    w_down,
    b_down,
):
    gathered = (
        lax.all_gather(w_qkv, ("dp", "ctx"), axis=0, tiled=True),
        lax.all_gather(b_query, ("dp", "ctx"), axis=0, tiled=True),
        lax.all_gather(b_value, ("dp", "ctx"), axis=0, tiled=True),
        lax.all_gather(w_out, ("dp", "ctx"), axis=0, tiled=True),
        lax.all_gather(b_out, ("dp", "ctx"), axis=0, tiled=True),
        lax.all_gather(norm1_gain, ("dp", "ctx"), axis=0, tiled=True),
        lax.all_gather(norm1_shift, ("dp", "ctx"), axis=0, tiled=True),
        lax.all_gather(norm2_gain, ("dp", "ctx"), axis=0, tiled=True),
        lax.all_gather(norm2_shift, ("dp", "ctx"), axis=0, tiled=True),
        lax.all_gather(w_up, ("dp", "ctx"), axis=0, tiled=True),
        lax.all_gather(b_up, ("dp", "ctx"), axis=0, tiled=True),
        lax.all_gather(w_down, ("dp", "ctx"), axis=0, tiled=True),
        lax.all_gather(b_down, ("dp", "ctx"), axis=0, tiled=True),
    )
    (
        qkv_stored,
        query_bias,
        value_bias,
        out_stored,
        out_bias,
        gain_one,
        shift_one,
        gain_two,
        shift_two,
        up_stored,
        up_bias,
        down_stored,
        down_bias,
    ) = gathered
    qkv_weight = unfold(qkv_stored)
    out_weight = unfold(out_stored)
    up_weight = unfold(up_stored)
    down_weight = unfold(down_stored)
    first_gain = gain_one.astype(jnp.float32)
    first_shift = shift_one.astype(jnp.float32)
    second_gain = gain_two.astype(jnp.float32)
    second_shift = shift_two.astype(jnp.float32)
    row_count = inputs.shape[0]
    model_width = out_weight.shape[0]
    head_count = model_width // HD
    score_scale = 1.0 / math.sqrt(HD)
    values_in = inputs.astype(jnp.float32)
    normed1 = layer_norm(values_in, first_gain, first_shift).astype(jnp.bfloat16)
    joined = matmul(normed1, qkv_weight)
    queries = (joined[:, :model_width] + query_bias.astype(jnp.float32)).astype(jnp.bfloat16)
    key_rows = joined[:, model_width : 2 * model_width].astype(jnp.bfloat16)
    value_rows = (joined[:, 2 * model_width :] + value_bias.astype(jnp.float32)).astype(
        jnp.bfloat16
    )
    key_all, value_all, seg_all = (
        lax.all_gather(key_rows, "ctx", axis=0, tiled=True),
        lax.all_gather(value_rows, "ctx", axis=0, tiled=True),
        lax.all_gather(segment.astype(jnp.bfloat16), "ctx", axis=0, tiled=True),
    )
    key_count = key_all.shape[0]
    query_heads = queries.reshape(row_count, head_count, HD)
    key_heads = key_all.reshape(key_count, head_count, HD)
    value_heads = value_all.reshape(key_count, head_count, HD)
    own_seg = segment.astype(jnp.float32)
    group_seg = seg_all.astype(jnp.float32)
    same_seg = own_seg[:, None] == group_seg[None, :]

    def make_scores():
        raw = (
            jnp.einsum("qhd,khd->hqk", query_heads, key_heads, preferred_element_type=jnp.float32)
            * score_scale
        )
        return jnp.where(same_seg[None], raw, -1e30)

    scores = make_scores()
    row_max = jnp.max(scores, axis=-1, keepdims=True)
    expo = jnp.exp(scores - row_max)
    row_total = jnp.sum(expo, axis=-1, keepdims=True)
    probs_low = (expo / row_total).astype(jnp.bfloat16)
    log_total = row_max + jnp.log(row_total)
    mixed = jnp.einsum("hqk,khd->qhd", probs_low, value_heads, preferred_element_type=jnp.float32)
    attended = mixed.reshape(row_count, model_width).astype(jnp.bfloat16)
    middle = values_in + matmul(attended, out_weight) + out_bias.astype(jnp.float32)
    normed2 = layer_norm(middle, second_gain, second_shift).astype(jnp.bfloat16)
    hidden = matmul(normed2, up_weight) + up_bias.astype(jnp.float32)
    active = gelu_exact(hidden).astype(jnp.bfloat16)
    outputs = (middle + matmul(active, down_weight) + down_bias.astype(jnp.float32)).astype(
        jnp.bfloat16
    )
    back_qkv, back_out, back_up, back_down = (qkv_weight, out_weight, up_weight, down_weight)
    valid = (segment >= 0).astype(jnp.float32)[:, None]
    d_out = cotangent.astype(jnp.float32) * valid
    d_out_low = d_out.astype(jnp.bfloat16)
    grad_down = refold(matmul(active.T, d_out_low))
    grad_down_bias = jnp.sum(d_out_low.astype(jnp.float32), axis=0)
    d_active = matmul(d_out_low, back_down.T)
    gelu_value, gelu_pull = jax.vjp(gelu_exact, hidden)
    d_hidden = gelu_pull(d_active)[0].astype(jnp.bfloat16)
    grad_up = refold(matmul(normed2.T, d_hidden))
    grad_up_bias = jnp.sum(d_hidden.astype(jnp.float32), axis=0)
    d_normed2 = matmul(d_hidden, back_up.T)
    norm_value, norm_pull = jax.vjp(layer_norm, middle, second_gain, second_shift)
    d_middle_norm, grad_gain_two, grad_shift_two = norm_pull(d_normed2)
    d_middle = d_out + d_middle_norm
    d_branch = d_middle.astype(jnp.bfloat16)
    grad_out = refold(matmul(attended.T, d_branch))
    grad_out_bias = jnp.sum(d_branch.astype(jnp.float32), axis=0)
    d_attended_flat = matmul(d_branch, back_out.T).astype(jnp.bfloat16)
    d_attended = d_attended_flat.reshape(row_count, head_count, HD)
    scores = make_scores()
    probs = jnp.exp(scores - log_total)
    d_probs = jnp.einsum(
        "qhd,khd->hqk", d_attended, value_heads, preferred_element_type=jnp.float32
    )
    delta_rows = jnp.sum(probs * d_probs, axis=-1, keepdims=True)
    d_scores = (probs * (d_probs - delta_rows)).astype(jnp.bfloat16)
    d_query = (
        jnp.einsum("hqk,khd->qhd", d_scores, key_heads, preferred_element_type=jnp.float32)
        * score_scale
    ).reshape(row_count, model_width)
    probs_again = probs.astype(jnp.bfloat16)
    d_key_all = (
        jnp.einsum("hqk,qhd->khd", d_scores, query_heads, preferred_element_type=jnp.float32)
        * score_scale
    ).reshape(key_count, model_width)
    d_value_all = jnp.einsum(
        "hqk,qhd->khd", probs_again, d_attended, preferred_element_type=jnp.float32
    ).reshape(key_count, model_width)
    d_key, d_value = (
        lax.psum_scatter(
            d_key_all.astype(jnp.bfloat16), "ctx", scatter_dimension=0, tiled=True
        ).astype(jnp.float32),
        lax.psum_scatter(
            d_value_all.astype(jnp.bfloat16), "ctx", scatter_dimension=0, tiled=True
        ).astype(jnp.float32),
    )
    d_query_low = d_query.astype(jnp.bfloat16)
    d_value_low = d_value.astype(jnp.bfloat16)
    d_joined = jnp.concatenate([d_query_low, d_key.astype(jnp.bfloat16), d_value_low], axis=1)
    grad_qkv = refold(matmul(normed1.T, d_joined))
    grad_query_bias = jnp.sum(d_query_low.astype(jnp.float32), axis=0)
    grad_value_bias = jnp.sum(d_value_low.astype(jnp.float32), axis=0)
    d_normed1 = matmul(d_joined, back_qkv.T)
    first_value, first_pull = jax.vjp(layer_norm, values_in, first_gain, first_shift)
    d_input_norm, grad_gain_one, grad_shift_one = first_pull(d_normed1)
    input_grad = d_middle + d_input_norm
    partial_sums = (
        lax.psum_scatter(
            grad_qkv.astype(jnp.bfloat16), "dp", scatter_dimension=0, tiled=True
        ).astype(jnp.float32),
        lax.psum_scatter(
            grad_query_bias.astype(jnp.bfloat16), "dp", scatter_dimension=0, tiled=True
        ).astype(jnp.float32),
        lax.psum_scatter(
            grad_value_bias.astype(jnp.bfloat16), "dp", scatter_dimension=0, tiled=True
        ).astype(jnp.float32),
        lax.psum_scatter(
            grad_out.astype(jnp.bfloat16), "dp", scatter_dimension=0, tiled=True
        ).astype(jnp.float32),
        lax.psum_scatter(
            grad_out_bias.astype(jnp.bfloat16), "dp", scatter_dimension=0, tiled=True
        ).astype(jnp.float32),
        lax.psum_scatter(
            grad_gain_one.astype(jnp.bfloat16), "dp", scatter_dimension=0, tiled=True
        ).astype(jnp.float32),
        lax.psum_scatter(
            grad_shift_one.astype(jnp.bfloat16), "dp", scatter_dimension=0, tiled=True
        ).astype(jnp.float32),
        lax.psum_scatter(
            grad_gain_two.astype(jnp.bfloat16), "dp", scatter_dimension=0, tiled=True
        ).astype(jnp.float32),
        lax.psum_scatter(
            grad_shift_two.astype(jnp.bfloat16), "dp", scatter_dimension=0, tiled=True
        ).astype(jnp.float32),
        lax.psum_scatter(
            grad_up.astype(jnp.bfloat16), "dp", scatter_dimension=0, tiled=True
        ).astype(jnp.float32),
        lax.psum_scatter(
            grad_up_bias.astype(jnp.bfloat16), "dp", scatter_dimension=0, tiled=True
        ).astype(jnp.float32),
        lax.psum_scatter(
            grad_down.astype(jnp.bfloat16), "dp", scatter_dimension=0, tiled=True
        ).astype(jnp.float32),
        lax.psum_scatter(
            grad_down_bias.astype(jnp.bfloat16), "dp", scatter_dimension=0, tiled=True
        ).astype(jnp.float32),
    )
    all_sums = (
        lax.psum_scatter(
            partial_sums[0].astype(jnp.bfloat16), "ctx", scatter_dimension=0, tiled=True
        ).astype(jnp.float32),
        lax.psum_scatter(
            partial_sums[1].astype(jnp.bfloat16), "ctx", scatter_dimension=0, tiled=True
        ).astype(jnp.float32),
        lax.psum_scatter(
            partial_sums[2].astype(jnp.bfloat16), "ctx", scatter_dimension=0, tiled=True
        ).astype(jnp.float32),
        lax.psum_scatter(
            partial_sums[3].astype(jnp.bfloat16), "ctx", scatter_dimension=0, tiled=True
        ).astype(jnp.float32),
        lax.psum_scatter(
            partial_sums[4].astype(jnp.bfloat16), "ctx", scatter_dimension=0, tiled=True
        ).astype(jnp.float32),
        lax.psum_scatter(
            partial_sums[5].astype(jnp.bfloat16), "ctx", scatter_dimension=0, tiled=True
        ).astype(jnp.float32),
        lax.psum_scatter(
            partial_sums[6].astype(jnp.bfloat16), "ctx", scatter_dimension=0, tiled=True
        ).astype(jnp.float32),
        lax.psum_scatter(
            partial_sums[7].astype(jnp.bfloat16), "ctx", scatter_dimension=0, tiled=True
        ).astype(jnp.float32),
        lax.psum_scatter(
            partial_sums[8].astype(jnp.bfloat16), "ctx", scatter_dimension=0, tiled=True
        ).astype(jnp.float32),
        lax.psum_scatter(
            partial_sums[9].astype(jnp.bfloat16), "ctx", scatter_dimension=0, tiled=True
        ).astype(jnp.float32),
        lax.psum_scatter(
            partial_sums[10].astype(jnp.bfloat16), "ctx", scatter_dimension=0, tiled=True
        ).astype(jnp.float32),
        lax.psum_scatter(
            partial_sums[11].astype(jnp.bfloat16), "ctx", scatter_dimension=0, tiled=True
        ).astype(jnp.float32),
        lax.psum_scatter(
            partial_sums[12].astype(jnp.bfloat16), "ctx", scatter_dimension=0, tiled=True
        ).astype(jnp.float32),
    )
    (
        sum_qkv,
        sum_query_bias,
        sum_value_bias,
        sum_out,
        sum_out_bias,
        sum_gain_one,
        sum_shift_one,
        sum_gain_two,
        sum_shift_two,
        sum_up,
        sum_up_bias,
        sum_down,
        sum_down_bias,
    ) = all_sums
    return (
        outputs,
        input_grad,
        sum_qkv,
        sum_query_bias,
        sum_value_bias,
        sum_out,
        sum_out_bias,
        sum_gain_one,
        sum_shift_one,
        sum_gain_two,
        sum_shift_two,
        sum_up,
        sum_up_bias,
        sum_down,
        sum_down_bias,
    )


SEQ = 577
IMAGES = 2
PAIR = 2 * HD
CHUNK = 256


def round_up(count, unit):
    return -(-count // unit) * unit


def chunks_of(count):
    return [(start, min(CHUNK, count - start)) for start in range(0, count, CHUNK)]


def nt_dot(left, right):
    return lax.dot_general(
        left, right, (((1,), (1,)), ((), ())), preferred_element_type=jnp.float32
    )


def half_mask(rows):
    return lax.broadcasted_iota(jnp.int32, (rows, PAIR), 1) < HD


def forward_kernel(query_ref, key_ref, value_ref, bias_ref, attended_ref, log_ref):
    rows = query_ref.shape[0]
    first = half_mask(rows)
    zero = jnp.zeros((rows, PAIR), jnp.bfloat16)
    key = key_ref[...]
    key_sides = (jnp.where(first, key, zero), jnp.where(first, zero, key))
    value_t = value_ref[...].astype(jnp.float32).T.astype(jnp.bfloat16)
    scale = jnp.bfloat16(1.0 / math.sqrt(HD))
    for start, size in chunks_of(rows):
        query = query_ref[start : start + size, :] * scale
        bias = bias_ref[:, start : start + size]
        outs = []
        for side in range(2):
            scores = nt_dot(key_sides[side], query) + bias
            top = jnp.max(scores, axis=0, keepdims=True)
            expo = jnp.exp(scores - top)
            total = jnp.sum(expo, axis=0, keepdims=True)
            probs_low = (expo * (1.0 / total)).astype(jnp.bfloat16)
            outs.append(matmul(value_t[side * HD : (side + 1) * HD, :], probs_low))
            log_ref[0, side : side + 1, start : start + size] = top + jnp.log(total)
        mixed = jnp.concatenate(outs, axis=0)
        attended_ref[start : start + size, :] = mixed.T.astype(jnp.bfloat16)


def backward_kernel(
    query_ref, key_ref, value_ref, d_ref, log_ref, bias_ref, dq_ref, dk_ref, dv_ref, dk_sum, dv_sum
):
    rows = query_ref.shape[0]
    first = half_mask(rows)
    zero = jnp.zeros((rows, PAIR), jnp.bfloat16)
    key = key_ref[...]
    value = value_ref[...]
    key_sides = (jnp.where(first, key, zero), jnp.where(first, zero, key))
    value_sides = (jnp.where(first, value, zero), jnp.where(first, zero, value))
    key_t = key.astype(jnp.float32).T.astype(jnp.bfloat16)
    scale = jnp.bfloat16(1.0 / math.sqrt(HD))
    for start, size in chunks_of(rows):
        query = query_ref[start : start + size, :] * scale
        d_rows = d_ref[start : start + size, :]
        bias = bias_ref[:, start : start + size]
        outs = []
        for side in range(2):
            scores = nt_dot(key_sides[side], query) + bias
            probs = jnp.exp(scores - log_ref[0, side : side + 1, start : start + size])
            d_probs = nt_dot(value_sides[side], d_rows)
            product = probs * d_probs
            delta = jnp.sum(product, axis=0, keepdims=True)
            d_scores = (product - probs * delta).astype(jnp.bfloat16)
            d_value = matmul(probs.astype(jnp.bfloat16), d_rows)
            d_key = matmul(d_scores, query)
            if start == 0:
                dv_sum[side] = d_value
                dk_sum[side] = d_key
            else:
                dv_sum[side] += d_value
                dk_sum[side] += d_key
            outs.append(matmul(key_t[side * HD : (side + 1) * HD, :], d_scores))
        d_query = jnp.concatenate(outs, axis=0) * (1.0 / math.sqrt(HD))
        dq_ref[start : start + size, :] = d_query.T.astype(jnp.bfloat16)
    dk_ref[...] = jnp.where(first, dk_sum[0], dk_sum[1]).astype(jnp.bfloat16)
    dv_ref[...] = jnp.where(first, dv_sum[0], dv_sum[1]).astype(jnp.bfloat16)


def attention_forward(joined, bias):
    rows, width = joined.shape[0], joined.shape[1] // 3
    pairs = width // PAIR
    flops = 4 * rows * rows * width
    return pl.pallas_call(
        forward_kernel,
        grid=(pairs,),
        in_specs=[
            pl.BlockSpec((rows, PAIR), lambda i: (0, i)),
            pl.BlockSpec((rows, PAIR), lambda i: (0, pairs + i)),
            pl.BlockSpec((rows, PAIR), lambda i: (0, 2 * pairs + i)),
            pl.BlockSpec((rows, rows), lambda i: (0, 0)),
        ],
        out_specs=[
            pl.BlockSpec((rows, PAIR), lambda i: (0, i)),
            pl.BlockSpec((1, 2, rows), lambda i: (i, 0, 0)),
        ],
        out_shape=[
            jax.ShapeDtypeStruct((rows, width), jnp.bfloat16),
            jax.ShapeDtypeStruct((pairs, 2, rows), jnp.float32),
        ],
        compiler_params=pltpu.CompilerParams(vmem_limit_bytes=40 * 2**20),
        cost_estimate=pl.CostEstimate(
            flops=4 * flops, bytes_accessed=8 * rows * width, transcendentals=rows * rows * 16
        ),
        name="attention_forward",
    )(joined, joined, joined, bias)


def attention_backward(joined, d_attended, log_total, bias):
    rows, width = d_attended.shape
    pairs = width // PAIR
    flops = 10 * rows * rows * width
    block = jax.ShapeDtypeStruct((rows, width), jnp.bfloat16)
    return pl.pallas_call(
        backward_kernel,
        grid=(pairs,),
        in_specs=[
            pl.BlockSpec((rows, PAIR), lambda i: (0, i)),
            pl.BlockSpec((rows, PAIR), lambda i: (0, pairs + i)),
            pl.BlockSpec((rows, PAIR), lambda i: (0, 2 * pairs + i)),
            pl.BlockSpec((rows, PAIR), lambda i: (0, i)),
            pl.BlockSpec((1, 2, rows), lambda i: (i, 0, 0)),
            pl.BlockSpec((rows, rows), lambda i: (0, 0)),
        ],
        out_specs=[pl.BlockSpec((rows, PAIR), lambda i: (0, i))] * 3,
        out_shape=[block] * 3,
        scratch_shapes=[pltpu.VMEM((2, rows, PAIR), jnp.float32)] * 2,
        compiler_params=pltpu.CompilerParams(vmem_limit_bytes=40 * 2**20),
        cost_estimate=pl.CostEstimate(
            flops=4 * flops, bytes_accessed=14 * rows * width, transcendentals=rows * rows * 16
        ),
        name="attention_backward",
    )(joined, joined, joined, d_attended, log_total, bias)


def standardize(value):
    center = value - jnp.mean(value, axis=-1, keepdims=True)
    variance = jnp.mean(center * center, axis=-1, keepdims=True)
    scale = lax.rsqrt(variance + EPSILON)
    return center * scale, scale


def norm_backward(d_normed, normal, scale, gain):
    scaled = d_normed * gain
    mean = jnp.mean(scaled, axis=-1, keepdims=True)
    along = jnp.mean(scaled * normal, axis=-1, keepdims=True)
    return (scaled - mean - normal * along) * scale


def gelu_slope(value):
    phi = 0.5 * (1.0 + lax.erf(value * math.sqrt(0.5)))
    return phi + value * jnp.exp(-0.5 * value * value) * (1.0 / math.sqrt(2.0 * math.pi))


def by_core(array, axis, chips):
    shape = array.shape
    cut = shape[:axis] + (chips, 2, shape[axis] // (2 * chips)) + shape[axis + 1 :]
    return jnp.swapaxes(array.reshape(cut), axis, axis + 1).reshape(shape)


def by_chip(array, axis, chips):
    shape = array.shape
    cut = shape[:axis] + (2, chips, shape[axis] // (2 * chips)) + shape[axis + 1 :]
    return jnp.swapaxes(array.reshape(cut), axis, axis + 1).reshape(shape)


def gather_rows(shard):
    near = lax.all_gather(shard, ("chip", "ctx"), axis=0, tiled=True)
    return lax.all_gather(near, "core", axis=0, tiled=True)


def scatter_rows(matrix):
    near = lax.psum_scatter(
        matrix.astype(jnp.bfloat16), "core", scatter_dimension=0, tiled=True
    )
    return lax.psum_scatter(near, ("chip", "ctx"), scatter_dimension=0, tiled=True)


def column_sums(array):
    return jnp.sum(array.astype(jnp.float32), axis=0)


def by_image(chips):
    def on_device(
        inputs,
        cotangent,
        segment,
        w_qkv,
        b_query,
        b_value,
        w_out,
        b_out,
        norm1_gain,
        norm1_shift,
        norm2_gain,
        norm2_shift,
        w_up,
        b_up,
        w_down,
        b_down,
    ):
        place = lax.axis_index("ctx")
        swap = lambda array: lax.ppermute(array, "ctx", [(0, 1), (1, 0)])
        slots, width = inputs.shape
        pads = 2 * slots - IMAGES * SEQ
        rows = round_up(SEQ + pads, 16)
        near_width = w_up.shape[0] // 8

        segment_far = swap(segment)
        inputs_far = swap(inputs)
        small = jnp.concatenate(
            [b_query, b_value, b_out, norm1_gain, norm1_shift, norm2_gain, norm2_shift, b_down, b_up]
        )
        small_all = lax.all_gather(small, ("chip", "core", "ctx"), axis=0, tiled=False)
        qkv_weight = gather_rows(unfold(w_qkv))
        out_weight = by_chip(gather_rows(by_core(unfold(w_out), 1, chips)), 0, chips)
        up_weight = gather_rows(by_core(unfold(w_up), 1, chips))
        down_weight = gather_rows(by_core(unfold(w_down), 1, chips))
        cotangent_far = swap(cotangent)

        small_all = small_all.astype(jnp.float32)
        small_core = by_core(small_all, 0, chips)
        piece = lambda table, index: table[:, index * near_width : (index + 1) * near_width].reshape(-1)
        query_bias = piece(small_all, 0)
        value_bias = piece(small_all, 1)
        out_bias, first_gain, first_shift, second_gain, second_shift, down_bias = (
            piece(small_core, index) for index in range(2, 8)
        )
        up_bias = small_core[:, 8 * near_width :].reshape(-1)

        slot = jnp.arange(slots)
        earlier = slot[:, None] < slot[None, :]

        def ranks(own, far, far_first):
            inside = jnp.sum((own[:, None] == own[None, :]) & earlier, axis=0)
            outside = jnp.sum(far[:, None] == own[None, :], axis=0)
            return inside + jnp.where(far_first, outside, 0)

        rank_near = ranks(segment, segment_far, place == 1)
        rank_far = ranks(segment_far, segment, place == 0)

        def positions(ids, rank, image):
            return jnp.where(ids == image, rank, jnp.where(ids < 0, SEQ + rank, -1))

        row = jnp.arange(rows)
        pick_near = (positions(segment, rank_near, place)[None, :] == row[:, None])
        pick_far = (positions(segment_far, rank_far, place)[None, :] == row[:, None])
        pick_near, pick_far = pick_near.astype(jnp.bfloat16), pick_far.astype(jnp.bfloat16)
        give_near = (positions(segment, rank_near, place)[:, None] == row[None, :])
        other_image = jnp.where(segment == 1 - place, rank_near, -1)
        give_far = other_image[:, None] == row[None, :]
        give_near, give_far = give_near.astype(jnp.bfloat16), give_far.astype(jnp.bfloat16)
        column = jnp.arange(width)
        order = by_core(column, 0, chips)
        to_core = (column[:, None] == order[None, :]).astype(jnp.bfloat16)

        def take(near, far):
            picked = matmul(pick_near, near) + matmul(pick_far, far)
            return matmul(picked.astype(jnp.bfloat16), to_core)

        def give(array):
            natural = nt_dot(array.astype(jnp.bfloat16), to_core).astype(jnp.bfloat16)
            return matmul(give_near, natural) + matmul(give_far, swap(natural))

        kind = (row >= SEQ).astype(jnp.int32) + (row >= SEQ + pads).astype(jnp.int32)
        bias = jnp.where(kind[:, None] == kind[None, :], 0.0, -1e30).astype(jnp.float32)

        values_in = take(inputs, inputs_far)
        normal1, scale1 = standardize(values_in)
        normed1 = (normal1 * first_gain + first_shift).astype(jnp.bfloat16)
        joined_bias = jnp.concatenate([query_bias, jnp.zeros_like(query_bias), value_bias])
        joined = (matmul(normed1, qkv_weight) + joined_bias).astype(jnp.bfloat16)
        attended, log_total = attention_forward(joined, bias)
        middle = values_in + matmul(attended, out_weight) + out_bias
        normal2, scale2 = standardize(middle)
        normed2 = (normal2 * second_gain + second_shift).astype(jnp.bfloat16)
        hidden = matmul(normed2, up_weight) + up_bias
        active = gelu_exact(hidden).astype(jnp.bfloat16)
        slope = gelu_slope(hidden).astype(jnp.bfloat16)
        outputs = give(middle + matmul(active, down_weight) + down_bias).astype(jnp.bfloat16)

        live = (row < SEQ).astype(jnp.float32)[:, None]
        d_out = take(cotangent, cotangent_far) * live
        d_out_low = d_out.astype(jnp.bfloat16)
        sum_down = scatter_rows(matmul(active.T, d_out_low))
        d_hidden = (matmul(d_out_low, down_weight.T) * slope.astype(jnp.float32)).astype(jnp.bfloat16)
        sum_up = scatter_rows(matmul(normed2.T, d_hidden))
        d_normed2 = matmul(d_hidden, up_weight.T)
        d_middle = d_out + norm_backward(d_normed2, normal2, scale2, second_gain)
        d_branch = d_middle.astype(jnp.bfloat16)
        sum_out = scatter_rows(by_core(matmul(attended.T, d_branch).astype(jnp.bfloat16), 0, chips))
        d_attended = matmul(d_branch, out_weight.T).astype(jnp.bfloat16)
        d_query, d_key, d_value = attention_backward(joined, d_attended, log_total, bias)
        d_joined = jnp.concatenate([d_query, d_key, d_value], axis=1)
        sum_qkv = scatter_rows(matmul(normed1.T, d_joined))
        d_normed1 = matmul(d_joined, qkv_weight.T)
        input_grad = give(d_middle + norm_backward(d_normed1, normal1, scale1, first_gain))

        part = lambda vector: vector.reshape(2 * chips * 2, -1)
        core_sums = jnp.concatenate(
            [
                part(vector)
                for vector in (
                    column_sums(d_branch),
                    column_sums(d_normed1 * normal1),
                    column_sums(d_normed1),
                    column_sums(d_normed2 * normal2),
                    column_sums(d_normed2),
                    column_sums(d_out_low),
                    column_sums(d_hidden),
                )
            ],
            axis=1,
        )
        chip_sums = jnp.concatenate([part(column_sums(d_query)), part(column_sums(d_value))], axis=1)
        small_sums = jnp.concatenate([chip_sums, by_chip(core_sums, 0, chips)], axis=1)
        small_sums = lax.psum_scatter(
            small_sums, ("chip", "core", "ctx"), scatter_dimension=0, tiled=True
        )[0]
        own = lambda index: small_sums[index * near_width : (index + 1) * near_width]
        back = lambda matrix: refold(by_chip(matrix, 1, chips).astype(jnp.float32))
        return (
            outputs,
            input_grad,
            refold(sum_qkv.astype(jnp.float32)),
            own(0),
            own(1),
            back(sum_out),
            own(2),
            own(3),
            own(4),
            own(5),
            own(6),
            back(sum_up),
            small_sums[8 * near_width :],
            back(sum_down),
            own(7),
        )

    return on_device


def solution(mesh):
    if mesh.shape["ctx"] == IMAGES and mesh.shape["dp"] % 2 == 0:
        chips = mesh.shape["dp"] // 2
        mesh = jax.sharding.Mesh(
            mesh.devices.reshape(chips, 2, IMAGES), ("chip", "core", "ctx")
        )
        body, axes = by_image(chips), ("chip", "core", "ctx")
    else:
        body, axes = on_device, ("dp", "ctx")
    matrix, vector = P(axes, None), P(axes)
    return jax.shard_map(
        body,
        mesh=mesh,
        in_specs=(matrix, matrix, vector, matrix, vector, vector, matrix)
        + (vector,) * 5
        + (matrix, vector, matrix, vector),
        out_specs=(matrix, matrix, matrix, vector, vector, matrix)
        + (vector,) * 5
        + (matrix, vector, matrix, vector),
        check_vma=False,
    )
```

```python
import math

import jax
import jax.numpy as jnp
from jax import lax
from jax.experimental import pallas as pl
from jax.experimental.pallas import tpu as pltpu
from jax.sharding import PartitionSpec as P

HD = 64


EPSILON = 1e-06


def layer_norm(value, gain, shift):
    center = value - jnp.mean(value, axis=-1, keepdims=True)
    variance = jnp.mean(center * center, axis=-1, keepdims=True)
    return center * lax.rsqrt(variance + EPSILON) * gain + shift


def gelu_exact(value):
    return jax.nn.gelu(value, approximate=False)


def matmul(left, right):
    return jnp.dot(left, right, preferred_element_type=jnp.float32)


def unfold(stored):
    return stored.reshape(stored.shape[0] // 8, stored.shape[1] * 8)


def refold(matrix):
    return matrix.reshape(matrix.shape[0] * 8, matrix.shape[1] // 8)


def on_device(
    inputs,
    cotangent,
    segment,
    w_qkv,
    b_query,
    b_value,
    w_out,
    b_out,
    norm1_gain,
    norm1_shift,
    norm2_gain,
    norm2_shift,
    w_up,
    b_up,
    w_down,
    b_down,
):
    gathered = (
        lax.all_gather(w_qkv, ("dp", "ctx"), axis=0, tiled=True),
        lax.all_gather(b_query, ("dp", "ctx"), axis=0, tiled=True),
        lax.all_gather(b_value, ("dp", "ctx"), axis=0, tiled=True),
        lax.all_gather(w_out, ("dp", "ctx"), axis=0, tiled=True),
        lax.all_gather(b_out, ("dp", "ctx"), axis=0, tiled=True),
        lax.all_gather(norm1_gain, ("dp", "ctx"), axis=0, tiled=True),
        lax.all_gather(norm1_shift, ("dp", "ctx"), axis=0, tiled=True),
        lax.all_gather(norm2_gain, ("dp", "ctx"), axis=0, tiled=True),
        lax.all_gather(norm2_shift, ("dp", "ctx"), axis=0, tiled=True),
        lax.all_gather(w_up, ("dp", "ctx"), axis=0, tiled=True),
        lax.all_gather(b_up, ("dp", "ctx"), axis=0, tiled=True),
        lax.all_gather(w_down, ("dp", "ctx"), axis=0, tiled=True),
        lax.all_gather(b_down, ("dp", "ctx"), axis=0, tiled=True),
    )
    (
        qkv_stored,
        query_bias,
        value_bias,
        out_stored,
        out_bias,
        gain_one,
        shift_one,
        gain_two,
        shift_two,
        up_stored,
        up_bias,
        down_stored,
        down_bias,
    ) = gathered
    qkv_weight = unfold(qkv_stored)
    out_weight = unfold(out_stored)
    up_weight = unfold(up_stored)
    down_weight = unfold(down_stored)
    first_gain = gain_one.astype(jnp.float32)
    first_shift = shift_one.astype(jnp.float32)
    second_gain = gain_two.astype(jnp.float32)
    second_shift = shift_two.astype(jnp.float32)
    row_count = inputs.shape[0]
    model_width = out_weight.shape[0]
    head_count = model_width // HD
    score_scale = 1.0 / math.sqrt(HD)
    values_in = inputs.astype(jnp.float32)
    normed1 = layer_norm(values_in, first_gain, first_shift).astype(jnp.bfloat16)
    joined = matmul(normed1, qkv_weight)
    queries = (joined[:, :model_width] + query_bias.astype(jnp.float32)).astype(jnp.bfloat16)
    key_rows = joined[:, model_width : 2 * model_width].astype(jnp.bfloat16)
    value_rows = (joined[:, 2 * model_width :] + value_bias.astype(jnp.float32)).astype(
        jnp.bfloat16
    )
    key_all, value_all, seg_all = (
        lax.all_gather(key_rows, "ctx", axis=0, tiled=True),
        lax.all_gather(value_rows, "ctx", axis=0, tiled=True),
        lax.all_gather(segment.astype(jnp.bfloat16), "ctx", axis=0, tiled=True),
    )
    key_count = key_all.shape[0]
    query_heads = queries.reshape(row_count, head_count, HD)
    key_heads = key_all.reshape(key_count, head_count, HD)
    value_heads = value_all.reshape(key_count, head_count, HD)
    own_seg = segment.astype(jnp.float32)
    group_seg = seg_all.astype(jnp.float32)
    same_seg = own_seg[:, None] == group_seg[None, :]

    def make_scores():
        raw = (
            jnp.einsum("qhd,khd->hqk", query_heads, key_heads, preferred_element_type=jnp.float32)
            * score_scale
        )
        return jnp.where(same_seg[None], raw, -1e30)

    scores = make_scores()
    row_max = jnp.max(scores, axis=-1, keepdims=True)
    expo = jnp.exp(scores - row_max)
    row_total = jnp.sum(expo, axis=-1, keepdims=True)
    probs_low = (expo / row_total).astype(jnp.bfloat16)
    log_total = row_max + jnp.log(row_total)
    mixed = jnp.einsum("hqk,khd->qhd", probs_low, value_heads, preferred_element_type=jnp.float32)
    attended = mixed.reshape(row_count, model_width).astype(jnp.bfloat16)
    middle = values_in + matmul(attended, out_weight) + out_bias.astype(jnp.float32)
    normed2 = layer_norm(middle, second_gain, second_shift).astype(jnp.bfloat16)
    hidden = matmul(normed2, up_weight) + up_bias.astype(jnp.float32)
    active = gelu_exact(hidden).astype(jnp.bfloat16)
    outputs = (middle + matmul(active, down_weight) + down_bias.astype(jnp.float32)).astype(
        jnp.bfloat16
    )
    back_qkv, back_out, back_up, back_down = (qkv_weight, out_weight, up_weight, down_weight)
    valid = (segment >= 0).astype(jnp.float32)[:, None]
    d_out = cotangent.astype(jnp.float32) * valid
    d_out_low = d_out.astype(jnp.bfloat16)
    grad_down = refold(matmul(active.T, d_out_low))
    grad_down_bias = jnp.sum(d_out_low.astype(jnp.float32), axis=0)
    d_active = matmul(d_out_low, back_down.T)
    gelu_value, gelu_pull = jax.vjp(gelu_exact, hidden)
    d_hidden = gelu_pull(d_active)[0].astype(jnp.bfloat16)
    grad_up = refold(matmul(normed2.T, d_hidden))
    grad_up_bias = jnp.sum(d_hidden.astype(jnp.float32), axis=0)
    d_normed2 = matmul(d_hidden, back_up.T)
    norm_value, norm_pull = jax.vjp(layer_norm, middle, second_gain, second_shift)
    d_middle_norm, grad_gain_two, grad_shift_two = norm_pull(d_normed2)
    d_middle = d_out + d_middle_norm
    d_branch = d_middle.astype(jnp.bfloat16)
    grad_out = refold(matmul(attended.T, d_branch))
    grad_out_bias = jnp.sum(d_branch.astype(jnp.float32), axis=0)
    d_attended_flat = matmul(d_branch, back_out.T).astype(jnp.bfloat16)
    d_attended = d_attended_flat.reshape(row_count, head_count, HD)
    scores = make_scores()
    probs = jnp.exp(scores - log_total)
    d_probs = jnp.einsum(
        "qhd,khd->hqk", d_attended, value_heads, preferred_element_type=jnp.float32
    )
    delta_rows = jnp.sum(probs * d_probs, axis=-1, keepdims=True)
    d_scores = (probs * (d_probs - delta_rows)).astype(jnp.bfloat16)
    d_query = (
        jnp.einsum("hqk,khd->qhd", d_scores, key_heads, preferred_element_type=jnp.float32)
        * score_scale
    ).reshape(row_count, model_width)
    probs_again = probs.astype(jnp.bfloat16)
    d_key_all = (
        jnp.einsum("hqk,qhd->khd", d_scores, query_heads, preferred_element_type=jnp.float32)
        * score_scale
    ).reshape(key_count, model_width)
    d_value_all = jnp.einsum(
        "hqk,qhd->khd", probs_again, d_attended, preferred_element_type=jnp.float32
    ).reshape(key_count, model_width)
    d_key, d_value = (
        lax.psum_scatter(
            d_key_all.astype(jnp.bfloat16), "ctx", scatter_dimension=0, tiled=True
        ).astype(jnp.float32),
        lax.psum_scatter(
            d_value_all.astype(jnp.bfloat16), "ctx", scatter_dimension=0, tiled=True
        ).astype(jnp.float32),
    )
    d_query_low = d_query.astype(jnp.bfloat16)
    d_value_low = d_value.astype(jnp.bfloat16)
    d_joined = jnp.concatenate([d_query_low, d_key.astype(jnp.bfloat16), d_value_low], axis=1)
    grad_qkv = refold(matmul(normed1.T, d_joined))
    grad_query_bias = jnp.sum(d_query_low.astype(jnp.float32), axis=0)
    grad_value_bias = jnp.sum(d_value_low.astype(jnp.float32), axis=0)
    d_normed1 = matmul(d_joined, back_qkv.T)
    first_value, first_pull = jax.vjp(layer_norm, values_in, first_gain, first_shift)
    d_input_norm, grad_gain_one, grad_shift_one = first_pull(d_normed1)
    input_grad = d_middle + d_input_norm
    partial_sums = (
        lax.psum_scatter(
            grad_qkv.astype(jnp.bfloat16), "dp", scatter_dimension=0, tiled=True
        ).astype(jnp.float32),
        lax.psum_scatter(
            grad_query_bias.astype(jnp.bfloat16), "dp", scatter_dimension=0, tiled=True
        ).astype(jnp.float32),
        lax.psum_scatter(
            grad_value_bias.astype(jnp.bfloat16), "dp", scatter_dimension=0, tiled=True
        ).astype(jnp.float32),
        lax.psum_scatter(
            grad_out.astype(jnp.bfloat16), "dp", scatter_dimension=0, tiled=True
        ).astype(jnp.float32),
        lax.psum_scatter(
            grad_out_bias.astype(jnp.bfloat16), "dp", scatter_dimension=0, tiled=True
        ).astype(jnp.float32),
        lax.psum_scatter(
            grad_gain_one.astype(jnp.bfloat16), "dp", scatter_dimension=0, tiled=True
        ).astype(jnp.float32),
        lax.psum_scatter(
            grad_shift_one.astype(jnp.bfloat16), "dp", scatter_dimension=0, tiled=True
        ).astype(jnp.float32),
        lax.psum_scatter(
            grad_gain_two.astype(jnp.bfloat16), "dp", scatter_dimension=0, tiled=True
        ).astype(jnp.float32),
        lax.psum_scatter(
            grad_shift_two.astype(jnp.bfloat16), "dp", scatter_dimension=0, tiled=True
        ).astype(jnp.float32),
        lax.psum_scatter(
            grad_up.astype(jnp.bfloat16), "dp", scatter_dimension=0, tiled=True
        ).astype(jnp.float32),
        lax.psum_scatter(
            grad_up_bias.astype(jnp.bfloat16), "dp", scatter_dimension=0, tiled=True
        ).astype(jnp.float32),
        lax.psum_scatter(
            grad_down.astype(jnp.bfloat16), "dp", scatter_dimension=0, tiled=True
        ).astype(jnp.float32),
        lax.psum_scatter(
            grad_down_bias.astype(jnp.bfloat16), "dp", scatter_dimension=0, tiled=True
        ).astype(jnp.float32),
    )
    all_sums = (
        lax.psum_scatter(
            partial_sums[0].astype(jnp.bfloat16), "ctx", scatter_dimension=0, tiled=True
        ).astype(jnp.float32),
        lax.psum_scatter(
            partial_sums[1].astype(jnp.bfloat16), "ctx", scatter_dimension=0, tiled=True
        ).astype(jnp.float32),
        lax.psum_scatter(
            partial_sums[2].astype(jnp.bfloat16), "ctx", scatter_dimension=0, tiled=True
        ).astype(jnp.float32),
        lax.psum_scatter(
            partial_sums[3].astype(jnp.bfloat16), "ctx", scatter_dimension=0, tiled=True
        ).astype(jnp.float32),
        lax.psum_scatter(
            partial_sums[4].astype(jnp.bfloat16), "ctx", scatter_dimension=0, tiled=True
        ).astype(jnp.float32),
        lax.psum_scatter(
            partial_sums[5].astype(jnp.bfloat16), "ctx", scatter_dimension=0, tiled=True
        ).astype(jnp.float32),
        lax.psum_scatter(
            partial_sums[6].astype(jnp.bfloat16), "ctx", scatter_dimension=0, tiled=True
        ).astype(jnp.float32),
        lax.psum_scatter(
            partial_sums[7].astype(jnp.bfloat16), "ctx", scatter_dimension=0, tiled=True
        ).astype(jnp.float32),
        lax.psum_scatter(
            partial_sums[8].astype(jnp.bfloat16), "ctx", scatter_dimension=0, tiled=True
        ).astype(jnp.float32),
        lax.psum_scatter(
            partial_sums[9].astype(jnp.bfloat16), "ctx", scatter_dimension=0, tiled=True
        ).astype(jnp.float32),
        lax.psum_scatter(
            partial_sums[10].astype(jnp.bfloat16), "ctx", scatter_dimension=0, tiled=True
        ).astype(jnp.float32),
        lax.psum_scatter(
            partial_sums[11].astype(jnp.bfloat16), "ctx", scatter_dimension=0, tiled=True
        ).astype(jnp.float32),
        lax.psum_scatter(
            partial_sums[12].astype(jnp.bfloat16), "ctx", scatter_dimension=0, tiled=True
        ).astype(jnp.float32),
    )
    (
        sum_qkv,
        sum_query_bias,
        sum_value_bias,
        sum_out,
        sum_out_bias,
        sum_gain_one,
        sum_shift_one,
        sum_gain_two,
        sum_shift_two,
        sum_up,
        sum_up_bias,
        sum_down,
        sum_down_bias,
    ) = all_sums
    return (
        outputs,
        input_grad,
        sum_qkv,
        sum_query_bias,
        sum_value_bias,
        sum_out,
        sum_out_bias,
        sum_gain_one,
        sum_shift_one,
        sum_gain_two,
        sum_shift_two,
        sum_up,
        sum_up_bias,
        sum_down,
        sum_down_bias,
    )


SEQ = 577
IMAGES = 2
PAIR = 2 * HD
CHUNK = 256


def round_up(count, unit):
    return -(-count // unit) * unit


def chunks_of(count):
    return [(start, min(CHUNK, count - start)) for start in range(0, count, CHUNK)]


def nt_dot(left, right):
    return lax.dot_general(
        left, right, (((1,), (1,)), ((), ())), preferred_element_type=jnp.float32
    )


def half_mask(rows):
    return lax.broadcasted_iota(jnp.int32, (rows, PAIR), 1) < HD


def forward_kernel(query_ref, key_ref, value_ref, bias_ref, attended_ref, log_ref):
    rows = query_ref.shape[0]
    first = half_mask(rows)
    zero = jnp.zeros((rows, PAIR), jnp.bfloat16)
    key = key_ref[...]
    key_sides = (jnp.where(first, key, zero), jnp.where(first, zero, key))
    value_t = value_ref[...].astype(jnp.float32).T.astype(jnp.bfloat16)
    scale = jnp.bfloat16(1.0 / math.sqrt(HD))
    for start, size in chunks_of(rows):
        query = query_ref[start : start + size, :] * scale
        bias = bias_ref[:, start : start + size]
        outs = []
        for side in range(2):
            scores = nt_dot(key_sides[side], query) + bias
            top = jnp.max(scores, axis=0, keepdims=True)
            expo = jnp.exp(scores - top)
            total = jnp.sum(expo, axis=0, keepdims=True)
            probs_low = (expo * (1.0 / total)).astype(jnp.bfloat16)
            outs.append(matmul(value_t[side * HD : (side + 1) * HD, :], probs_low))
            log_ref[0, side : side + 1, start : start + size] = top + jnp.log(total)
        mixed = jnp.concatenate(outs, axis=0)
        attended_ref[start : start + size, :] = mixed.T.astype(jnp.bfloat16)


def backward_kernel(
    query_ref, key_ref, value_ref, d_ref, log_ref, bias_ref, dq_ref, dk_ref, dv_ref, dk_sum, dv_sum
):
    rows = query_ref.shape[0]
    first = half_mask(rows)
    zero = jnp.zeros((rows, PAIR), jnp.bfloat16)
    key = key_ref[...]
    value = value_ref[...]
    key_sides = (jnp.where(first, key, zero), jnp.where(first, zero, key))
    value_sides = (jnp.where(first, value, zero), jnp.where(first, zero, value))
    key_t = key.astype(jnp.float32).T.astype(jnp.bfloat16)
    scale = jnp.bfloat16(1.0 / math.sqrt(HD))
    for start, size in chunks_of(rows):
        query = query_ref[start : start + size, :] * scale
        d_rows = d_ref[start : start + size, :]
        bias = bias_ref[:, start : start + size]
        outs = []
        for side in range(2):
            scores = nt_dot(key_sides[side], query) + bias
            probs = jnp.exp(scores - log_ref[0, side : side + 1, start : start + size])
            d_probs = nt_dot(value_sides[side], d_rows)
            product = probs * d_probs
            delta = jnp.sum(product, axis=0, keepdims=True)
            d_scores = (product - probs * delta).astype(jnp.bfloat16)
            d_value = matmul(probs.astype(jnp.bfloat16), d_rows)
            d_key = matmul(d_scores, query)
            if start == 0:
                dv_sum[side] = d_value
                dk_sum[side] = d_key
            else:
                dv_sum[side] += d_value
                dk_sum[side] += d_key
            outs.append(matmul(key_t[side * HD : (side + 1) * HD, :], d_scores))
        d_query = jnp.concatenate(outs, axis=0) * (1.0 / math.sqrt(HD))
        dq_ref[start : start + size, :] = d_query.T.astype(jnp.bfloat16)
    dk_ref[...] = jnp.where(first, dk_sum[0], dk_sum[1]).astype(jnp.bfloat16)
    dv_ref[...] = jnp.where(first, dv_sum[0], dv_sum[1]).astype(jnp.bfloat16)


def attention_forward(joined, bias):
    rows, width = joined.shape[0], joined.shape[1] // 3
    pairs = width // PAIR
    flops = 4 * rows * rows * width
    return pl.pallas_call(
        forward_kernel,
        grid=(pairs,),
        in_specs=[
            pl.BlockSpec((rows, PAIR), lambda i: (0, i)),
            pl.BlockSpec((rows, PAIR), lambda i: (0, pairs + i)),
            pl.BlockSpec((rows, PAIR), lambda i: (0, 2 * pairs + i)),
            pl.BlockSpec((rows, rows), lambda i: (0, 0)),
        ],
        out_specs=[
            pl.BlockSpec((rows, PAIR), lambda i: (0, i)),
            pl.BlockSpec((1, 2, rows), lambda i: (i, 0, 0)),
        ],
        out_shape=[
            jax.ShapeDtypeStruct((rows, width), jnp.bfloat16),
            jax.ShapeDtypeStruct((pairs, 2, rows), jnp.float32),
        ],
        compiler_params=pltpu.CompilerParams(vmem_limit_bytes=40 * 2**20),
        cost_estimate=pl.CostEstimate(
            flops=4 * flops, bytes_accessed=8 * rows * width, transcendentals=rows * rows * 16
        ),
        name="attention_forward",
    )(joined, joined, joined, bias)


def attention_backward(joined, d_attended, log_total, bias):
    rows, width = d_attended.shape
    pairs = width // PAIR
    flops = 10 * rows * rows * width
    block = jax.ShapeDtypeStruct((rows, width), jnp.bfloat16)
    return pl.pallas_call(
        backward_kernel,
        grid=(pairs,),
        in_specs=[
            pl.BlockSpec((rows, PAIR), lambda i: (0, i)),
            pl.BlockSpec((rows, PAIR), lambda i: (0, pairs + i)),
            pl.BlockSpec((rows, PAIR), lambda i: (0, 2 * pairs + i)),
            pl.BlockSpec((rows, PAIR), lambda i: (0, i)),
            pl.BlockSpec((1, 2, rows), lambda i: (i, 0, 0)),
            pl.BlockSpec((rows, rows), lambda i: (0, 0)),
        ],
        out_specs=[pl.BlockSpec((rows, PAIR), lambda i: (0, i))] * 3,
        out_shape=[block] * 3,
        scratch_shapes=[pltpu.VMEM((2, rows, PAIR), jnp.float32)] * 2,
        compiler_params=pltpu.CompilerParams(vmem_limit_bytes=40 * 2**20),
        cost_estimate=pl.CostEstimate(
            flops=4 * flops, bytes_accessed=14 * rows * width, transcendentals=rows * rows * 16
        ),
        name="attention_backward",
    )(joined, joined, joined, d_attended, log_total, bias)


def standardize(value):
    center = value - jnp.mean(value, axis=-1, keepdims=True)
    variance = jnp.mean(center * center, axis=-1, keepdims=True)
    scale = lax.rsqrt(variance + EPSILON)
    return center * scale, scale


def norm_backward(d_normed, normal, scale, gain):
    scaled = d_normed * gain
    mean = jnp.mean(scaled, axis=-1, keepdims=True)
    along = jnp.mean(scaled * normal, axis=-1, keepdims=True)
    return (scaled - mean - normal * along) * scale


def gelu_slope(value):
    phi = 0.5 * (1.0 + lax.erf(value * math.sqrt(0.5)))
    return phi + value * jnp.exp(-0.5 * value * value) * (1.0 / math.sqrt(2.0 * math.pi))


def to_local(array, axis, far):
    shape = array.shape
    cut = shape[:axis] + (far, 2, 2, 2, shape[axis] // (8 * far)) + shape[axis + 1 :]
    spots = [axis + 2, axis + 1, axis + 3, axis]
    spots = list(range(axis)) + spots + list(range(axis + 4, len(cut)))
    return array.reshape(cut).transpose(spots).reshape(shape)


def to_natural(array, axis, far):
    shape = array.shape
    cut = shape[:axis] + (2, 2, 2, far, shape[axis] // (8 * far)) + shape[axis + 1 :]
    spots = [axis + 3, axis + 1, axis, axis + 2]
    spots = list(range(axis)) + spots + list(range(axis + 4, len(cut)))
    return array.reshape(cut).transpose(spots).reshape(shape)


def assemble_kernel(index_ref, *refs):
    *pieces, whole, arrived = refs
    copies = []
    for number, piece in enumerate(pieces):
        size = piece.shape[0]
        start = pl.multiple_of(index_ref[number] * size, 16)
        copies.append(
            pltpu.make_async_copy(piece, whole.at[pl.ds(start, size)], arrived.at[number])
        )
    for copy in copies:
        copy.start()
    for copy in copies:
        copy.wait()


def assemble(pieces, indices):
    size, width = pieces[0].shape
    count = len(pieces)
    return pl.pallas_call(
        assemble_kernel,
        in_specs=[pl.BlockSpec(memory_space=pltpu.SMEM)]
        + [pl.BlockSpec(memory_space=pl.ANY)] * count,
        out_specs=pl.BlockSpec(memory_space=pl.ANY),
        out_shape=jax.ShapeDtypeStruct((count * size, width), pieces[0].dtype),
        scratch_shapes=[pltpu.SemaphoreType.DMA((count,))],
        cost_estimate=pl.CostEstimate(
            flops=0, bytes_accessed=4 * count * size * width, transcendentals=0
        ),
        name="assemble",
    )(jnp.stack(indices).astype(jnp.int32), *pieces)


def trade(array, axis):
    return lax.ppermute(array, axis, [(0, 1), (1, 0)])


def after(array, other):
    return lax.optimization_barrier((array, other))[0]


def gather_far(shard, far):
    place = lax.axis_index("z")
    pieces, indices = [shard], [place]
    for step in range(1, far):
        pieces.append(lax.ppermute(shard, "z", [(i, (i + step) % far) for i in range(far)]))
        indices.append((place - step) % far)
    return assemble(pieces, indices)


def gather_near(block):
    own = 4 * lax.axis_index("core") + 2 * lax.axis_index("x") + lax.axis_index("ctx")
    blocks = [block]
    for axis in ("ctx", "x", "core"):
        blocks = blocks + [trade(one, axis) for one in blocks]
    return assemble(blocks, [own ^ number for number in range(8)])


def scatter_rows(matrix, far):
    for axis in ("core", "x", "ctx"):
        half = matrix.shape[0] // 2
        place = lax.axis_index(axis)
        kept = lax.dynamic_slice_in_dim(matrix, place * half, half)
        sent = lax.dynamic_slice_in_dim(matrix, (1 - place) * half, half)
        total = kept.astype(jnp.float32) + trade(sent, axis).astype(jnp.float32)
        matrix = total.astype(matrix.dtype)
    size = matrix.shape[0] // far
    place = lax.axis_index("z")
    total = lax.dynamic_slice_in_dim(matrix, place * size, size).astype(jnp.float32)
    for step in range(1, far):
        sent = lax.dynamic_slice_in_dim(matrix, ((place + step) % far) * size, size)
        got = lax.ppermute(sent, "z", [(i, (i + step) % far) for i in range(far)])
        total = total + got.astype(jnp.float32)
    return total


def scatter_low(matrix, far):
    return scatter_rows(matrix.astype(jnp.bfloat16), far)


def column_sums(array):
    return jnp.sum(array.astype(jnp.float32), axis=0)


def by_image(far):
    def on_device(
        inputs,
        cotangent,
        segment,
        w_qkv,
        b_query,
        b_value,
        w_out,
        b_out,
        norm1_gain,
        norm1_shift,
        norm2_gain,
        norm2_shift,
        w_up,
        b_up,
        w_down,
        b_down,
    ):
        place = lax.axis_index("ctx")
        swap = lambda array: trade(array, "ctx")
        slots, width = inputs.shape
        pads = 2 * slots - IMAGES * SEQ
        rows = round_up(SEQ + pads, 16)
        near_width = w_up.shape[0] // 8

        segment_far = swap(segment)
        inputs_far = swap(inputs)
        small = jnp.concatenate(
            [b_query, b_value, b_out, norm1_gain, norm1_shift, norm2_gain, norm2_shift, b_down, b_up]
        )
        small_all = lax.all_gather(small, ("z", "x", "core", "ctx"), axis=0, tiled=False)
        far_qkv = gather_far(unfold(w_qkv), far)
        qkv_weight = gather_near(far_qkv)
        far_out = gather_far(to_local(after(unfold(w_out), far_qkv), 1, far), far)
        far_up = gather_far(to_local(after(unfold(w_up), far_qkv), 1, far), far)
        far_down = gather_far(to_local(after(unfold(w_down), far_up), 1, far), far)
        out_weight = to_natural(gather_near(far_out), 0, far)
        up_weight = gather_near(far_up)
        down_weight = gather_near(far_down)

        small_all = small_all.astype(jnp.float32)
        small_core = to_local(small_all, 0, far)
        piece = lambda table, index: table[:, index * near_width : (index + 1) * near_width].reshape(-1)
        query_bias = piece(small_all, 0)
        value_bias = piece(small_all, 1)
        out_bias, first_gain, first_shift, second_gain, second_shift, down_bias = (
            piece(small_core, index) for index in range(2, 8)
        )
        up_bias = small_core[:, 8 * near_width :].reshape(-1)

        slot = jnp.arange(slots)
        earlier = slot[:, None] < slot[None, :]

        def ranks(own, far, far_first):
            inside = jnp.sum((own[:, None] == own[None, :]) & earlier, axis=0)
            outside = jnp.sum(far[:, None] == own[None, :], axis=0)
            return inside + jnp.where(far_first, outside, 0)

        rank_near = ranks(segment, segment_far, place == 1)
        rank_far = ranks(segment_far, segment, place == 0)

        def positions(ids, rank, image):
            return jnp.where(ids == image, rank, jnp.where(ids < 0, SEQ + rank, -1))

        row = jnp.arange(rows)
        pick_near = (positions(segment, rank_near, place)[None, :] == row[:, None])
        pick_far = (positions(segment_far, rank_far, place)[None, :] == row[:, None])
        pick_near, pick_far = pick_near.astype(jnp.bfloat16), pick_far.astype(jnp.bfloat16)
        give_near = (positions(segment, rank_near, place)[:, None] == row[None, :])
        other_image = jnp.where(segment == 1 - place, rank_near, -1)
        give_far = other_image[:, None] == row[None, :]
        give_near, give_far = give_near.astype(jnp.bfloat16), give_far.astype(jnp.bfloat16)
        column = jnp.arange(width)
        order = to_local(column, 0, far)
        to_core = (column[:, None] == order[None, :]).astype(jnp.bfloat16)

        def take(near, far):
            picked = matmul(pick_near, near) + matmul(pick_far, far)
            return matmul(picked.astype(jnp.bfloat16), to_core)

        def give(array):
            natural = nt_dot(array.astype(jnp.bfloat16), to_core).astype(jnp.bfloat16)
            return matmul(give_near, natural) + matmul(give_far, swap(natural))

        kind = (row >= SEQ).astype(jnp.int32) + (row >= SEQ + pads).astype(jnp.int32)
        bias = jnp.where(kind[:, None] == kind[None, :], 0.0, -1e30).astype(jnp.float32)

        values_in = take(inputs, inputs_far)
        normal1, scale1 = standardize(values_in)
        normed1 = (normal1 * first_gain + first_shift).astype(jnp.bfloat16)
        joined_bias = jnp.concatenate([query_bias, jnp.zeros_like(query_bias), value_bias])
        joined = (matmul(normed1, qkv_weight) + joined_bias).astype(jnp.bfloat16)
        attended, log_total = attention_forward(joined, bias)
        middle = values_in + matmul(attended, out_weight) + out_bias
        normal2, scale2 = standardize(middle)
        normed2 = (normal2 * second_gain + second_shift).astype(jnp.bfloat16)
        hidden = matmul(normed2, up_weight) + up_bias
        active = gelu_exact(hidden).astype(jnp.bfloat16)
        slope = gelu_slope(hidden).astype(jnp.bfloat16)
        outputs = give(middle + matmul(active, down_weight) + down_bias).astype(jnp.bfloat16)

        live = (row < SEQ).astype(jnp.float32)[:, None]
        cotangent_far = swap(after(cotangent, joined))
        d_out = take(cotangent, cotangent_far) * live
        d_out_low = d_out.astype(jnp.bfloat16)
        sum_down = scatter_low(matmul(active.T, d_out_low), far)
        d_hidden = (matmul(d_out_low, down_weight.T) * slope.astype(jnp.float32)).astype(jnp.bfloat16)
        sum_up = scatter_low(matmul(normed2.T, d_hidden), far)
        d_normed2 = matmul(d_hidden, up_weight.T)
        d_middle = d_out + norm_backward(d_normed2, normal2, scale2, second_gain)
        d_branch = d_middle.astype(jnp.bfloat16)
        sum_out = scatter_low(
            to_local(matmul(attended.T, d_branch).astype(jnp.bfloat16), 0, far), far
        )
        d_attended = matmul(d_branch, out_weight.T).astype(jnp.bfloat16)
        d_query, d_key, d_value = attention_backward(joined, d_attended, log_total, bias)
        d_joined = jnp.concatenate([d_query, d_key, d_value], axis=1)
        sum_qkv = scatter_low(matmul(normed1.T, d_joined), far)
        d_normed1 = matmul(d_joined, qkv_weight.T)
        input_grad = give(d_middle + norm_backward(d_normed1, normal1, scale1, first_gain))

        part = lambda vector: vector.reshape(8 * far, -1)
        core_sums = jnp.concatenate(
            [
                part(vector)
                for vector in (
                    column_sums(d_branch),
                    column_sums(d_normed1 * normal1),
                    column_sums(d_normed1),
                    column_sums(d_normed2 * normal2),
                    column_sums(d_normed2),
                    column_sums(d_out_low),
                    column_sums(d_hidden),
                )
            ],
            axis=1,
        )
        chip_sums = jnp.concatenate([part(column_sums(d_query)), part(column_sums(d_value))], axis=1)
        small_sums = jnp.concatenate([to_local(chip_sums, 0, far), core_sums], axis=1)
        small_sums = scatter_rows(small_sums, far)[0]
        own = lambda index: small_sums[index * near_width : (index + 1) * near_width]
        back = lambda matrix: refold(to_natural(matrix, 1, far))
        return (
            outputs,
            input_grad,
            refold(sum_qkv),
            own(0),
            own(1),
            back(sum_out),
            own(2),
            own(3),
            own(4),
            own(5),
            own(6),
            back(sum_up),
            small_sums[8 * near_width :],
            back(sum_down),
            own(7),
        )

    return on_device


def solution(mesh):
    if mesh.shape["ctx"] == IMAGES and mesh.shape["dp"] % 4 == 0:
        far, axes = mesh.shape["dp"] // 4, ("z", "x", "core", "ctx")
        mesh = jax.sharding.Mesh(mesh.devices.reshape(far, 2, 2, IMAGES), axes)
        body = by_image(far)
    else:
        body, axes = on_device, ("dp", "ctx")
    matrix, vector = P(axes, None), P(axes)
    return jax.shard_map(
        body,
        mesh=mesh,
        in_specs=(matrix, matrix, vector, matrix, vector, vector, matrix)
        + (vector,) * 5
        + (matrix, vector, matrix, vector),
        out_specs=(matrix, matrix, matrix, vector, vector, matrix)
        + (vector,) * 5
        + (matrix, vector, matrix, vector),
        check_vma=False,
    )
```

```python
import math

import jax
import jax.numpy as jnp
from jax import lax
from jax.experimental import pallas as pl
from jax.experimental.pallas import tpu as pltpu
from jax.sharding import PartitionSpec as P

HD = 64


EPSILON = 1e-06


def layer_norm(value, gain, shift):
    center = value - jnp.mean(value, axis=-1, keepdims=True)
    variance = jnp.mean(center * center, axis=-1, keepdims=True)
    return center * lax.rsqrt(variance + EPSILON) * gain + shift


def gelu_exact(value):
    return jax.nn.gelu(value, approximate=False)


def matmul(left, right):
    return jnp.dot(left, right, preferred_element_type=jnp.float32)


def unfold(stored):
    return stored.reshape(stored.shape[0] // 8, stored.shape[1] * 8)


def refold(matrix):
    return matrix.reshape(matrix.shape[0] * 8, matrix.shape[1] // 8)


def on_device(
    inputs,
    cotangent,
    segment,
    w_qkv,
    b_query,
    b_value,
    w_out,
    b_out,
    norm1_gain,
    norm1_shift,
    norm2_gain,
    norm2_shift,
    w_up,
    b_up,
    w_down,
    b_down,
):
    gathered = (
        lax.all_gather(w_qkv, ("dp", "ctx"), axis=0, tiled=True),
        lax.all_gather(b_query, ("dp", "ctx"), axis=0, tiled=True),
        lax.all_gather(b_value, ("dp", "ctx"), axis=0, tiled=True),
        lax.all_gather(w_out, ("dp", "ctx"), axis=0, tiled=True),
        lax.all_gather(b_out, ("dp", "ctx"), axis=0, tiled=True),
        lax.all_gather(norm1_gain, ("dp", "ctx"), axis=0, tiled=True),
        lax.all_gather(norm1_shift, ("dp", "ctx"), axis=0, tiled=True),
        lax.all_gather(norm2_gain, ("dp", "ctx"), axis=0, tiled=True),
        lax.all_gather(norm2_shift, ("dp", "ctx"), axis=0, tiled=True),
        lax.all_gather(w_up, ("dp", "ctx"), axis=0, tiled=True),
        lax.all_gather(b_up, ("dp", "ctx"), axis=0, tiled=True),
        lax.all_gather(w_down, ("dp", "ctx"), axis=0, tiled=True),
        lax.all_gather(b_down, ("dp", "ctx"), axis=0, tiled=True),
    )
    (
        qkv_stored,
        query_bias,
        value_bias,
        out_stored,
        out_bias,
        gain_one,
        shift_one,
        gain_two,
        shift_two,
        up_stored,
        up_bias,
        down_stored,
        down_bias,
    ) = gathered
    qkv_weight = unfold(qkv_stored)
    out_weight = unfold(out_stored)
    up_weight = unfold(up_stored)
    down_weight = unfold(down_stored)
    first_gain = gain_one.astype(jnp.float32)
    first_shift = shift_one.astype(jnp.float32)
    second_gain = gain_two.astype(jnp.float32)
    second_shift = shift_two.astype(jnp.float32)
    row_count = inputs.shape[0]
    model_width = out_weight.shape[0]
    head_count = model_width // HD
    score_scale = 1.0 / math.sqrt(HD)
    values_in = inputs.astype(jnp.float32)
    normed1 = layer_norm(values_in, first_gain, first_shift).astype(jnp.bfloat16)
    joined = matmul(normed1, qkv_weight)
    queries = (joined[:, :model_width] + query_bias.astype(jnp.float32)).astype(jnp.bfloat16)
    key_rows = joined[:, model_width : 2 * model_width].astype(jnp.bfloat16)
    value_rows = (joined[:, 2 * model_width :] + value_bias.astype(jnp.float32)).astype(
        jnp.bfloat16
    )
    key_all, value_all, seg_all = (
        lax.all_gather(key_rows, "ctx", axis=0, tiled=True),
        lax.all_gather(value_rows, "ctx", axis=0, tiled=True),
        lax.all_gather(segment.astype(jnp.bfloat16), "ctx", axis=0, tiled=True),
    )
    key_count = key_all.shape[0]
    query_heads = queries.reshape(row_count, head_count, HD)
    key_heads = key_all.reshape(key_count, head_count, HD)
    value_heads = value_all.reshape(key_count, head_count, HD)
    own_seg = segment.astype(jnp.float32)
    group_seg = seg_all.astype(jnp.float32)
    same_seg = own_seg[:, None] == group_seg[None, :]

    def make_scores():
        raw = (
            jnp.einsum("qhd,khd->hqk", query_heads, key_heads, preferred_element_type=jnp.float32)
            * score_scale
        )
        return jnp.where(same_seg[None], raw, -1e30)

    scores = make_scores()
    row_max = jnp.max(scores, axis=-1, keepdims=True)
    expo = jnp.exp(scores - row_max)
    row_total = jnp.sum(expo, axis=-1, keepdims=True)
    probs_low = (expo / row_total).astype(jnp.bfloat16)
    log_total = row_max + jnp.log(row_total)
    mixed = jnp.einsum("hqk,khd->qhd", probs_low, value_heads, preferred_element_type=jnp.float32)
    attended = mixed.reshape(row_count, model_width).astype(jnp.bfloat16)
    middle = values_in + matmul(attended, out_weight) + out_bias.astype(jnp.float32)
    normed2 = layer_norm(middle, second_gain, second_shift).astype(jnp.bfloat16)
    hidden = matmul(normed2, up_weight) + up_bias.astype(jnp.float32)
    active = gelu_exact(hidden).astype(jnp.bfloat16)
    outputs = (middle + matmul(active, down_weight) + down_bias.astype(jnp.float32)).astype(
        jnp.bfloat16
    )
    back_qkv, back_out, back_up, back_down = (qkv_weight, out_weight, up_weight, down_weight)
    valid = (segment >= 0).astype(jnp.float32)[:, None]
    d_out = cotangent.astype(jnp.float32) * valid
    d_out_low = d_out.astype(jnp.bfloat16)
    grad_down = refold(matmul(active.T, d_out_low))
    grad_down_bias = jnp.sum(d_out_low.astype(jnp.float32), axis=0)
    d_active = matmul(d_out_low, back_down.T)
    gelu_value, gelu_pull = jax.vjp(gelu_exact, hidden)
    d_hidden = gelu_pull(d_active)[0].astype(jnp.bfloat16)
    grad_up = refold(matmul(normed2.T, d_hidden))
    grad_up_bias = jnp.sum(d_hidden.astype(jnp.float32), axis=0)
    d_normed2 = matmul(d_hidden, back_up.T)
    norm_value, norm_pull = jax.vjp(layer_norm, middle, second_gain, second_shift)
    d_middle_norm, grad_gain_two, grad_shift_two = norm_pull(d_normed2)
    d_middle = d_out + d_middle_norm
    d_branch = d_middle.astype(jnp.bfloat16)
    grad_out = refold(matmul(attended.T, d_branch))
    grad_out_bias = jnp.sum(d_branch.astype(jnp.float32), axis=0)
    d_attended_flat = matmul(d_branch, back_out.T).astype(jnp.bfloat16)
    d_attended = d_attended_flat.reshape(row_count, head_count, HD)
    scores = make_scores()
    probs = jnp.exp(scores - log_total)
    d_probs = jnp.einsum(
        "qhd,khd->hqk", d_attended, value_heads, preferred_element_type=jnp.float32
    )
    delta_rows = jnp.sum(probs * d_probs, axis=-1, keepdims=True)
    d_scores = (probs * (d_probs - delta_rows)).astype(jnp.bfloat16)
    d_query = (
        jnp.einsum("hqk,khd->qhd", d_scores, key_heads, preferred_element_type=jnp.float32)
        * score_scale
    ).reshape(row_count, model_width)
    probs_again = probs.astype(jnp.bfloat16)
    d_key_all = (
        jnp.einsum("hqk,qhd->khd", d_scores, query_heads, preferred_element_type=jnp.float32)
        * score_scale
    ).reshape(key_count, model_width)
    d_value_all = jnp.einsum(
        "hqk,qhd->khd", probs_again, d_attended, preferred_element_type=jnp.float32
    ).reshape(key_count, model_width)
    d_key, d_value = (
        lax.psum_scatter(
            d_key_all.astype(jnp.bfloat16), "ctx", scatter_dimension=0, tiled=True
        ).astype(jnp.float32),
        lax.psum_scatter(
            d_value_all.astype(jnp.bfloat16), "ctx", scatter_dimension=0, tiled=True
        ).astype(jnp.float32),
    )
    d_query_low = d_query.astype(jnp.bfloat16)
    d_value_low = d_value.astype(jnp.bfloat16)
    d_joined = jnp.concatenate([d_query_low, d_key.astype(jnp.bfloat16), d_value_low], axis=1)
    grad_qkv = refold(matmul(normed1.T, d_joined))
    grad_query_bias = jnp.sum(d_query_low.astype(jnp.float32), axis=0)
    grad_value_bias = jnp.sum(d_value_low.astype(jnp.float32), axis=0)
    d_normed1 = matmul(d_joined, back_qkv.T)
    first_value, first_pull = jax.vjp(layer_norm, values_in, first_gain, first_shift)
    d_input_norm, grad_gain_one, grad_shift_one = first_pull(d_normed1)
    input_grad = d_middle + d_input_norm
    partial_sums = (
        lax.psum_scatter(
            grad_qkv.astype(jnp.bfloat16), "dp", scatter_dimension=0, tiled=True
        ).astype(jnp.float32),
        lax.psum_scatter(
            grad_query_bias.astype(jnp.bfloat16), "dp", scatter_dimension=0, tiled=True
        ).astype(jnp.float32),
        lax.psum_scatter(
            grad_value_bias.astype(jnp.bfloat16), "dp", scatter_dimension=0, tiled=True
        ).astype(jnp.float32),
        lax.psum_scatter(
            grad_out.astype(jnp.bfloat16), "dp", scatter_dimension=0, tiled=True
        ).astype(jnp.float32),
        lax.psum_scatter(
            grad_out_bias.astype(jnp.bfloat16), "dp", scatter_dimension=0, tiled=True
        ).astype(jnp.float32),
        lax.psum_scatter(
            grad_gain_one.astype(jnp.bfloat16), "dp", scatter_dimension=0, tiled=True
        ).astype(jnp.float32),
        lax.psum_scatter(
            grad_shift_one.astype(jnp.bfloat16), "dp", scatter_dimension=0, tiled=True
        ).astype(jnp.float32),
        lax.psum_scatter(
            grad_gain_two.astype(jnp.bfloat16), "dp", scatter_dimension=0, tiled=True
        ).astype(jnp.float32),
        lax.psum_scatter(
            grad_shift_two.astype(jnp.bfloat16), "dp", scatter_dimension=0, tiled=True
        ).astype(jnp.float32),
        lax.psum_scatter(
            grad_up.astype(jnp.bfloat16), "dp", scatter_dimension=0, tiled=True
        ).astype(jnp.float32),
        lax.psum_scatter(
            grad_up_bias.astype(jnp.bfloat16), "dp", scatter_dimension=0, tiled=True
        ).astype(jnp.float32),
        lax.psum_scatter(
            grad_down.astype(jnp.bfloat16), "dp", scatter_dimension=0, tiled=True
        ).astype(jnp.float32),
        lax.psum_scatter(
            grad_down_bias.astype(jnp.bfloat16), "dp", scatter_dimension=0, tiled=True
        ).astype(jnp.float32),
    )
    all_sums = (
        lax.psum_scatter(
            partial_sums[0].astype(jnp.bfloat16), "ctx", scatter_dimension=0, tiled=True
        ).astype(jnp.float32),
        lax.psum_scatter(
            partial_sums[1].astype(jnp.bfloat16), "ctx", scatter_dimension=0, tiled=True
        ).astype(jnp.float32),
        lax.psum_scatter(
            partial_sums[2].astype(jnp.bfloat16), "ctx", scatter_dimension=0, tiled=True
        ).astype(jnp.float32),
        lax.psum_scatter(
            partial_sums[3].astype(jnp.bfloat16), "ctx", scatter_dimension=0, tiled=True
        ).astype(jnp.float32),
        lax.psum_scatter(
            partial_sums[4].astype(jnp.bfloat16), "ctx", scatter_dimension=0, tiled=True
        ).astype(jnp.float32),
        lax.psum_scatter(
            partial_sums[5].astype(jnp.bfloat16), "ctx", scatter_dimension=0, tiled=True
        ).astype(jnp.float32),
        lax.psum_scatter(
            partial_sums[6].astype(jnp.bfloat16), "ctx", scatter_dimension=0, tiled=True
        ).astype(jnp.float32),
        lax.psum_scatter(
            partial_sums[7].astype(jnp.bfloat16), "ctx", scatter_dimension=0, tiled=True
        ).astype(jnp.float32),
        lax.psum_scatter(
            partial_sums[8].astype(jnp.bfloat16), "ctx", scatter_dimension=0, tiled=True
        ).astype(jnp.float32),
        lax.psum_scatter(
            partial_sums[9].astype(jnp.bfloat16), "ctx", scatter_dimension=0, tiled=True
        ).astype(jnp.float32),
        lax.psum_scatter(
            partial_sums[10].astype(jnp.bfloat16), "ctx", scatter_dimension=0, tiled=True
        ).astype(jnp.float32),
        lax.psum_scatter(
            partial_sums[11].astype(jnp.bfloat16), "ctx", scatter_dimension=0, tiled=True
        ).astype(jnp.float32),
        lax.psum_scatter(
            partial_sums[12].astype(jnp.bfloat16), "ctx", scatter_dimension=0, tiled=True
        ).astype(jnp.float32),
    )
    (
        sum_qkv,
        sum_query_bias,
        sum_value_bias,
        sum_out,
        sum_out_bias,
        sum_gain_one,
        sum_shift_one,
        sum_gain_two,
        sum_shift_two,
        sum_up,
        sum_up_bias,
        sum_down,
        sum_down_bias,
    ) = all_sums
    return (
        outputs,
        input_grad,
        sum_qkv,
        sum_query_bias,
        sum_value_bias,
        sum_out,
        sum_out_bias,
        sum_gain_one,
        sum_shift_one,
        sum_gain_two,
        sum_shift_two,
        sum_up,
        sum_up_bias,
        sum_down,
        sum_down_bias,
    )


SEQ = 577
IMAGES = 2
PAIR = 2 * HD
CHUNK = 256


def round_up(count, unit):
    return -(-count // unit) * unit


def chunks_of(count):
    return [(start, min(CHUNK, count - start)) for start in range(0, count, CHUNK)]


def nt_dot(left, right):
    return lax.dot_general(
        left, right, (((1,), (1,)), ((), ())), preferred_element_type=jnp.float32
    )


def half_mask(rows):
    return lax.broadcasted_iota(jnp.int32, (rows, PAIR), 1) < HD


def forward_kernel(query_ref, key_ref, value_ref, bias_ref, attended_ref, log_ref):
    rows = query_ref.shape[0]
    first = half_mask(rows)
    zero = jnp.zeros((rows, PAIR), jnp.bfloat16)
    key = key_ref[...]
    key_sides = (jnp.where(first, key, zero), jnp.where(first, zero, key))
    value_t = value_ref[...].astype(jnp.float32).T.astype(jnp.bfloat16)
    scale = jnp.bfloat16(1.0 / math.sqrt(HD))
    for start, size in chunks_of(rows):
        query = query_ref[start : start + size, :] * scale
        bias = bias_ref[:, start : start + size]
        outs = []
        for side in range(2):
            scores = nt_dot(key_sides[side], query) + bias
            top = jnp.max(scores, axis=0, keepdims=True)
            expo = jnp.exp(scores - top)
            total = jnp.sum(expo, axis=0, keepdims=True)
            probs_low = (expo * (1.0 / total)).astype(jnp.bfloat16)
            outs.append(matmul(value_t[side * HD : (side + 1) * HD, :], probs_low))
            log_ref[0, side : side + 1, start : start + size] = top + jnp.log(total)
        mixed = jnp.concatenate(outs, axis=0)
        attended_ref[start : start + size, :] = mixed.T.astype(jnp.bfloat16)


def backward_kernel(
    query_ref, key_ref, value_ref, d_ref, log_ref, bias_ref, dq_ref, dk_ref, dv_ref, dk_sum, dv_sum
):
    rows = query_ref.shape[0]
    first = half_mask(rows)
    zero = jnp.zeros((rows, PAIR), jnp.bfloat16)
    key = key_ref[...]
    value = value_ref[...]
    key_sides = (jnp.where(first, key, zero), jnp.where(first, zero, key))
    value_sides = (jnp.where(first, value, zero), jnp.where(first, zero, value))
    key_t = key.astype(jnp.float32).T.astype(jnp.bfloat16)
    scale = jnp.bfloat16(1.0 / math.sqrt(HD))
    for start, size in chunks_of(rows):
        query = query_ref[start : start + size, :] * scale
        d_rows = d_ref[start : start + size, :]
        bias = bias_ref[:, start : start + size]
        outs = []
        for side in range(2):
            scores = nt_dot(key_sides[side], query) + bias
            probs = jnp.exp(scores - log_ref[0, side : side + 1, start : start + size])
            d_probs = nt_dot(value_sides[side], d_rows)
            product = probs * d_probs
            delta = jnp.sum(product, axis=0, keepdims=True)
            d_scores = (product - probs * delta).astype(jnp.bfloat16)
            d_value = matmul(probs.astype(jnp.bfloat16), d_rows)
            d_key = matmul(d_scores, query)
            if start == 0:
                dv_sum[side] = d_value
                dk_sum[side] = d_key
            else:
                dv_sum[side] += d_value
                dk_sum[side] += d_key
            outs.append(matmul(key_t[side * HD : (side + 1) * HD, :], d_scores))
        d_query = jnp.concatenate(outs, axis=0) * (1.0 / math.sqrt(HD))
        dq_ref[start : start + size, :] = d_query.T.astype(jnp.bfloat16)
    dk_ref[...] = jnp.where(first, dk_sum[0], dk_sum[1]).astype(jnp.bfloat16)
    dv_ref[...] = jnp.where(first, dv_sum[0], dv_sum[1]).astype(jnp.bfloat16)


def attention_forward(joined, bias):
    rows, width = joined.shape[0], joined.shape[1] // 3
    pairs = width // PAIR
    flops = 4 * rows * rows * width
    return pl.pallas_call(
        forward_kernel,
        grid=(pairs,),
        in_specs=[
            pl.BlockSpec((rows, PAIR), lambda i: (0, i)),
            pl.BlockSpec((rows, PAIR), lambda i: (0, pairs + i)),
            pl.BlockSpec((rows, PAIR), lambda i: (0, 2 * pairs + i)),
            pl.BlockSpec((rows, rows), lambda i: (0, 0)),
        ],
        out_specs=[
            pl.BlockSpec((rows, PAIR), lambda i: (0, i)),
            pl.BlockSpec((1, 2, rows), lambda i: (i, 0, 0)),
        ],
        out_shape=[
            jax.ShapeDtypeStruct((rows, width), jnp.bfloat16),
            jax.ShapeDtypeStruct((pairs, 2, rows), jnp.float32),
        ],
        compiler_params=pltpu.CompilerParams(vmem_limit_bytes=40 * 2**20),
        cost_estimate=pl.CostEstimate(
            flops=4 * flops, bytes_accessed=8 * rows * width, transcendentals=rows * rows * 16
        ),
        name="attention_forward",
    )(joined, joined, joined, bias)


def attention_backward(joined, d_attended, log_total, bias):
    rows, width = d_attended.shape
    pairs = width // PAIR
    flops = 10 * rows * rows * width
    block = jax.ShapeDtypeStruct((rows, width), jnp.bfloat16)
    return pl.pallas_call(
        backward_kernel,
        grid=(pairs,),
        in_specs=[
            pl.BlockSpec((rows, PAIR), lambda i: (0, i)),
            pl.BlockSpec((rows, PAIR), lambda i: (0, pairs + i)),
            pl.BlockSpec((rows, PAIR), lambda i: (0, 2 * pairs + i)),
            pl.BlockSpec((rows, PAIR), lambda i: (0, i)),
            pl.BlockSpec((1, 2, rows), lambda i: (i, 0, 0)),
            pl.BlockSpec((rows, rows), lambda i: (0, 0)),
        ],
        out_specs=[pl.BlockSpec((rows, PAIR), lambda i: (0, i))] * 3,
        out_shape=[block] * 3,
        scratch_shapes=[pltpu.VMEM((2, rows, PAIR), jnp.float32)] * 2,
        compiler_params=pltpu.CompilerParams(vmem_limit_bytes=40 * 2**20),
        cost_estimate=pl.CostEstimate(
            flops=4 * flops, bytes_accessed=14 * rows * width, transcendentals=rows * rows * 16
        ),
        name="attention_backward",
    )(joined, joined, joined, d_attended, log_total, bias)


def standardize(value):
    center = value - jnp.mean(value, axis=-1, keepdims=True)
    variance = jnp.mean(center * center, axis=-1, keepdims=True)
    scale = lax.rsqrt(variance + EPSILON)
    return center * scale, scale


def norm_backward(d_normed, normal, scale, gain):
    scaled = d_normed * gain
    mean = jnp.mean(scaled, axis=-1, keepdims=True)
    along = jnp.mean(scaled * normal, axis=-1, keepdims=True)
    return (scaled - mean - normal * along) * scale


def gelu_slope(value):
    phi = 0.5 * (1.0 + lax.erf(value * math.sqrt(0.5)))
    return phi + value * jnp.exp(-0.5 * value * value) * (1.0 / math.sqrt(2.0 * math.pi))


def to_local(array, axis, far):
    shape = array.shape
    cut = shape[:axis] + (far, 2, 2, 2, shape[axis] // (8 * far)) + shape[axis + 1 :]
    spots = [axis + 2, axis + 1, axis + 3, axis]
    spots = list(range(axis)) + spots + list(range(axis + 4, len(cut)))
    return array.reshape(cut).transpose(spots).reshape(shape)


def to_natural(array, axis, far):
    shape = array.shape
    cut = shape[:axis] + (2, 2, 2, far, shape[axis] // (8 * far)) + shape[axis + 1 :]
    spots = [axis + 3, axis + 1, axis, axis + 2]
    spots = list(range(axis)) + spots + list(range(axis + 4, len(cut)))
    return array.reshape(cut).transpose(spots).reshape(shape)


def assemble_kernel(index_ref, *refs):
    pieces, (*wholes, stage, arrived, left) = refs[: index_ref.shape[0]], refs[index_ref.shape[0] :]
    incoming = [
        pltpu.make_async_copy(piece, stage.at[number], arrived.at[number])
        for number, piece in enumerate(pieces)
    ]
    for copy in incoming:
        copy.start()
    outgoing = []
    for number, piece in enumerate(pieces):
        incoming[number].wait()
        size = piece.shape[0]
        start = pl.multiple_of(index_ref[number] * size, 16)
        column = 0
        for part, whole in enumerate(wholes):
            width = whole.shape[1]
            copy = pltpu.make_async_copy(
                stage.at[number, :, pl.ds(column, width)],
                whole.at[pl.ds(start, size)],
                left.at[part, number],
            )
            copy.start()
            outgoing.append(copy)
            column += width
    for copy in outgoing:
        copy.wait()


def assemble(pieces, indices, extra=0):
    size, width = pieces[0].shape
    count = len(pieces)
    widths = (width - extra, extra) if extra else (width,)
    anywhere = pl.BlockSpec(memory_space=pl.ANY)
    wholes = pl.pallas_call(
        assemble_kernel,
        in_specs=[pl.BlockSpec(memory_space=pltpu.SMEM)] + [anywhere] * count,
        out_specs=[anywhere] * len(widths),
        out_shape=[jax.ShapeDtypeStruct((count * size, one), pieces[0].dtype) for one in widths],
        scratch_shapes=[
            pltpu.VMEM((count, size, width), pieces[0].dtype),
            pltpu.SemaphoreType.DMA((count,)),
            pltpu.SemaphoreType.DMA((len(widths), count)),
        ],
        compiler_params=pltpu.CompilerParams(vmem_limit_bytes=16 * 2**20),
        cost_estimate=pl.CostEstimate(
            flops=0, bytes_accessed=4 * count * size * width, transcendentals=0
        ),
        name="assemble",
    )(jnp.stack(indices).astype(jnp.int32), *pieces)
    return wholes if extra else wholes[0]


def trade(array, axis):
    return lax.ppermute(array, axis, [(0, 1), (1, 0)])


def after(array, other):
    return lax.optimization_barrier((array, other))[0]


def gather_far(shard, far):
    place = lax.axis_index("z")
    pieces, indices = [shard], [place]
    for step in range(1, far):
        pieces.append(lax.ppermute(shard, "z", [(i, (i + step) % far) for i in range(far)]))
        indices.append((place - step) % far)
    return assemble(pieces, indices)


SPOT = {"core": 4, "x": 2, "ctx": 1}


def spread(blocks, axis):
    return blocks | {key ^ SPOT[axis]: trade(block, axis) for key, block in blocks.items()}


def order_blocks(blocks, extra=0):
    own = sum(spot * lax.axis_index(axis) for axis, spot in SPOT.items())
    return assemble(list(blocks.values()), [own ^ key for key in blocks], extra)


def send_half(matrix, axis, outer=1):
    rows, width = matrix.shape
    place = lax.axis_index(axis)
    blocks = matrix.reshape(outer, 2, rows // (2 * outer), width)
    kept = lax.dynamic_index_in_dim(blocks, place, 1, False).reshape(rows // 2, width)
    sent = lax.dynamic_index_in_dim(blocks, 1 - place, 1, False).reshape(rows // 2, width)
    return kept, trade(sent, axis)


def add_half(halves, follow=None):
    kept, got = halves
    if follow is not None:
        got = after(got, follow)
    return (kept.astype(jnp.float32) + got.astype(jnp.float32)).astype(kept.dtype)


def send_far(matrix, far):
    size = matrix.shape[0] // far
    place = lax.axis_index("z")
    arrays = [lax.dynamic_slice_in_dim(matrix, place * size, size)]
    for step in range(1, far):
        sent = lax.dynamic_slice_in_dim(matrix, ((place + step) % far) * size, size)
        arrays.append(lax.ppermute(sent, "z", [(i, (i + step) % far) for i in range(far)]))
    return arrays


def add_far(arrays):
    return sum(array.astype(jnp.float32) for array in arrays)


def column_sums(array):
    return jnp.sum(array.astype(jnp.float32), axis=0)


def by_image(far):
    def on_device(
        inputs,
        cotangent,
        segment,
        w_qkv,
        b_query,
        b_value,
        w_out,
        b_out,
        norm1_gain,
        norm1_shift,
        norm2_gain,
        norm2_shift,
        w_up,
        b_up,
        w_down,
        b_down,
    ):
        place = lax.axis_index("ctx")
        swap = lambda array: trade(array, "ctx")
        slots, width = inputs.shape
        pads = 2 * slots - IMAGES * SEQ
        rows = round_up(SEQ + pads, 16)
        near_width = w_up.shape[0] // 8

        segment_far = swap(segment)
        inputs_far = swap(inputs)
        small = jnp.concatenate(
            [b_query, b_value, b_out, norm1_gain, norm1_shift, norm2_gain, norm2_shift, b_down, b_up]
        )
        shard_qkv = unfold(w_qkv)
        shard_rows = shard_qkv.shape[0]
        small = small.reshape(shard_rows, -1)
        small_width = small.shape[1]
        extra = round_up(small_width, 128)
        small = jnp.pad(small, ((0, 0), (0, extra - small_width)))
        far_qkv = gather_far(jnp.concatenate([shard_qkv, small], axis=1), far)
        far_out = gather_far(to_local(after(unfold(w_out), far_qkv), 1, far), far)
        far_down = gather_far(to_local(after(unfold(w_down), far_qkv), 1, far), far)
        far_up = gather_far(to_local(after(unfold(w_up), far_down), 1, far), far)
        far_qkv = after(far_qkv, inputs_far)
        qkv_blocks = spread(spread({0: far_qkv}, "x"), "ctx")
        out_blocks = spread(spread({0: far_out}, "ctx"), "x")
        down_blocks = spread({0: far_down}, "x")
        up_blocks = spread({0: after(far_up, qkv_blocks[3])}, "ctx")
        up_blocks = spread(up_blocks, "x")
        down_blocks = spread(
            {key: after(block, up_blocks[1]) for key, block in down_blocks.items()}, "ctx"
        )
        qkv_weight, small_local = order_blocks(spread(qkv_blocks, "core"), extra)
        out_weight = to_natural(order_blocks(spread(out_blocks, "core")), 0, far)
        up_blocks = spread(up_blocks, "core")
        down_blocks = spread(down_blocks, "core")

        small_core = small_local[:, :small_width].astype(jnp.float32).reshape(8 * far, -1)
        small_all = to_natural(small_core, 0, far)
        piece = lambda table, index: table[:, index * near_width : (index + 1) * near_width].reshape(-1)
        query_bias = piece(small_all, 0)
        value_bias = piece(small_all, 1)
        out_bias, first_gain, first_shift, second_gain, second_shift, down_bias = (
            piece(small_core, index) for index in range(2, 8)
        )
        up_bias = small_core[:, 8 * near_width :].reshape(-1)

        slot = jnp.arange(slots)
        earlier = slot[:, None] < slot[None, :]

        def ranks(own, far, far_first):
            inside = jnp.sum((own[:, None] == own[None, :]) & earlier, axis=0)
            outside = jnp.sum(far[:, None] == own[None, :], axis=0)
            return inside + jnp.where(far_first, outside, 0)

        rank_near = ranks(segment, segment_far, place == 1)
        rank_far = ranks(segment_far, segment, place == 0)

        def positions(ids, rank, image):
            return jnp.where(ids == image, rank, jnp.where(ids < 0, SEQ + rank, -1))

        row = jnp.arange(rows)
        pick_near = (positions(segment, rank_near, place)[None, :] == row[:, None])
        pick_far = (positions(segment_far, rank_far, place)[None, :] == row[:, None])
        pick_near, pick_far = pick_near.astype(jnp.bfloat16), pick_far.astype(jnp.bfloat16)
        give_near = (positions(segment, rank_near, place)[:, None] == row[None, :])
        other_image = jnp.where(segment == 1 - place, rank_near, -1)
        give_far = other_image[:, None] == row[None, :]
        give_near, give_far = give_near.astype(jnp.bfloat16), give_far.astype(jnp.bfloat16)
        column = jnp.arange(width)
        order = to_local(column, 0, far)
        to_core = (column[:, None] == order[None, :]).astype(jnp.bfloat16)

        def take(near, far):
            picked = matmul(pick_near, near) + matmul(pick_far, far)
            return matmul(picked.astype(jnp.bfloat16), to_core)

        def to_give(array):
            natural = nt_dot(array.astype(jnp.bfloat16), to_core).astype(jnp.bfloat16)
            return natural, swap(natural)

        def give(both, follow):
            near, far_rows = both
            return matmul(give_near, near) + matmul(give_far, after(far_rows, follow))

        kind = (row >= SEQ).astype(jnp.int32) + (row >= SEQ + pads).astype(jnp.int32)
        bias = jnp.where(kind[:, None] == kind[None, :], 0.0, -1e30).astype(jnp.float32)

        values_in = take(inputs, inputs_far)
        normal1, scale1 = standardize(values_in)
        normed1 = (normal1 * first_gain + first_shift).astype(jnp.bfloat16)
        joined_bias = jnp.concatenate([query_bias, jnp.zeros_like(query_bias), value_bias])
        joined = (matmul(normed1, qkv_weight) + joined_bias).astype(jnp.bfloat16)
        attended, log_total = attention_forward(joined, bias)
        middle = values_in + matmul(attended, out_weight) + out_bias
        normal2, scale2 = standardize(middle)
        normed2 = (normal2 * second_gain + second_shift).astype(jnp.bfloat16)
        up_weight = order_blocks(up_blocks)
        hidden = matmul(normed2, up_weight) + up_bias
        active = gelu_exact(hidden).astype(jnp.bfloat16)
        slope = gelu_slope(hidden).astype(jnp.bfloat16)
        down_weight = order_blocks(down_blocks)

        live = (row < SEQ).astype(jnp.float32)[:, None]
        cotangent_far = swap(after(cotangent, joined))
        d_out = take(cotangent, cotangent_far) * live
        d_out_low = d_out.astype(jnp.bfloat16)
        grad_down = matmul(active.T, d_out_low).astype(jnp.bfloat16)
        down_core = send_half(grad_down, "core")
        last = middle + matmul(after(active, grad_down), down_weight) + down_bias
        last_given = to_give(last)
        d_hidden = (
            matmul(after(d_out_low, last_given[0]), down_weight.T) * slope.astype(jnp.float32)
        ).astype(jnp.bfloat16)
        grad_up = matmul(normed2.T, d_hidden).astype(jnp.bfloat16)
        up_core = send_half(grad_up, "core")
        down_x = send_half(add_half(down_core, grad_up), "x")
        d_normed2 = matmul(after(d_hidden, down_x[0]), up_weight.T)
        d_middle = d_out + norm_backward(d_normed2, normal2, scale2, second_gain)
        d_branch = d_middle.astype(jnp.bfloat16)
        up_y = send_half(add_half(up_core, d_branch), "ctx", 2)
        grad_out = to_local(matmul(attended.T, after(d_branch, up_y[0])).astype(jnp.bfloat16), 0, far)
        out_core = send_half(grad_out, "core")
        d_attended = matmul(d_branch, out_weight.T).astype(jnp.bfloat16)
        out_x = send_half(add_half(out_core, d_attended), "x")
        d_query, d_key, d_value = attention_backward(
            joined, after(d_attended, out_x[0]), log_total, bias
        )
        outputs = give(last_given, d_query).astype(jnp.bfloat16)
        d_joined = jnp.concatenate([d_query, d_key, d_value], axis=1)
        out_y = send_half(add_half(out_x, d_joined), "ctx")
        grad_qkv = matmul(normed1.T, d_joined).astype(jnp.bfloat16)
        qkv_core = send_half(grad_qkv, "core")
        down_y = send_half(add_half(down_x, grad_qkv), "ctx")
        d_normed1 = matmul(after(d_joined, grad_qkv), qkv_weight.T)
        d_last = d_middle + norm_backward(d_normed1, normal1, scale1, first_gain)
        d_last_given = to_give(d_last)
        qkv_x = send_half(add_half(qkv_core, d_last_given[0]), "x")
        up_x = send_half(add_half(up_y, qkv_x[0]), "x")
        out_far = send_far(add_half(out_y, up_x[0]), far)
        down_far = send_far(add_half(down_y, out_far[0]), far)
        up_far = send_far(add_half(up_x, down_far[0]), far)
        qkv_y = send_half(add_half(qkv_x, up_far[0]), "ctx")
        qkv_far = send_far(add_half(qkv_y), far)
        sum_down, sum_up, sum_out, sum_qkv = (
            add_far(arrays) for arrays in (down_far, up_far, out_far, qkv_far)
        )
        input_grad = give(d_last_given, qkv_far[0])

        part = lambda vector: vector.reshape(8 * far, -1)
        core_sums = jnp.concatenate(
            [
                part(vector)
                for vector in (
                    column_sums(d_branch),
                    column_sums(d_normed1 * normal1),
                    column_sums(d_normed1),
                    column_sums(d_normed2 * normal2),
                    column_sums(d_normed2),
                    column_sums(d_out_low),
                    column_sums(d_hidden),
                )
            ],
            axis=1,
        )
        chip_sums = jnp.concatenate([part(column_sums(d_query)), part(column_sums(d_value))], axis=1)
        small_sums = jnp.concatenate([to_local(chip_sums, 0, far), core_sums], axis=1)
        for axis in ("core", "x", "ctx"):
            small_sums = add_half(send_half(small_sums, axis))
        small_sums = add_far(send_far(small_sums, far))[0]
        own = lambda index: small_sums[index * near_width : (index + 1) * near_width]
        back = lambda matrix: refold(to_natural(matrix, 1, far))
        return (
            outputs,
            input_grad,
            refold(sum_qkv),
            own(0),
            own(1),
            back(sum_out),
            own(2),
            own(3),
            own(4),
            own(5),
            own(6),
            back(sum_up),
            small_sums[8 * near_width :],
            back(sum_down),
            own(7),
        )

    return on_device


def solution(mesh):
    if mesh.shape["ctx"] == IMAGES and mesh.shape["dp"] % 4 == 0:
        far, axes = mesh.shape["dp"] // 4, ("z", "x", "core", "ctx")
        mesh = jax.sharding.Mesh(mesh.devices.reshape(far, 2, 2, IMAGES), axes)
        body = by_image(far)
    else:
        body, axes = on_device, ("dp", "ctx")
    matrix, vector = P(axes, None), P(axes)
    return jax.shard_map(
        body,
        mesh=mesh,
        in_specs=(matrix, matrix, vector, matrix, vector, vector, matrix)
        + (vector,) * 5
        + (matrix, vector, matrix, vector),
        out_specs=(matrix, matrix, matrix, vector, vector, matrix)
        + (vector,) * 5
        + (matrix, vector, matrix, vector),
        check_vma=False,
    )
```

```python
import math

import jax
import jax.numpy as jnp
from jax import lax
from jax.experimental import pallas as pl
from jax.experimental.pallas import tpu as pltpu
from jax.sharding import PartitionSpec as P

HD = 64


EPSILON = 1e-06


def layer_norm(value, gain, shift):
    center = value - jnp.mean(value, axis=-1, keepdims=True)
    variance = jnp.mean(center * center, axis=-1, keepdims=True)
    return center * lax.rsqrt(variance + EPSILON) * gain + shift


def gelu_exact(value):
    return jax.nn.gelu(value, approximate=False)


def matmul(left, right):
    return jnp.dot(left, right, preferred_element_type=jnp.float32)


def unfold(stored):
    return stored.reshape(stored.shape[0] // 8, stored.shape[1] * 8)


def refold(matrix):
    return matrix.reshape(matrix.shape[0] * 8, matrix.shape[1] // 8)


def on_device(
    inputs,
    cotangent,
    segment,
    w_qkv,
    b_query,
    b_value,
    w_out,
    b_out,
    norm1_gain,
    norm1_shift,
    norm2_gain,
    norm2_shift,
    w_up,
    b_up,
    w_down,
    b_down,
):
    gathered = (
        lax.all_gather(w_qkv, ("dp", "ctx"), axis=0, tiled=True),
        lax.all_gather(b_query, ("dp", "ctx"), axis=0, tiled=True),
        lax.all_gather(b_value, ("dp", "ctx"), axis=0, tiled=True),
        lax.all_gather(w_out, ("dp", "ctx"), axis=0, tiled=True),
        lax.all_gather(b_out, ("dp", "ctx"), axis=0, tiled=True),
        lax.all_gather(norm1_gain, ("dp", "ctx"), axis=0, tiled=True),
        lax.all_gather(norm1_shift, ("dp", "ctx"), axis=0, tiled=True),
        lax.all_gather(norm2_gain, ("dp", "ctx"), axis=0, tiled=True),
        lax.all_gather(norm2_shift, ("dp", "ctx"), axis=0, tiled=True),
        lax.all_gather(w_up, ("dp", "ctx"), axis=0, tiled=True),
        lax.all_gather(b_up, ("dp", "ctx"), axis=0, tiled=True),
        lax.all_gather(w_down, ("dp", "ctx"), axis=0, tiled=True),
        lax.all_gather(b_down, ("dp", "ctx"), axis=0, tiled=True),
    )
    (
        qkv_stored,
        query_bias,
        value_bias,
        out_stored,
        out_bias,
        gain_one,
        shift_one,
        gain_two,
        shift_two,
        up_stored,
        up_bias,
        down_stored,
        down_bias,
    ) = gathered
    qkv_weight = unfold(qkv_stored)
    out_weight = unfold(out_stored)
    up_weight = unfold(up_stored)
    down_weight = unfold(down_stored)
    first_gain = gain_one.astype(jnp.float32)
    first_shift = shift_one.astype(jnp.float32)
    second_gain = gain_two.astype(jnp.float32)
    second_shift = shift_two.astype(jnp.float32)
    row_count = inputs.shape[0]
    model_width = out_weight.shape[0]
    head_count = model_width // HD
    score_scale = 1.0 / math.sqrt(HD)
    values_in = inputs.astype(jnp.float32)
    normed1 = layer_norm(values_in, first_gain, first_shift).astype(jnp.bfloat16)
    joined = matmul(normed1, qkv_weight)
    queries = (joined[:, :model_width] + query_bias.astype(jnp.float32)).astype(jnp.bfloat16)
    key_rows = joined[:, model_width : 2 * model_width].astype(jnp.bfloat16)
    value_rows = (joined[:, 2 * model_width :] + value_bias.astype(jnp.float32)).astype(
        jnp.bfloat16
    )
    key_all, value_all, seg_all = (
        lax.all_gather(key_rows, "ctx", axis=0, tiled=True),
        lax.all_gather(value_rows, "ctx", axis=0, tiled=True),
        lax.all_gather(segment.astype(jnp.bfloat16), "ctx", axis=0, tiled=True),
    )
    key_count = key_all.shape[0]
    query_heads = queries.reshape(row_count, head_count, HD)
    key_heads = key_all.reshape(key_count, head_count, HD)
    value_heads = value_all.reshape(key_count, head_count, HD)
    own_seg = segment.astype(jnp.float32)
    group_seg = seg_all.astype(jnp.float32)
    same_seg = own_seg[:, None] == group_seg[None, :]

    def make_scores():
        raw = (
            jnp.einsum("qhd,khd->hqk", query_heads, key_heads, preferred_element_type=jnp.float32)
            * score_scale
        )
        return jnp.where(same_seg[None], raw, -1e30)

    scores = make_scores()
    row_max = jnp.max(scores, axis=-1, keepdims=True)
    expo = jnp.exp(scores - row_max)
    row_total = jnp.sum(expo, axis=-1, keepdims=True)
    probs_low = (expo / row_total).astype(jnp.bfloat16)
    log_total = row_max + jnp.log(row_total)
    mixed = jnp.einsum("hqk,khd->qhd", probs_low, value_heads, preferred_element_type=jnp.float32)
    attended = mixed.reshape(row_count, model_width).astype(jnp.bfloat16)
    middle = values_in + matmul(attended, out_weight) + out_bias.astype(jnp.float32)
    normed2 = layer_norm(middle, second_gain, second_shift).astype(jnp.bfloat16)
    hidden = matmul(normed2, up_weight) + up_bias.astype(jnp.float32)
    active = gelu_exact(hidden).astype(jnp.bfloat16)
    outputs = (middle + matmul(active, down_weight) + down_bias.astype(jnp.float32)).astype(
        jnp.bfloat16
    )
    back_qkv, back_out, back_up, back_down = (qkv_weight, out_weight, up_weight, down_weight)
    valid = (segment >= 0).astype(jnp.float32)[:, None]
    d_out = cotangent.astype(jnp.float32) * valid
    d_out_low = d_out.astype(jnp.bfloat16)
    grad_down = refold(matmul(active.T, d_out_low))
    grad_down_bias = jnp.sum(d_out_low.astype(jnp.float32), axis=0)
    d_active = matmul(d_out_low, back_down.T)
    gelu_value, gelu_pull = jax.vjp(gelu_exact, hidden)
    d_hidden = gelu_pull(d_active)[0].astype(jnp.bfloat16)
    grad_up = refold(matmul(normed2.T, d_hidden))
    grad_up_bias = jnp.sum(d_hidden.astype(jnp.float32), axis=0)
    d_normed2 = matmul(d_hidden, back_up.T)
    norm_value, norm_pull = jax.vjp(layer_norm, middle, second_gain, second_shift)
    d_middle_norm, grad_gain_two, grad_shift_two = norm_pull(d_normed2)
    d_middle = d_out + d_middle_norm
    d_branch = d_middle.astype(jnp.bfloat16)
    grad_out = refold(matmul(attended.T, d_branch))
    grad_out_bias = jnp.sum(d_branch.astype(jnp.float32), axis=0)
    d_attended_flat = matmul(d_branch, back_out.T).astype(jnp.bfloat16)
    d_attended = d_attended_flat.reshape(row_count, head_count, HD)
    scores = make_scores()
    probs = jnp.exp(scores - log_total)
    d_probs = jnp.einsum(
        "qhd,khd->hqk", d_attended, value_heads, preferred_element_type=jnp.float32
    )
    delta_rows = jnp.sum(probs * d_probs, axis=-1, keepdims=True)
    d_scores = (probs * (d_probs - delta_rows)).astype(jnp.bfloat16)
    d_query = (
        jnp.einsum("hqk,khd->qhd", d_scores, key_heads, preferred_element_type=jnp.float32)
        * score_scale
    ).reshape(row_count, model_width)
    probs_again = probs.astype(jnp.bfloat16)
    d_key_all = (
        jnp.einsum("hqk,qhd->khd", d_scores, query_heads, preferred_element_type=jnp.float32)
        * score_scale
    ).reshape(key_count, model_width)
    d_value_all = jnp.einsum(
        "hqk,qhd->khd", probs_again, d_attended, preferred_element_type=jnp.float32
    ).reshape(key_count, model_width)
    d_key, d_value = (
        lax.psum_scatter(
            d_key_all.astype(jnp.bfloat16), "ctx", scatter_dimension=0, tiled=True
        ).astype(jnp.float32),
        lax.psum_scatter(
            d_value_all.astype(jnp.bfloat16), "ctx", scatter_dimension=0, tiled=True
        ).astype(jnp.float32),
    )
    d_query_low = d_query.astype(jnp.bfloat16)
    d_value_low = d_value.astype(jnp.bfloat16)
    d_joined = jnp.concatenate([d_query_low, d_key.astype(jnp.bfloat16), d_value_low], axis=1)
    grad_qkv = refold(matmul(normed1.T, d_joined))
    grad_query_bias = jnp.sum(d_query_low.astype(jnp.float32), axis=0)
    grad_value_bias = jnp.sum(d_value_low.astype(jnp.float32), axis=0)
    d_normed1 = matmul(d_joined, back_qkv.T)
    first_value, first_pull = jax.vjp(layer_norm, values_in, first_gain, first_shift)
    d_input_norm, grad_gain_one, grad_shift_one = first_pull(d_normed1)
    input_grad = d_middle + d_input_norm
    partial_sums = (
        lax.psum_scatter(
            grad_qkv.astype(jnp.bfloat16), "dp", scatter_dimension=0, tiled=True
        ).astype(jnp.float32),
        lax.psum_scatter(
            grad_query_bias.astype(jnp.bfloat16), "dp", scatter_dimension=0, tiled=True
        ).astype(jnp.float32),
        lax.psum_scatter(
            grad_value_bias.astype(jnp.bfloat16), "dp", scatter_dimension=0, tiled=True
        ).astype(jnp.float32),
        lax.psum_scatter(
            grad_out.astype(jnp.bfloat16), "dp", scatter_dimension=0, tiled=True
        ).astype(jnp.float32),
        lax.psum_scatter(
            grad_out_bias.astype(jnp.bfloat16), "dp", scatter_dimension=0, tiled=True
        ).astype(jnp.float32),
        lax.psum_scatter(
            grad_gain_one.astype(jnp.bfloat16), "dp", scatter_dimension=0, tiled=True
        ).astype(jnp.float32),
        lax.psum_scatter(
            grad_shift_one.astype(jnp.bfloat16), "dp", scatter_dimension=0, tiled=True
        ).astype(jnp.float32),
        lax.psum_scatter(
            grad_gain_two.astype(jnp.bfloat16), "dp", scatter_dimension=0, tiled=True
        ).astype(jnp.float32),
        lax.psum_scatter(
            grad_shift_two.astype(jnp.bfloat16), "dp", scatter_dimension=0, tiled=True
        ).astype(jnp.float32),
        lax.psum_scatter(
            grad_up.astype(jnp.bfloat16), "dp", scatter_dimension=0, tiled=True
        ).astype(jnp.float32),
        lax.psum_scatter(
            grad_up_bias.astype(jnp.bfloat16), "dp", scatter_dimension=0, tiled=True
        ).astype(jnp.float32),
        lax.psum_scatter(
            grad_down.astype(jnp.bfloat16), "dp", scatter_dimension=0, tiled=True
        ).astype(jnp.float32),
        lax.psum_scatter(
            grad_down_bias.astype(jnp.bfloat16), "dp", scatter_dimension=0, tiled=True
        ).astype(jnp.float32),
    )
    all_sums = (
        lax.psum_scatter(
            partial_sums[0].astype(jnp.bfloat16), "ctx", scatter_dimension=0, tiled=True
        ).astype(jnp.float32),
        lax.psum_scatter(
            partial_sums[1].astype(jnp.bfloat16), "ctx", scatter_dimension=0, tiled=True
        ).astype(jnp.float32),
        lax.psum_scatter(
            partial_sums[2].astype(jnp.bfloat16), "ctx", scatter_dimension=0, tiled=True
        ).astype(jnp.float32),
        lax.psum_scatter(
            partial_sums[3].astype(jnp.bfloat16), "ctx", scatter_dimension=0, tiled=True
        ).astype(jnp.float32),
        lax.psum_scatter(
            partial_sums[4].astype(jnp.bfloat16), "ctx", scatter_dimension=0, tiled=True
        ).astype(jnp.float32),
        lax.psum_scatter(
            partial_sums[5].astype(jnp.bfloat16), "ctx", scatter_dimension=0, tiled=True
        ).astype(jnp.float32),
        lax.psum_scatter(
            partial_sums[6].astype(jnp.bfloat16), "ctx", scatter_dimension=0, tiled=True
        ).astype(jnp.float32),
        lax.psum_scatter(
            partial_sums[7].astype(jnp.bfloat16), "ctx", scatter_dimension=0, tiled=True
        ).astype(jnp.float32),
        lax.psum_scatter(
            partial_sums[8].astype(jnp.bfloat16), "ctx", scatter_dimension=0, tiled=True
        ).astype(jnp.float32),
        lax.psum_scatter(
            partial_sums[9].astype(jnp.bfloat16), "ctx", scatter_dimension=0, tiled=True
        ).astype(jnp.float32),
        lax.psum_scatter(
            partial_sums[10].astype(jnp.bfloat16), "ctx", scatter_dimension=0, tiled=True
        ).astype(jnp.float32),
        lax.psum_scatter(
            partial_sums[11].astype(jnp.bfloat16), "ctx", scatter_dimension=0, tiled=True
        ).astype(jnp.float32),
        lax.psum_scatter(
            partial_sums[12].astype(jnp.bfloat16), "ctx", scatter_dimension=0, tiled=True
        ).astype(jnp.float32),
    )
    (
        sum_qkv,
        sum_query_bias,
        sum_value_bias,
        sum_out,
        sum_out_bias,
        sum_gain_one,
        sum_shift_one,
        sum_gain_two,
        sum_shift_two,
        sum_up,
        sum_up_bias,
        sum_down,
        sum_down_bias,
    ) = all_sums
    return (
        outputs,
        input_grad,
        sum_qkv,
        sum_query_bias,
        sum_value_bias,
        sum_out,
        sum_out_bias,
        sum_gain_one,
        sum_shift_one,
        sum_gain_two,
        sum_shift_two,
        sum_up,
        sum_up_bias,
        sum_down,
        sum_down_bias,
    )


SEQ = 577
IMAGES = 2
PAIR = 2 * HD
CHUNK = 256


def round_up(count, unit):
    return -(-count // unit) * unit


def chunks_of(count):
    return [(start, min(CHUNK, count - start)) for start in range(0, count, CHUNK)]


def nt_dot(left, right):
    return lax.dot_general(
        left, right, (((1,), (1,)), ((), ())), preferred_element_type=jnp.float32
    )


def half_mask(rows):
    return lax.broadcasted_iota(jnp.int32, (rows, PAIR), 1) < HD


def forward_kernel(query_ref, key_ref, value_ref, bias_ref, attended_ref, log_ref):
    rows = query_ref.shape[0]
    first = half_mask(rows)
    zero = jnp.zeros((rows, PAIR), jnp.bfloat16)
    key = key_ref[...]
    key_sides = (jnp.where(first, key, zero), jnp.where(first, zero, key))
    value_t = value_ref[...].astype(jnp.float32).T.astype(jnp.bfloat16)
    scale = jnp.bfloat16(1.0 / math.sqrt(HD))
    for start, size in chunks_of(rows):
        query = query_ref[start : start + size, :] * scale
        bias = bias_ref[:, start : start + size]
        outs = []
        for side in range(2):
            scores = nt_dot(key_sides[side], query) + bias
            top = jnp.max(scores, axis=0, keepdims=True)
            expo = jnp.exp(scores - top)
            total = jnp.sum(expo, axis=0, keepdims=True)
            probs_low = (expo * (1.0 / total)).astype(jnp.bfloat16)
            outs.append(matmul(value_t[side * HD : (side + 1) * HD, :], probs_low))
            log_ref[0, side : side + 1, start : start + size] = top + jnp.log(total)
        mixed = jnp.concatenate(outs, axis=0)
        attended_ref[start : start + size, :] = mixed.T.astype(jnp.bfloat16)


def backward_kernel(
    query_ref, key_ref, value_ref, d_ref, log_ref, bias_ref, dq_ref, dk_ref, dv_ref, dk_sum, dv_sum
):
    rows = query_ref.shape[0]
    first = half_mask(rows)
    zero = jnp.zeros((rows, PAIR), jnp.bfloat16)
    key = key_ref[...]
    value = value_ref[...]
    key_sides = (jnp.where(first, key, zero), jnp.where(first, zero, key))
    value_sides = (jnp.where(first, value, zero), jnp.where(first, zero, value))
    key_t = key.astype(jnp.float32).T.astype(jnp.bfloat16)
    scale = jnp.bfloat16(1.0 / math.sqrt(HD))
    for start, size in chunks_of(rows):
        query = query_ref[start : start + size, :] * scale
        d_rows = d_ref[start : start + size, :]
        bias = bias_ref[:, start : start + size]
        outs = []
        for side in range(2):
            scores = nt_dot(key_sides[side], query) + bias
            probs = jnp.exp(scores - log_ref[0, side : side + 1, start : start + size])
            d_probs = nt_dot(value_sides[side], d_rows)
            product = probs * d_probs
            delta = jnp.sum(product, axis=0, keepdims=True)
            d_scores = (product - probs * delta).astype(jnp.bfloat16)
            d_value = matmul(probs.astype(jnp.bfloat16), d_rows)
            d_key = matmul(d_scores, query)
            if start == 0:
                dv_sum[side] = d_value
                dk_sum[side] = d_key
            else:
                dv_sum[side] += d_value
                dk_sum[side] += d_key
            outs.append(matmul(key_t[side * HD : (side + 1) * HD, :], d_scores))
        d_query = jnp.concatenate(outs, axis=0) * (1.0 / math.sqrt(HD))
        dq_ref[start : start + size, :] = d_query.T.astype(jnp.bfloat16)
    dk_ref[...] = jnp.where(first, dk_sum[0], dk_sum[1]).astype(jnp.bfloat16)
    dv_ref[...] = jnp.where(first, dv_sum[0], dv_sum[1]).astype(jnp.bfloat16)


def attention_forward(joined, bias):
    rows, width = joined.shape[0], joined.shape[1] // 3
    pairs = width // PAIR
    flops = 4 * rows * rows * width
    return pl.pallas_call(
        forward_kernel,
        grid=(pairs,),
        in_specs=[
            pl.BlockSpec((rows, PAIR), lambda i: (0, i)),
            pl.BlockSpec((rows, PAIR), lambda i: (0, pairs + i)),
            pl.BlockSpec((rows, PAIR), lambda i: (0, 2 * pairs + i)),
            pl.BlockSpec((rows, rows), lambda i: (0, 0)),
        ],
        out_specs=[
            pl.BlockSpec((rows, PAIR), lambda i: (0, i)),
            pl.BlockSpec((1, 2, rows), lambda i: (i, 0, 0)),
        ],
        out_shape=[
            jax.ShapeDtypeStruct((rows, width), jnp.bfloat16),
            jax.ShapeDtypeStruct((pairs, 2, rows), jnp.float32),
        ],
        compiler_params=pltpu.CompilerParams(vmem_limit_bytes=40 * 2**20),
        cost_estimate=pl.CostEstimate(
            flops=4 * flops, bytes_accessed=8 * rows * width, transcendentals=rows * rows * 16
        ),
        name="attention_forward",
    )(joined, joined, joined, bias)


def attention_backward(joined, d_attended, log_total, bias):
    rows, width = d_attended.shape
    pairs = width // PAIR
    flops = 10 * rows * rows * width
    block = jax.ShapeDtypeStruct((rows, width), jnp.bfloat16)
    return pl.pallas_call(
        backward_kernel,
        grid=(pairs,),
        in_specs=[
            pl.BlockSpec((rows, PAIR), lambda i: (0, i)),
            pl.BlockSpec((rows, PAIR), lambda i: (0, pairs + i)),
            pl.BlockSpec((rows, PAIR), lambda i: (0, 2 * pairs + i)),
            pl.BlockSpec((rows, PAIR), lambda i: (0, i)),
            pl.BlockSpec((1, 2, rows), lambda i: (i, 0, 0)),
            pl.BlockSpec((rows, rows), lambda i: (0, 0)),
        ],
        out_specs=[pl.BlockSpec((rows, PAIR), lambda i: (0, i))] * 3,
        out_shape=[block] * 3,
        scratch_shapes=[pltpu.VMEM((2, rows, PAIR), jnp.float32)] * 2,
        compiler_params=pltpu.CompilerParams(vmem_limit_bytes=40 * 2**20),
        cost_estimate=pl.CostEstimate(
            flops=4 * flops, bytes_accessed=14 * rows * width, transcendentals=rows * rows * 16
        ),
        name="attention_backward",
    )(joined, joined, joined, d_attended, log_total, bias)


def standardize(value):
    center = value - jnp.mean(value, axis=-1, keepdims=True)
    variance = jnp.mean(center * center, axis=-1, keepdims=True)
    scale = lax.rsqrt(variance + EPSILON)
    return center * scale, scale


def norm_backward(d_normed, normal, scale, gain):
    scaled = d_normed * gain
    mean = jnp.mean(scaled, axis=-1, keepdims=True)
    along = jnp.mean(scaled * normal, axis=-1, keepdims=True)
    return (scaled - mean - normal * along) * scale


def gelu_slope(value):
    phi = 0.5 * (1.0 + lax.erf(value * math.sqrt(0.5)))
    return phi + value * jnp.exp(-0.5 * value * value) * (1.0 / math.sqrt(2.0 * math.pi))


def to_local(array, axis, far):
    shape = array.shape
    cut = shape[:axis] + (far, 2, 2, 2, shape[axis] // (8 * far)) + shape[axis + 1 :]
    spots = [axis + 2, axis + 1, axis + 3, axis]
    spots = list(range(axis)) + spots + list(range(axis + 4, len(cut)))
    return array.reshape(cut).transpose(spots).reshape(shape)


def hidden_to_local(array, axis, far):
    shape = array.shape
    cut = shape[:axis] + (far, 2, 2, 2, shape[axis] // (8 * far)) + shape[axis + 1 :]
    spots = [axis + 2, axis + 1, axis, axis + 3]
    spots = list(range(axis)) + spots + list(range(axis + 4, len(cut)))
    return array.reshape(cut).transpose(spots).reshape(shape)


def to_natural(array, axis, far):
    shape = array.shape
    cut = shape[:axis] + (2, 2, 2, far, shape[axis] // (8 * far)) + shape[axis + 1 :]
    spots = [axis + 3, axis + 1, axis, axis + 2]
    spots = list(range(axis)) + spots + list(range(axis + 4, len(cut)))
    return array.reshape(cut).transpose(spots).reshape(shape)


def hidden_to_natural(array, axis, far):
    shape = array.shape
    cut = shape[:axis] + (2, 2, far, 2, shape[axis] // (8 * far)) + shape[axis + 1 :]
    spots = [axis + 2, axis + 1, axis, axis + 3]
    spots = list(range(axis)) + spots + list(range(axis + 4, len(cut)))
    return array.reshape(cut).transpose(spots).reshape(shape)


def assemble_kernel(index_ref, *refs):
    pieces, (*wholes, stage, arrived, left) = refs[: index_ref.shape[0]], refs[index_ref.shape[0] :]
    incoming = [
        pltpu.make_async_copy(piece, stage.at[number], arrived.at[number])
        for number, piece in enumerate(pieces)
    ]
    for copy in incoming:
        copy.start()
    outgoing = []
    for number, piece in enumerate(pieces):
        incoming[number].wait()
        size = piece.shape[0]
        start = pl.multiple_of(index_ref[number] * size, 16)
        column = 0
        for part, whole in enumerate(wholes):
            width = whole.shape[1]
            copy = pltpu.make_async_copy(
                stage.at[number, :, pl.ds(column, width)],
                whole.at[pl.ds(start, size)],
                left.at[part, number],
            )
            copy.start()
            outgoing.append(copy)
            column += width
    for copy in outgoing:
        copy.wait()


def assemble(pieces, indices, extra=0):
    size, width = pieces[0].shape
    count = len(pieces)
    widths = (width - extra, extra) if extra else (width,)
    anywhere = pl.BlockSpec(memory_space=pl.ANY)
    wholes = pl.pallas_call(
        assemble_kernel,
        in_specs=[pl.BlockSpec(memory_space=pltpu.SMEM)] + [anywhere] * count,
        out_specs=[anywhere] * len(widths),
        out_shape=[jax.ShapeDtypeStruct((count * size, one), pieces[0].dtype) for one in widths],
        scratch_shapes=[
            pltpu.VMEM((count, size, width), pieces[0].dtype),
            pltpu.SemaphoreType.DMA((count,)),
            pltpu.SemaphoreType.DMA((len(widths), count)),
        ],
        compiler_params=pltpu.CompilerParams(vmem_limit_bytes=16 * 2**20),
        cost_estimate=pl.CostEstimate(
            flops=0, bytes_accessed=4 * count * size * width, transcendentals=0
        ),
        name="assemble",
    )(jnp.stack(indices).astype(jnp.int32), *pieces)
    return wholes if extra else wholes[0]


def trade(array, axis):
    return lax.ppermute(array, axis, [(0, 1), (1, 0)])


def after(array, other):
    return lax.optimization_barrier((array, other))[0]


def gather_far(shard, far):
    place = lax.axis_index("z")
    pieces, indices = [shard], [place]
    for step in range(1, far):
        pieces.append(lax.ppermute(shard, "z", [(i, (i + step) % far) for i in range(far)]))
        indices.append((place - step) % far)
    return assemble(pieces, indices)


def spread(blocks, axis):
    return blocks | {key | {axis}: trade(block, axis) for key, block in blocks.items()}


def order_blocks(blocks, axes, extra=0):
    indices = []
    for key in blocks:
        index = 0
        for axis in axes:
            place = lax.axis_index(axis)
            index = 2 * index + (1 - place if axis in key else place)
        indices.append(index)
    return assemble(list(blocks.values()), indices, extra)


def tie_blocks(blocks, other):
    return {key: after(block, other) for key, block in blocks.items()}


OWN = frozenset()


def send_half(matrix, axis, outer=1):
    rows, width = matrix.shape
    place = lax.axis_index(axis)
    blocks = matrix.reshape(outer, 2, rows // (2 * outer), width)
    kept = lax.dynamic_index_in_dim(blocks, place, 1, False).reshape(rows // 2, width)
    sent = lax.dynamic_index_in_dim(blocks, 1 - place, 1, False).reshape(rows // 2, width)
    return kept, trade(sent, axis)


def add_half(halves, follow=None):
    kept, got = halves
    if follow is not None:
        got = after(got, follow)
    return (kept.astype(jnp.float32) + got.astype(jnp.float32)).astype(kept.dtype)


def send_far(matrix, far):
    size = matrix.shape[0] // far
    place = lax.axis_index("z")
    arrays = [lax.dynamic_slice_in_dim(matrix, place * size, size)]
    for step in range(1, far):
        sent = lax.dynamic_slice_in_dim(matrix, ((place + step) % far) * size, size)
        arrays.append(lax.ppermute(sent, "z", [(i, (i + step) % far) for i in range(far)]))
    return arrays


def add_far(arrays, follow=None):
    own, *got = arrays
    if follow is not None:
        got = [after(array, follow) for array in got]
    return sum(array.astype(jnp.float32) for array in [own, *got])


def column_sums(array):
    return jnp.sum(array.astype(jnp.float32), axis=0)


def by_image(far):
    def on_device(
        inputs,
        cotangent,
        segment,
        w_qkv,
        b_query,
        b_value,
        w_out,
        b_out,
        norm1_gain,
        norm1_shift,
        norm2_gain,
        norm2_shift,
        w_up,
        b_up,
        w_down,
        b_down,
    ):
        place = lax.axis_index("ctx")
        swap = lambda array: trade(array, "ctx")
        slots, width = inputs.shape
        pads = 2 * slots - IMAGES * SEQ
        rows = round_up(SEQ + pads, 16)
        near_width = w_up.shape[0] // 8

        segment_far = swap(segment)
        inputs_far = swap(inputs)
        small = jnp.concatenate(
            [b_query, b_value, b_out, norm1_gain, norm1_shift, norm2_gain, norm2_shift, b_down, b_up]
        )
        shard_qkv = unfold(w_qkv)
        shard_rows = shard_qkv.shape[0]
        small = small.reshape(shard_rows, -1)
        small_width = small.shape[1]
        extra = round_up(small_width, 128)
        small = jnp.pad(small, ((0, 0), (0, extra - small_width)))
        far_qkv = gather_far(jnp.concatenate([shard_qkv, small], axis=1), far)
        shard_up = jnp.concatenate(
            [hidden_to_local(unfold(w_up), 1, far), to_local(unfold(w_out), 1, far)], axis=1
        )
        far_up = gather_far(after(shard_up, far_qkv), far)
        qkv_blocks = spread({OWN: after(far_qkv, inputs_far)}, "x")
        far_x = qkv_blocks[frozenset({"x"})]
        qkv_blocks = spread(qkv_blocks, "ctx")
        up_blocks = spread({OWN: after(far_up, far_x)}, "x")
        shard_down = after(to_local(unfold(w_down), 1, far), far_up)
        near_down = order_blocks(spread({OWN: shard_down}, "ctx"), ["ctx"])
        qkv_weight, small_local = order_blocks(
            spread(qkv_blocks, "core"), ["core", "x", "ctx"], extra
        )
        up_blocks = spread(tie_blocks(up_blocks, qkv_blocks[frozenset({"x", "ctx"})]), "ctx")
        far_down = gather_far(near_down, far)

        small_core = small_local[:, :small_width].astype(jnp.float32).reshape(8 * far, -1)
        small_all = to_natural(small_core, 0, far)
        piece = lambda table, index: table[:, index * near_width : (index + 1) * near_width].reshape(-1)
        query_bias = piece(small_all, 0)
        value_bias = piece(small_all, 1)
        out_bias, first_gain, first_shift, second_gain, second_shift, down_bias = (
            piece(small_core, index) for index in range(2, 8)
        )
        up_bias = hidden_to_local(small_all[:, 8 * near_width :].reshape(-1), 0, far)

        slot = jnp.arange(slots)
        earlier = slot[:, None] < slot[None, :]

        def ranks(own, far, far_first):
            inside = jnp.sum((own[:, None] == own[None, :]) & earlier, axis=0)
            outside = jnp.sum(far[:, None] == own[None, :], axis=0)
            return inside + jnp.where(far_first, outside, 0)

        rank_near = ranks(segment, segment_far, place == 1)
        rank_far = ranks(segment_far, segment, place == 0)

        def positions(ids, rank, image):
            return jnp.where(ids == image, rank, jnp.where(ids < 0, SEQ + rank, -1))

        row = jnp.arange(rows)
        pick_near = (positions(segment, rank_near, place)[None, :] == row[:, None])
        pick_far = (positions(segment_far, rank_far, place)[None, :] == row[:, None])
        pick_near, pick_far = pick_near.astype(jnp.bfloat16), pick_far.astype(jnp.bfloat16)
        give_near = (positions(segment, rank_near, place)[:, None] == row[None, :])
        other_image = jnp.where(segment == 1 - place, rank_near, -1)
        give_far = other_image[:, None] == row[None, :]
        give_near, give_far = give_near.astype(jnp.bfloat16), give_far.astype(jnp.bfloat16)
        column = jnp.arange(width)
        order = to_local(column, 0, far)
        to_core = (column[:, None] == order[None, :]).astype(jnp.bfloat16)

        def take(near, far):
            picked = matmul(pick_near, near) + matmul(pick_far, far)
            return matmul(picked.astype(jnp.bfloat16), to_core)

        def to_give(array):
            natural = nt_dot(array.astype(jnp.bfloat16), to_core).astype(jnp.bfloat16)
            return natural, swap(natural)

        def give(both, follow):
            near, far_rows = both
            return matmul(give_near, near) + matmul(give_far, after(far_rows, follow))

        kind = (row >= SEQ).astype(jnp.int32) + (row >= SEQ + pads).astype(jnp.int32)
        bias = jnp.where(kind[:, None] == kind[None, :], 0.0, -1e30).astype(jnp.float32)

        values_in = take(inputs, inputs_far)
        normal1, scale1 = standardize(values_in)
        normed1 = (normal1 * first_gain + first_shift).astype(jnp.bfloat16)
        joined_bias = jnp.concatenate([query_bias, jnp.zeros_like(query_bias), value_bias])
        joined = (matmul(normed1, qkv_weight) + joined_bias).astype(jnp.bfloat16)
        up_near = order_blocks(up_blocks, ["x", "ctx"])
        attended, log_total = attention_forward(after(joined, near_down), bias)
        down_blocks = spread({OWN: after(far_down, attended)}, "x")
        up_weight, out_rows = order_blocks(
            spread({OWN: after(up_near, attended)}, "core"), ["core"], width
        )
        out_weight = to_natural(out_rows, 0, far)
        middle = values_in + matmul(attended, out_weight) + out_bias
        normal2, scale2 = standardize(middle)
        normed2 = (normal2 * second_gain + second_shift).astype(jnp.bfloat16)
        hidden = matmul(normed2, up_weight) + up_bias
        active = gelu_exact(hidden).astype(jnp.bfloat16)
        slope = gelu_slope(hidden).astype(jnp.bfloat16)
        down_blocks = tie_blocks(down_blocks, active)
        down_weight = order_blocks(spread(down_blocks, "core"), ["core", "x"])

        live = (row < SEQ).astype(jnp.float32)[:, None]
        cotangent_far = swap(after(cotangent, joined))
        d_out = take(cotangent, cotangent_far) * live
        d_out_low = d_out.astype(jnp.bfloat16)
        grad_down = matmul(active.T, d_out_low).astype(jnp.bfloat16)
        down_core = send_half(grad_down, "core")
        last = middle + matmul(after(active, down_core[0]), down_weight) + down_bias
        last_given = to_give(last)
        down_x = send_half(add_half(down_core, last_given[0]), "x")
        d_hidden = (
            matmul(after(d_out_low, down_x[0]), down_weight.T) * slope.astype(jnp.float32)
        ).astype(jnp.bfloat16)
        grad_up = matmul(normed2.T, d_hidden).astype(jnp.bfloat16)
        up_core = send_half(grad_up, "core")
        d_normed2 = matmul(after(d_hidden, up_core[0]), up_weight.T)
        d_middle = d_out + norm_backward(d_normed2, normal2, scale2, second_gain)
        d_branch = d_middle.astype(jnp.bfloat16)
        outputs = give(last_given, d_branch).astype(jnp.bfloat16)
        up_y = send_half(add_half(up_core, d_branch), "ctx", 2)
        grad_out = to_local(matmul(attended.T, after(d_branch, up_y[0])).astype(jnp.bfloat16), 0, far)
        out_core = send_half(grad_out, "core")
        d_attended = matmul(d_branch, out_weight.T).astype(jnp.bfloat16)
        down_far = send_far(add_half(down_x, d_attended), far)
        out_x = send_half(add_half(out_core, d_attended), "x")
        d_attended = after(after(d_attended, out_x[0]), down_far[0])
        d_query, d_key, d_value = attention_backward(joined, d_attended, log_total, bias)
        d_joined = jnp.concatenate([d_query, d_key, d_value], axis=1)
        out_y = send_half(add_half(out_x, d_joined), "ctx")
        up_x = send_half(add_half(up_y, d_joined), "x")
        grad_qkv = matmul(normed1.T, after(after(d_joined, out_y[0]), up_x[0])).astype(jnp.bfloat16)
        qkv_core = send_half(grad_qkv, "core")
        d_normed1 = matmul(after(d_joined, qkv_core[0]), qkv_weight.T)
        d_last = d_middle + norm_backward(d_normed1, normal1, scale1, first_gain)
        qkv_x = send_half(add_half(qkv_core, d_last), "x")
        out_far = send_far(add_half(out_y, d_last), far)
        down_y = send_half(add_far(down_far, d_last).astype(jnp.bfloat16), "ctx")
        d_last_given = to_give(after(after(d_last, qkv_x[0]), down_y[0]))
        up_far = send_far(add_half(up_x, d_last_given[0]), far)
        qkv_y = send_half(add_half(qkv_x, up_far[0]), "ctx")
        sum_down = add_half(down_y, qkv_y[0]).astype(jnp.float32)
        sum_up, sum_out = add_far(up_far, qkv_y[0]), add_far(out_far, qkv_y[0])
        qkv_far = send_far(add_half(qkv_y), far)
        input_grad = give(d_last_given, qkv_far[0])
        sum_qkv = add_far(qkv_far)

        part = lambda vector: vector.reshape(8 * far, -1)
        core_sums = jnp.concatenate(
            [
                part(vector)
                for vector in (
                    column_sums(d_branch),
                    column_sums(d_normed1 * normal1),
                    column_sums(d_normed1),
                    column_sums(d_normed2 * normal2),
                    column_sums(d_normed2),
                    column_sums(d_out_low),
                )
            ],
            axis=1,
        )
        chip_sums = jnp.concatenate([part(column_sums(d_query)), part(column_sums(d_value))], axis=1)
        up_sums = part(hidden_to_natural(column_sums(d_hidden), 0, far))
        small_sums = jnp.concatenate(
            [to_local(chip_sums, 0, far), core_sums, to_local(up_sums, 0, far)], axis=1
        )
        for axis in ("core", "x", "ctx"):
            small_sums = add_half(send_half(small_sums, axis))
        small_sums = add_far(send_far(small_sums, far))[0]
        own = lambda index: small_sums[index * near_width : (index + 1) * near_width]
        back = lambda matrix: refold(to_natural(matrix, 1, far))
        return (
            outputs,
            input_grad,
            refold(sum_qkv),
            own(0),
            own(1),
            back(sum_out),
            own(2),
            own(3),
            own(4),
            own(5),
            own(6),
            refold(hidden_to_natural(sum_up, 1, far)),
            small_sums[8 * near_width :],
            back(sum_down),
            own(7),
        )

    return on_device


def solution(mesh):
    if mesh.shape["ctx"] == IMAGES and mesh.shape["dp"] % 4 == 0:
        far, axes = mesh.shape["dp"] // 4, ("z", "x", "core", "ctx")
        mesh = jax.sharding.Mesh(mesh.devices.reshape(far, 2, 2, IMAGES), axes)
        body = by_image(far)
    else:
        body, axes = on_device, ("dp", "ctx")
    matrix, vector = P(axes, None), P(axes)
    return jax.shard_map(
        body,
        mesh=mesh,
        in_specs=(matrix, matrix, vector, matrix, vector, vector, matrix)
        + (vector,) * 5
        + (matrix, vector, matrix, vector),
        out_specs=(matrix, matrix, matrix, vector, vector, matrix)
        + (vector,) * 5
        + (matrix, vector, matrix, vector),
        check_vma=False,
    )
```

```python
import functools
import math

import jax
import jax.numpy as jnp
from jax import lax
from jax.experimental import pallas as pl
from jax.experimental.pallas import tpu as pltpu
from jax.sharding import PartitionSpec as P

HD = 64


EPSILON = 1e-06


def layer_norm(value, gain, shift):
    center = value - jnp.mean(value, axis=-1, keepdims=True)
    variance = jnp.mean(center * center, axis=-1, keepdims=True)
    return center * lax.rsqrt(variance + EPSILON) * gain + shift


def gelu_exact(value):
    return jax.nn.gelu(value, approximate=False)


def matmul(left, right):
    return jnp.dot(left, right, preferred_element_type=jnp.float32)


def unfold(stored):
    return stored.reshape(stored.shape[0] // 8, stored.shape[1] * 8)


def refold(matrix):
    return matrix.reshape(matrix.shape[0] * 8, matrix.shape[1] // 8)


def on_device(
    inputs,
    cotangent,
    segment,
    w_qkv,
    b_query,
    b_value,
    w_out,
    b_out,
    norm1_gain,
    norm1_shift,
    norm2_gain,
    norm2_shift,
    w_up,
    b_up,
    w_down,
    b_down,
):
    gathered = (
        lax.all_gather(w_qkv, ("dp", "ctx"), axis=0, tiled=True),
        lax.all_gather(b_query, ("dp", "ctx"), axis=0, tiled=True),
        lax.all_gather(b_value, ("dp", "ctx"), axis=0, tiled=True),
        lax.all_gather(w_out, ("dp", "ctx"), axis=0, tiled=True),
        lax.all_gather(b_out, ("dp", "ctx"), axis=0, tiled=True),
        lax.all_gather(norm1_gain, ("dp", "ctx"), axis=0, tiled=True),
        lax.all_gather(norm1_shift, ("dp", "ctx"), axis=0, tiled=True),
        lax.all_gather(norm2_gain, ("dp", "ctx"), axis=0, tiled=True),
        lax.all_gather(norm2_shift, ("dp", "ctx"), axis=0, tiled=True),
        lax.all_gather(w_up, ("dp", "ctx"), axis=0, tiled=True),
        lax.all_gather(b_up, ("dp", "ctx"), axis=0, tiled=True),
        lax.all_gather(w_down, ("dp", "ctx"), axis=0, tiled=True),
        lax.all_gather(b_down, ("dp", "ctx"), axis=0, tiled=True),
    )
    (
        qkv_stored,
        query_bias,
        value_bias,
        out_stored,
        out_bias,
        gain_one,
        shift_one,
        gain_two,
        shift_two,
        up_stored,
        up_bias,
        down_stored,
        down_bias,
    ) = gathered
    qkv_weight = unfold(qkv_stored)
    out_weight = unfold(out_stored)
    up_weight = unfold(up_stored)
    down_weight = unfold(down_stored)
    first_gain = gain_one.astype(jnp.float32)
    first_shift = shift_one.astype(jnp.float32)
    second_gain = gain_two.astype(jnp.float32)
    second_shift = shift_two.astype(jnp.float32)
    row_count = inputs.shape[0]
    model_width = out_weight.shape[0]
    head_count = model_width // HD
    score_scale = 1.0 / math.sqrt(HD)
    values_in = inputs.astype(jnp.float32)
    normed1 = layer_norm(values_in, first_gain, first_shift).astype(jnp.bfloat16)
    joined = matmul(normed1, qkv_weight)
    queries = (joined[:, :model_width] + query_bias.astype(jnp.float32)).astype(jnp.bfloat16)
    key_rows = joined[:, model_width : 2 * model_width].astype(jnp.bfloat16)
    value_rows = (joined[:, 2 * model_width :] + value_bias.astype(jnp.float32)).astype(
        jnp.bfloat16
    )
    key_all, value_all, seg_all = (
        lax.all_gather(key_rows, "ctx", axis=0, tiled=True),
        lax.all_gather(value_rows, "ctx", axis=0, tiled=True),
        lax.all_gather(segment.astype(jnp.bfloat16), "ctx", axis=0, tiled=True),
    )
    key_count = key_all.shape[0]
    query_heads = queries.reshape(row_count, head_count, HD)
    key_heads = key_all.reshape(key_count, head_count, HD)
    value_heads = value_all.reshape(key_count, head_count, HD)
    own_seg = segment.astype(jnp.float32)
    group_seg = seg_all.astype(jnp.float32)
    same_seg = own_seg[:, None] == group_seg[None, :]

    def make_scores():
        raw = (
            jnp.einsum("qhd,khd->hqk", query_heads, key_heads, preferred_element_type=jnp.float32)
            * score_scale
        )
        return jnp.where(same_seg[None], raw, -1e30)

    scores = make_scores()
    row_max = jnp.max(scores, axis=-1, keepdims=True)
    expo = jnp.exp(scores - row_max)
    row_total = jnp.sum(expo, axis=-1, keepdims=True)
    probs_low = (expo / row_total).astype(jnp.bfloat16)
    log_total = row_max + jnp.log(row_total)
    mixed = jnp.einsum("hqk,khd->qhd", probs_low, value_heads, preferred_element_type=jnp.float32)
    attended = mixed.reshape(row_count, model_width).astype(jnp.bfloat16)
    middle = values_in + matmul(attended, out_weight) + out_bias.astype(jnp.float32)
    normed2 = layer_norm(middle, second_gain, second_shift).astype(jnp.bfloat16)
    hidden = matmul(normed2, up_weight) + up_bias.astype(jnp.float32)
    active = gelu_exact(hidden).astype(jnp.bfloat16)
    outputs = (middle + matmul(active, down_weight) + down_bias.astype(jnp.float32)).astype(
        jnp.bfloat16
    )
    back_qkv, back_out, back_up, back_down = (qkv_weight, out_weight, up_weight, down_weight)
    valid = (segment >= 0).astype(jnp.float32)[:, None]
    d_out = cotangent.astype(jnp.float32) * valid
    d_out_low = d_out.astype(jnp.bfloat16)
    grad_down = refold(matmul(active.T, d_out_low))
    grad_down_bias = jnp.sum(d_out_low.astype(jnp.float32), axis=0)
    d_active = matmul(d_out_low, back_down.T)
    gelu_value, gelu_pull = jax.vjp(gelu_exact, hidden)
    d_hidden = gelu_pull(d_active)[0].astype(jnp.bfloat16)
    grad_up = refold(matmul(normed2.T, d_hidden))
    grad_up_bias = jnp.sum(d_hidden.astype(jnp.float32), axis=0)
    d_normed2 = matmul(d_hidden, back_up.T)
    norm_value, norm_pull = jax.vjp(layer_norm, middle, second_gain, second_shift)
    d_middle_norm, grad_gain_two, grad_shift_two = norm_pull(d_normed2)
    d_middle = d_out + d_middle_norm
    d_branch = d_middle.astype(jnp.bfloat16)
    grad_out = refold(matmul(attended.T, d_branch))
    grad_out_bias = jnp.sum(d_branch.astype(jnp.float32), axis=0)
    d_attended_flat = matmul(d_branch, back_out.T).astype(jnp.bfloat16)
    d_attended = d_attended_flat.reshape(row_count, head_count, HD)
    scores = make_scores()
    probs = jnp.exp(scores - log_total)
    d_probs = jnp.einsum(
        "qhd,khd->hqk", d_attended, value_heads, preferred_element_type=jnp.float32
    )
    delta_rows = jnp.sum(probs * d_probs, axis=-1, keepdims=True)
    d_scores = (probs * (d_probs - delta_rows)).astype(jnp.bfloat16)
    d_query = (
        jnp.einsum("hqk,khd->qhd", d_scores, key_heads, preferred_element_type=jnp.float32)
        * score_scale
    ).reshape(row_count, model_width)
    probs_again = probs.astype(jnp.bfloat16)
    d_key_all = (
        jnp.einsum("hqk,qhd->khd", d_scores, query_heads, preferred_element_type=jnp.float32)
        * score_scale
    ).reshape(key_count, model_width)
    d_value_all = jnp.einsum(
        "hqk,qhd->khd", probs_again, d_attended, preferred_element_type=jnp.float32
    ).reshape(key_count, model_width)
    d_key, d_value = (
        lax.psum_scatter(
            d_key_all.astype(jnp.bfloat16), "ctx", scatter_dimension=0, tiled=True
        ).astype(jnp.float32),
        lax.psum_scatter(
            d_value_all.astype(jnp.bfloat16), "ctx", scatter_dimension=0, tiled=True
        ).astype(jnp.float32),
    )
    d_query_low = d_query.astype(jnp.bfloat16)
    d_value_low = d_value.astype(jnp.bfloat16)
    d_joined = jnp.concatenate([d_query_low, d_key.astype(jnp.bfloat16), d_value_low], axis=1)
    grad_qkv = refold(matmul(normed1.T, d_joined))
    grad_query_bias = jnp.sum(d_query_low.astype(jnp.float32), axis=0)
    grad_value_bias = jnp.sum(d_value_low.astype(jnp.float32), axis=0)
    d_normed1 = matmul(d_joined, back_qkv.T)
    first_value, first_pull = jax.vjp(layer_norm, values_in, first_gain, first_shift)
    d_input_norm, grad_gain_one, grad_shift_one = first_pull(d_normed1)
    input_grad = d_middle + d_input_norm
    partial_sums = (
        lax.psum_scatter(
            grad_qkv.astype(jnp.bfloat16), "dp", scatter_dimension=0, tiled=True
        ).astype(jnp.float32),
        lax.psum_scatter(
            grad_query_bias.astype(jnp.bfloat16), "dp", scatter_dimension=0, tiled=True
        ).astype(jnp.float32),
        lax.psum_scatter(
            grad_value_bias.astype(jnp.bfloat16), "dp", scatter_dimension=0, tiled=True
        ).astype(jnp.float32),
        lax.psum_scatter(
            grad_out.astype(jnp.bfloat16), "dp", scatter_dimension=0, tiled=True
        ).astype(jnp.float32),
        lax.psum_scatter(
            grad_out_bias.astype(jnp.bfloat16), "dp", scatter_dimension=0, tiled=True
        ).astype(jnp.float32),
        lax.psum_scatter(
            grad_gain_one.astype(jnp.bfloat16), "dp", scatter_dimension=0, tiled=True
        ).astype(jnp.float32),
        lax.psum_scatter(
            grad_shift_one.astype(jnp.bfloat16), "dp", scatter_dimension=0, tiled=True
        ).astype(jnp.float32),
        lax.psum_scatter(
            grad_gain_two.astype(jnp.bfloat16), "dp", scatter_dimension=0, tiled=True
        ).astype(jnp.float32),
        lax.psum_scatter(
            grad_shift_two.astype(jnp.bfloat16), "dp", scatter_dimension=0, tiled=True
        ).astype(jnp.float32),
        lax.psum_scatter(
            grad_up.astype(jnp.bfloat16), "dp", scatter_dimension=0, tiled=True
        ).astype(jnp.float32),
        lax.psum_scatter(
            grad_up_bias.astype(jnp.bfloat16), "dp", scatter_dimension=0, tiled=True
        ).astype(jnp.float32),
        lax.psum_scatter(
            grad_down.astype(jnp.bfloat16), "dp", scatter_dimension=0, tiled=True
        ).astype(jnp.float32),
        lax.psum_scatter(
            grad_down_bias.astype(jnp.bfloat16), "dp", scatter_dimension=0, tiled=True
        ).astype(jnp.float32),
    )
    all_sums = (
        lax.psum_scatter(
            partial_sums[0].astype(jnp.bfloat16), "ctx", scatter_dimension=0, tiled=True
        ).astype(jnp.float32),
        lax.psum_scatter(
            partial_sums[1].astype(jnp.bfloat16), "ctx", scatter_dimension=0, tiled=True
        ).astype(jnp.float32),
        lax.psum_scatter(
            partial_sums[2].astype(jnp.bfloat16), "ctx", scatter_dimension=0, tiled=True
        ).astype(jnp.float32),
        lax.psum_scatter(
            partial_sums[3].astype(jnp.bfloat16), "ctx", scatter_dimension=0, tiled=True
        ).astype(jnp.float32),
        lax.psum_scatter(
            partial_sums[4].astype(jnp.bfloat16), "ctx", scatter_dimension=0, tiled=True
        ).astype(jnp.float32),
        lax.psum_scatter(
            partial_sums[5].astype(jnp.bfloat16), "ctx", scatter_dimension=0, tiled=True
        ).astype(jnp.float32),
        lax.psum_scatter(
            partial_sums[6].astype(jnp.bfloat16), "ctx", scatter_dimension=0, tiled=True
        ).astype(jnp.float32),
        lax.psum_scatter(
            partial_sums[7].astype(jnp.bfloat16), "ctx", scatter_dimension=0, tiled=True
        ).astype(jnp.float32),
        lax.psum_scatter(
            partial_sums[8].astype(jnp.bfloat16), "ctx", scatter_dimension=0, tiled=True
        ).astype(jnp.float32),
        lax.psum_scatter(
            partial_sums[9].astype(jnp.bfloat16), "ctx", scatter_dimension=0, tiled=True
        ).astype(jnp.float32),
        lax.psum_scatter(
            partial_sums[10].astype(jnp.bfloat16), "ctx", scatter_dimension=0, tiled=True
        ).astype(jnp.float32),
        lax.psum_scatter(
            partial_sums[11].astype(jnp.bfloat16), "ctx", scatter_dimension=0, tiled=True
        ).astype(jnp.float32),
        lax.psum_scatter(
            partial_sums[12].astype(jnp.bfloat16), "ctx", scatter_dimension=0, tiled=True
        ).astype(jnp.float32),
    )
    (
        sum_qkv,
        sum_query_bias,
        sum_value_bias,
        sum_out,
        sum_out_bias,
        sum_gain_one,
        sum_shift_one,
        sum_gain_two,
        sum_shift_two,
        sum_up,
        sum_up_bias,
        sum_down,
        sum_down_bias,
    ) = all_sums
    return (
        outputs,
        input_grad,
        sum_qkv,
        sum_query_bias,
        sum_value_bias,
        sum_out,
        sum_out_bias,
        sum_gain_one,
        sum_shift_one,
        sum_gain_two,
        sum_shift_two,
        sum_up,
        sum_up_bias,
        sum_down,
        sum_down_bias,
    )


SEQ = 577
IMAGES = 2
PAIR = 2 * HD
CHUNK = 256
BLOCK = 512
HINT = pl.CostEstimate(flops=1, bytes_accessed=1, transcendentals=0)
ERFC = (
    0.09873409569263458,
    0.09871950000524521,
    0.09271052479743958,
    0.08134904503822327,
    0.056456614285707474,
    0.07422702759504318,
    -0.050631966441869736,
    0.11820460855960846,
    -0.09110676497220993,
    0.021337319165468216,
)
ERFC_STEP = 0.35


def round_up(count, unit):
    return -(-count // unit) * unit


def limit(mebibytes):
    return pltpu.CompilerParams(vmem_limit_bytes=mebibytes * 2**20)


def chunks_of(count):
    return [(start, min(CHUNK, count - start)) for start in range(0, count, CHUNK)]


def nt_dot(left, right):
    return lax.dot_general(
        left, right, (((1,), (1,)), ((), ())), preferred_element_type=jnp.float32
    )


def tn_dot(left, right):
    return lax.dot_general(
        left, right, (((0,), (0,)), ((), ())), preferred_element_type=jnp.float32
    )


def half_mask(rows):
    return lax.broadcasted_iota(jnp.int32, (rows, PAIR), 1) < HD


def forward_kernel(query_ref, key_ref, value_ref, bias_ref, attended_ref, log_ref):
    rows = query_ref.shape[1]
    first = half_mask(rows)
    zero = jnp.zeros((rows, PAIR), jnp.bfloat16)
    key = key_ref[0]
    key_sides = (jnp.where(first, key, zero), jnp.where(first, zero, key))
    value_t = value_ref[0].astype(jnp.float32).T.astype(jnp.bfloat16)
    scale = jnp.bfloat16(1.0 / math.sqrt(HD))
    for start, size in chunks_of(rows):
        query = query_ref[0, start : start + size, :] * scale
        bias = bias_ref[:, start : start + size]
        outs = []
        for side in range(2):
            scores = nt_dot(key_sides[side], query) + bias
            top = jnp.max(scores, axis=0, keepdims=True)
            expo = jnp.exp(scores - top)
            total = jnp.sum(expo, axis=0, keepdims=True)
            probs_low = (expo * (1.0 / total)).astype(jnp.bfloat16)
            outs.append(matmul(value_t[side * HD : (side + 1) * HD, :], probs_low))
            log_ref[0, side : side + 1, start : start + size] = top + jnp.log(total)
        mixed = jnp.concatenate(outs, axis=0)
        attended_ref[start : start + size, :] = mixed.T.astype(jnp.bfloat16)


def backward_kernel(
    query_ref, key_ref, value_ref, d_ref, log_ref, bias_ref, joined_ref, dk_sum, dv_sum
):
    rows = query_ref.shape[1]
    first = half_mask(rows)
    zero = jnp.zeros((rows, PAIR), jnp.bfloat16)
    key = key_ref[0]
    value = value_ref[0]
    key_sides = (jnp.where(first, key, zero), jnp.where(first, zero, key))
    value_sides = (jnp.where(first, value, zero), jnp.where(first, zero, value))
    key_t = key.astype(jnp.float32).T.astype(jnp.bfloat16)
    scale = jnp.bfloat16(1.0 / math.sqrt(HD))
    for start, size in chunks_of(rows):
        query = query_ref[0, start : start + size, :] * scale
        d_rows = d_ref[start : start + size, :]
        bias = bias_ref[:, start : start + size]
        outs = []
        for side in range(2):
            scores = nt_dot(key_sides[side], query) + bias
            probs = jnp.exp(scores - log_ref[0, side : side + 1, start : start + size])
            d_probs = nt_dot(value_sides[side], d_rows)
            product = probs * d_probs
            delta = jnp.sum(product, axis=0, keepdims=True)
            d_scores = (product - probs * delta).astype(jnp.bfloat16)
            d_value = matmul(probs.astype(jnp.bfloat16), d_rows)
            d_key = matmul(d_scores, query)
            if start == 0:
                dv_sum[side] = d_value
                dk_sum[side] = d_key
            else:
                dv_sum[side] += d_value
                dk_sum[side] += d_key
            outs.append(matmul(key_t[side * HD : (side + 1) * HD, :], d_scores))
        d_query = jnp.concatenate(outs, axis=0) * (1.0 / math.sqrt(HD))
        joined_ref[0, start : start + size, :] = d_query.T.astype(jnp.bfloat16)
    joined_ref[1] = jnp.where(first, dk_sum[0], dk_sum[1]).astype(jnp.bfloat16)
    joined_ref[2] = jnp.where(first, dv_sum[0], dv_sum[1]).astype(jnp.bfloat16)


def pair_spec(rows, part):
    return pl.BlockSpec((1, rows, PAIR), lambda i: (part, 0, i))


def attention_forward(joined, bias):
    rows, width = joined.shape[1:]
    pairs = width // PAIR
    return pl.pallas_call(
        forward_kernel,
        grid=(pairs,),
        in_specs=[pair_spec(rows, part) for part in range(3)]
        + [pl.BlockSpec((rows, rows), lambda i: (0, 0))],
        out_specs=[
            pl.BlockSpec((rows, PAIR), lambda i: (0, i)),
            pl.BlockSpec((1, 2, rows), lambda i: (i, 0, 0)),
        ],
        out_shape=[
            jax.ShapeDtypeStruct((rows, width), jnp.bfloat16),
            jax.ShapeDtypeStruct((pairs, 2, rows), jnp.float32),
        ],
        compiler_params=limit(32),
        cost_estimate=HINT,
        name="attention_forward",
    )(joined, joined, joined, bias)


def attention_backward(joined, d_attended, first_pair, log_total, bias):
    rows, width = joined.shape[1:]
    return pl.pallas_call(
        backward_kernel,
        grid=(width // PAIR,),
        in_specs=[pair_spec(rows, part) for part in range(3)]
        + [
            pl.BlockSpec((rows, PAIR), lambda i: (0, first_pair + i)),
            pl.BlockSpec((1, 2, rows), lambda i: (i, 0, 0)),
            pl.BlockSpec((rows, rows), lambda i: (0, 0)),
        ],
        out_specs=pl.BlockSpec((3, rows, PAIR), lambda i: (0, 0, i)),
        out_shape=jax.ShapeDtypeStruct((3, rows, width), jnp.bfloat16),
        scratch_shapes=[pltpu.VMEM((2, rows, PAIR), jnp.float32)] * 2,
        compiler_params=limit(32),
        cost_estimate=HINT,
        name="attention_backward",
    )(joined, joined, joined, d_attended, log_total, bias)


def whole_spec(shape):
    return pl.BlockSpec(shape, lambda *_: (0,) * len(shape))


def project_kernel(x_ref, weight_ref, bias_ref, out_ref):
    out_ref[0] = (matmul(x_ref[...], weight_ref[...]) + bias_ref[...]).astype(out_ref.dtype)


def project(x, weight, bias):
    rows, depth = x.shape
    width = weight.shape[1] // 3
    return pl.pallas_call(
        project_kernel,
        grid=(3,),
        in_specs=[
            whole_spec(x.shape),
            pl.BlockSpec((depth, width), lambda i: (0, i)),
            pl.BlockSpec((1, width), lambda i: (0, i)),
        ],
        out_specs=pl.BlockSpec((1, rows, width), lambda i: (i, 0, 0)),
        out_shape=jax.ShapeDtypeStruct((3, rows, width), jnp.bfloat16),
        compiler_params=limit(24),
        cost_estimate=HINT,
        name="project",
    )(x, weight, bias[None, :])


def hidden_kernel(x_ref, weight_ref, bias_ref, active_ref, slope_ref):
    hidden = matmul(x_ref[...], weight_ref[...]) + bias_ref[...]
    share = 1.0 / (1.0 + (ERFC_STEP * math.sqrt(0.5)) * jnp.abs(hidden))
    density = jnp.exp(-0.5 * hidden * hidden)
    tail = jnp.full_like(share, ERFC[-1])
    for factor in ERFC[-2::-1]:
        tail = tail * share + factor
    tail = tail * share * density
    phi = jnp.where(hidden < 0.0, tail, 1.0 - tail)
    active_ref[...] = (hidden * phi).astype(jnp.bfloat16)
    slope = phi + hidden * density * (1.0 / math.sqrt(2.0 * math.pi))
    slope_ref[...] = slope.astype(jnp.bfloat16)


def hidden_layer(x, weight, bias):
    rows, depth = x.shape
    width = weight.shape[1]
    block = pl.BlockSpec((rows, BLOCK), lambda i: (0, i))
    return pl.pallas_call(
        hidden_kernel,
        grid=(width // BLOCK,),
        in_specs=[
            whole_spec(x.shape),
            pl.BlockSpec((depth, BLOCK), lambda i: (0, i)),
            pl.BlockSpec((1, BLOCK), lambda i: (0, i)),
        ],
        out_specs=[block, block],
        out_shape=[jax.ShapeDtypeStruct((rows, width), jnp.bfloat16)] * 2,
        compiler_params=limit(32),
        cost_estimate=HINT,
        name="hidden_layer",
    )(x, weight, bias[None, :])


def last_kernel(active_ref, weight_ref, middle_ref, bias_ref, out_ref, total):
    step = pl.program_id(0)

    @pl.when(step == 0)
    def _():
        total[...] = middle_ref[...] + bias_ref[...]

    total[...] += matmul(active_ref[...], weight_ref[...])

    @pl.when(step == pl.num_programs(0) - 1)
    def _():
        out_ref[...] = total[...].astype(out_ref.dtype)


def last_layer(active, weight, middle, bias):
    rows, depth = active.shape
    width = weight.shape[1]
    return pl.pallas_call(
        last_kernel,
        grid=(depth // BLOCK,),
        in_specs=[
            pl.BlockSpec((rows, BLOCK), lambda i: (0, i)),
            pl.BlockSpec((BLOCK, width), lambda i: (i, 0)),
            whole_spec((rows, width)),
            whole_spec((1, width)),
        ],
        out_specs=whole_spec((rows, width)),
        out_shape=jax.ShapeDtypeStruct((rows, width), jnp.bfloat16),
        scratch_shapes=[pltpu.VMEM((rows, width), jnp.float32)],
        compiler_params=limit(24),
        cost_estimate=HINT,
        name="last_layer",
    )(active, weight, middle, bias[None, :])


def d_hidden_kernel(d_ref, weight_ref, slope_ref, out_ref, sum_ref):
    d_active = nt_dot(d_ref[...], weight_ref[...])
    d_hidden = (d_active * slope_ref[...].astype(jnp.float32)).astype(jnp.bfloat16)
    out_ref[...] = d_hidden
    sum_ref[...] = jnp.sum(d_hidden.astype(jnp.float32), axis=0, keepdims=True)


def d_hidden_layer(d_out, weight, slope):
    rows, depth = d_out.shape
    width = weight.shape[0]
    block = pl.BlockSpec((rows, BLOCK), lambda i: (0, i))
    return pl.pallas_call(
        d_hidden_kernel,
        grid=(width // BLOCK,),
        in_specs=[
            whole_spec(d_out.shape),
            pl.BlockSpec((BLOCK, depth), lambda i: (i, 0)),
            block,
        ],
        out_specs=[block, pl.BlockSpec((1, BLOCK), lambda i: (0, i))],
        out_shape=[
            jax.ShapeDtypeStruct((rows, width), jnp.bfloat16),
            jax.ShapeDtypeStruct((1, width), jnp.float32),
        ],
        compiler_params=limit(24),
        cost_estimate=HINT,
        name="d_hidden_layer",
    )(d_out, weight, slope)


def d_normed_kernel(d_ref, weight_ref, *refs):
    out_ref = refs[-1]
    d_rows = d_ref[0] if len(d_ref.shape) == 3 else d_ref[...]
    product = nt_dot(d_rows, weight_ref[...])
    step = pl.program_id(0)

    @pl.when(step == 0)
    def _():
        out_ref[...] = product + refs[0][...] if len(refs) == 2 else product

    @pl.when(step > 0)
    def _():
        out_ref[...] += product


def d_normed(d_rows, weight, base=None):
    rows, depth = d_rows.shape[-2], weight.shape[0]
    if d_rows.ndim == 3:
        d_spec = pl.BlockSpec((1, rows, BLOCK), lambda i: (i, 0, 0))
    else:
        d_spec = pl.BlockSpec((rows, BLOCK), lambda i: (0, i))
    extra = [] if base is None else [base]
    return pl.pallas_call(
        d_normed_kernel,
        grid=(weight.shape[1] // BLOCK,),
        in_specs=[d_spec, pl.BlockSpec((depth, BLOCK), lambda i: (0, i))]
        + [whole_spec((rows, depth)) for _ in extra],
        out_specs=whole_spec((rows, depth)),
        out_shape=jax.ShapeDtypeStruct((rows, depth), jnp.float32),
        compiler_params=limit(24),
        cost_estimate=HINT,
        name="d_normed",
    )(d_rows, weight, *extra)


def gradient_kernel(index_ref, x_ref, d_ref, *refs):
    out_ref = refs[-1]
    x = x_ref[...]
    width = d_ref.shape[-1]
    for part in range(out_ref.shape[1] // width):
        columns = slice(part * width, (part + 1) * width)
        product = tn_dot(x, d_ref[part] if len(d_ref.shape) == 3 else d_ref[...])
        if len(refs) == 2:
            product = product + refs[0][:, columns].astype(jnp.float32)
        out_ref[:, columns] = product.astype(out_ref.dtype)


def gradient(x, d_rows, half, column=0, columns=1, got=None):
    rows, depth = x.shape
    size = depth // 2
    blocks = size // CHUNK
    if d_rows.ndim == 3:
        d_spec = pl.BlockSpec(d_rows.shape, lambda i, index: (0, 0, 0))
        width = d_rows.shape[0] * d_rows.shape[2]
    else:
        width = d_rows.shape[1] // columns
        d_spec = pl.BlockSpec((rows, width), lambda i, index: (0, column))
    block = pl.BlockSpec((CHUNK, width), lambda i, index: (i, 0))
    extra = [] if got is None else [got]
    return pl.pallas_call(
        gradient_kernel,
        grid_spec=pltpu.PrefetchScalarGridSpec(
            num_scalar_prefetch=1,
            grid=(blocks,),
            in_specs=[
                pl.BlockSpec((rows, CHUNK), lambda i, index: (0, index[0] * blocks + i)),
                d_spec,
            ]
            + [block for _ in extra],
            out_specs=block,
        ),
        out_shape=jax.ShapeDtypeStruct((size, width), jnp.bfloat16),
        compiler_params=limit(32),
        cost_estimate=HINT,
        name="gradient",
    )(half.reshape(1).astype(jnp.int32), x, d_rows, *extra)


def standardize(value):
    center = value - jnp.mean(value, axis=-1, keepdims=True)
    variance = jnp.mean(center * center, axis=-1, keepdims=True)
    scale = lax.rsqrt(variance + EPSILON)
    return center * scale, scale


def norm_backward(d_normed_rows, normal, scale, gain):
    scaled = d_normed_rows * gain
    mean = jnp.mean(scaled, axis=-1, keepdims=True)
    along = jnp.mean(scaled * normal, axis=-1, keepdims=True)
    return (scaled - mean - normal * along) * scale


def reorder(array, axis, sizes, spots):
    shape = array.shape
    count = math.prod(sizes)
    cut = shape[:axis] + tuple(sizes) + (shape[axis] // count,) + shape[axis + 1 :]
    spots = list(range(axis)) + [axis + spot for spot in spots]
    return array.reshape(cut).transpose(spots + list(range(len(spots), len(cut)))).reshape(shape)


def to_local(array, axis, far):
    return reorder(array, axis, (far, 2, 2, 2), (2, 1, 3, 0))


def to_natural(array, axis, far):
    return reorder(array, axis, (2, 2, 2, far), (3, 1, 0, 2))


def hidden_to_local(array, axis, far):
    return reorder(array, axis, (far, 2, 2, 2), (2, 1, 0, 3))


def hidden_to_natural(array, axis, far):
    return reorder(array, axis, (2, 2, far, 2), (2, 1, 0, 3))


def assemble_kernel(routes, index_ref, *refs):
    count = len(routes)
    pieces, stages = refs[:count], refs[-count - 2 : -2]
    wholes, (arrived, left) = refs[count : -count - 2], refs[-2:]
    incoming = [
        pltpu.make_async_copy(piece, stage, arrived.at[number])
        for number, (piece, stage) in enumerate(zip(pieces, stages))
    ]
    for copy in incoming:
        copy.start()
    outgoing = []
    for number, route in enumerate(routes):
        incoming[number].wait()
        size = pieces[number].shape[0]
        start = pl.multiple_of(index_ref[number] * size, 16)
        for part, (source, width, whole, target) in enumerate(route):
            copy = pltpu.make_async_copy(
                stages[number].at[:, pl.ds(source, width)],
                wholes[whole].at[pl.ds(start, size), pl.ds(target, width)],
                left.at[part, number],
            )
            copy.start()
            outgoing.append(copy)
    for copy in outgoing:
        copy.wait()


def assemble(pieces, indices, outs, routes=None):
    if routes is None:
        routes = [[(0, piece.shape[1], 0, 0)] for piece in pieces]
    count = len(pieces)
    anywhere = pl.BlockSpec(memory_space=pl.ANY)
    kind = pieces[0].dtype
    return pl.pallas_call(
        functools.partial(assemble_kernel, routes),
        in_specs=[pl.BlockSpec(memory_space=pltpu.SMEM)] + [anywhere] * count,
        out_specs=[anywhere] * len(outs),
        out_shape=[jax.ShapeDtypeStruct(shape, kind) for shape in outs],
        scratch_shapes=[pltpu.VMEM(piece.shape, kind) for piece in pieces]
        + [
            pltpu.SemaphoreType.DMA((count,)),
            pltpu.SemaphoreType.DMA((max(len(route) for route in routes), count)),
        ],
        compiler_params=limit(16),
        cost_estimate=HINT,
        name="assemble",
    )(jnp.stack(indices).astype(jnp.int32), *pieces)


def trade(array, axis):
    return lax.ppermute(array, axis, [(0, 1), (1, 0)])


def after(array, *others):
    return lax.optimization_barrier((array, *others))[0]


def gather_far(shard, far, widths=None):
    place = lax.axis_index("z")
    pieces, indices = [shard], [place]
    for step in range(1, far):
        pieces.append(lax.ppermute(shard, "z", [(i, (i + step) % far) for i in range(far)]))
        indices.append((place - step) % far)
    rows, width = shard.shape
    widths = widths or [width]
    route, column = [], 0
    for number, one in enumerate(widths):
        route.append((column, one, number, 0))
        column += one
    return assemble(pieces, indices, [(far * rows, one) for one in widths], [route] * far)


def spread(blocks, axis):
    return blocks | {key | {axis}: trade(block, axis) for key, block in blocks.items()}


def places(blocks, axes):
    indices = []
    for key in blocks:
        index = 0
        for axis in axes:
            place = lax.axis_index(axis)
            index = 2 * index + (1 - place if axis in key else place)
        indices.append(index)
    return indices


def order_blocks(blocks, axes):
    pieces = list(blocks.values())
    rows, width = pieces[0].shape
    return assemble(pieces, places(blocks, axes), [(len(pieces) * rows, width)])[0]


OWN = frozenset()
X, Y, XY = frozenset({"x"}), frozenset({"ctx"}), frozenset({"x", "ctx"})


def send_half(matrix, axis, outer=1):
    rows, width = matrix.shape
    place = lax.axis_index(axis)
    blocks = matrix.reshape(outer, 2, rows // (2 * outer), width)
    kept = lax.dynamic_index_in_dim(blocks, place, 1, False).reshape(rows // 2, width)
    sent = lax.dynamic_index_in_dim(blocks, 1 - place, 1, False).reshape(rows // 2, width)
    return kept, trade(sent, axis)


def add_half(halves, *follow):
    kept, got = halves
    got = after(got, *follow) if follow else got
    return (kept.astype(jnp.float32) + got.astype(jnp.float32)).astype(kept.dtype)


def send_far(matrix, far):
    size = matrix.shape[0] // far
    place = lax.axis_index("z")
    arrays = [lax.dynamic_slice_in_dim(matrix, place * size, size)]
    for step in range(1, far):
        sent = lax.dynamic_slice_in_dim(matrix, ((place + step) % far) * size, size)
        arrays.append(lax.ppermute(sent, "z", [(i, (i + step) % far) for i in range(far)]))
    return arrays


def add_far(arrays, *follow):
    own, *got = arrays
    if follow:
        got = [after(array, *follow) for array in got]
    return sum(array.astype(jnp.float32) for array in [own, *got])


def column_sums(array):
    return jnp.sum(array.astype(jnp.float32), axis=0)


def by_image(far):
    def on_device(
        inputs,
        cotangent,
        segment,
        w_qkv,
        b_query,
        b_value,
        w_out,
        b_out,
        norm1_gain,
        norm1_shift,
        norm2_gain,
        norm2_shift,
        w_up,
        b_up,
        w_down,
        b_down,
    ):
        place, core = lax.axis_index("ctx"), lax.axis_index("core")
        swap = lambda array: trade(array, "ctx")
        slots, width = inputs.shape
        half_width = width // 2
        pads = 2 * slots - IMAGES * SEQ
        rows = round_up(SEQ + pads, 16)
        near_width = w_up.shape[0] // 8

        inputs_far = swap(inputs)
        segment_far = swap(segment)
        small = jnp.concatenate(
            [b_query, b_value, b_out, norm1_gain, norm1_shift, norm2_gain, norm2_shift, b_down, b_up]
        )
        shard_rows = w_qkv.shape[0] // 8
        small_count = small.shape[0]
        small_rows = round_up(small_count, 128) // 128
        small = jnp.pad(small, (0, shard_rows * 128 - small_count)).reshape(shard_rows, 128)
        shard_qkv = unfold(w_qkv).reshape(shard_rows, 3, 2, half_width)
        halves = [shard_qkv[:, :, side].reshape(shard_rows, 3 * half_width) for side in range(2)]
        half_qkv = 3 * half_width
        far_one, far_two = gather_far(
            jnp.concatenate([halves[0], small, halves[1]], axis=1), far, [half_qkv + 128, half_qkv]
        )
        shard_up = jnp.concatenate(
            [to_local(unfold(w_out), 1, far), hidden_to_local(unfold(w_up), 1, far)], axis=1
        )
        up_width = w_up.shape[1] * 8
        up_cut = (width + up_width) // 2
        far_up = gather_far(after(shard_up, far_one), far, [up_cut, up_cut])
        far_one, far_two = after(far_one, inputs_far), after(far_two, inputs_far)
        one = spread(spread({OWN: far_one}, "x"), "ctx")
        two = spread(spread({OWN: far_two}, "ctx"), "x")
        shard_down = after(to_local(unfold(w_down), 1, far), far_up[0])
        near_down = order_blocks(spread({OWN: shard_down}, "ctx"), ["ctx"])
        one_core, two_core = spread(one, "core"), spread(two, "core")
        axes = ["core", "x", "ctx"]
        routes = [[(0, half_qkv, 0, 0), (half_qkv, 128, 1, 0)]] * 8
        qkv_one, small_local = assemble(
            list(one_core.values()),
            places(one_core, axes),
            [(width, half_qkv), (width, 128)],
            routes,
        )
        qkv_two = order_blocks(two_core, axes)
        up_one = spread(spread({OWN: after(far_up[0], one[XY])}, "x"), "ctx")
        up_two = spread(spread({OWN: after(far_up[1], two[XY])}, "ctx"), "x")
        far_down = gather_far(near_down, far)[0]

        devices = 8 * far
        small_core = small_local.reshape(devices, shard_rows, 128)[:, :small_rows]
        small_core = small_core.astype(jnp.float32).reshape(devices, -1)
        small_all = to_natural(small_core, 0, far)
        piece = lambda table, index: table[:, index * near_width : (index + 1) * near_width].reshape(-1)
        query_bias = piece(small_all, 0)
        value_bias = piece(small_all, 1)
        out_bias, first_gain, first_shift, second_gain, second_shift, down_bias = (
            piece(small_core, index) for index in range(2, 8)
        )
        up_bias = small_all[:, 8 * near_width : small_count].reshape(-1)
        up_bias = hidden_to_local(up_bias, 0, far)

        slot = jnp.arange(slots)
        earlier = slot[:, None] < slot[None, :]

        def ranks(own, other, other_first):
            inside = jnp.sum((own[:, None] == own[None, :]) & earlier, axis=0)
            outside = jnp.sum(other[:, None] == own[None, :], axis=0)
            return inside + jnp.where(other_first, outside, 0)

        rank_near = ranks(segment, segment_far, place == 1)
        rank_far = ranks(segment_far, segment, place == 0)

        def positions(ids, rank, image):
            return jnp.where(ids == image, rank, jnp.where(ids < 0, SEQ + rank, -1))

        row = jnp.arange(rows)
        spot_near = positions(segment, rank_near, place)
        spot_far = positions(segment_far, rank_far, place)
        pick_near = (spot_near[None, :] == row[:, None]).astype(jnp.bfloat16)
        pick_far = (spot_far[None, :] == row[:, None]).astype(jnp.bfloat16)
        spot_other = jnp.where(segment == 1 - place, rank_near, -1)
        give_near = (spot_near[:, None] == row[None, :]).astype(jnp.bfloat16)
        give_far = (spot_other[:, None] == row[None, :]).astype(jnp.bfloat16)
        column = jnp.arange(width)
        to_core = (column[:, None] == to_local(column, 0, far)[None, :]).astype(jnp.bfloat16)

        def take(near, other):
            picked = matmul(pick_near, near) + matmul(pick_far, other)
            return matmul(picked.astype(jnp.bfloat16), to_core)

        def to_give(array):
            natural = nt_dot(array.astype(jnp.bfloat16), to_core).astype(jnp.bfloat16)
            return natural, swap(natural)

        def give(both, *follow):
            near, other = both
            return matmul(give_near, near) + matmul(give_far, after(other, *follow))

        kind = (row >= SEQ).astype(jnp.int32) + (row >= SEQ + pads).astype(jnp.int32)
        bias = jnp.where(kind[:, None] == kind[None, :], 0.0, -1e30).astype(jnp.float32)

        values_in = take(inputs, inputs_far)
        normal1, scale1 = standardize(values_in)
        normed1 = (normal1 * first_gain + first_shift).astype(jnp.bfloat16)
        joined_bias = [
            jnp.concatenate(
                [query_bias[cut], jnp.zeros((half_width,), jnp.float32), value_bias[cut]]
            )
            for cut in (slice(0, half_width), slice(half_width, width))
        ]
        joined_one = project(normed1, qkv_one, joined_bias[0])
        attended_one, log_one = attention_forward(after(joined_one, near_down), bias)
        joined_two = project(after(normed1, attended_one), qkv_two, joined_bias[1])
        up_near = assemble(
            list(up_one.values()) + list(up_two.values()),
            places(up_one, ["x", "ctx"]) + places(up_two, ["x", "ctx"]),
            [(half_width, width + up_width)],
            [[(0, up_cut, 0, 0)]] * 4 + [[(0, up_cut, 0, up_cut)]] * 4,
        )[0]
        up_blocks = spread({OWN: up_near}, "core")
        attended_two, log_two = attention_forward(joined_two, bias)
        attended = jnp.concatenate([attended_one, attended_two], axis=1)
        cotangent_far = swap(after(cotangent, up_near))
        down_blocks = spread({OWN: after(far_down, up_near)}, "x")
        out_rows, up_weight = assemble(
            list(up_blocks.values()),
            places(up_blocks, ["core"]),
            [(width, width), (width, up_width)],
            [[(0, width, 0, 0), (width, up_width, 1, 0)]] * 2,
        )
        out_weight = to_natural(out_rows, 0, far)
        middle = values_in + matmul(attended, out_weight) + out_bias
        normal2, scale2 = standardize(middle)
        normed2 = (normal2 * second_gain + second_shift).astype(jnp.bfloat16)
        active, slope = hidden_layer(normed2, up_weight, up_bias)

        live = (row < SEQ).astype(jnp.float32)[:, None]
        d_out = take(cotangent, cotangent_far) * live
        d_out_low = d_out.astype(jnp.bfloat16)
        down_core = trade(gradient(active, d_out_low, 1 - core), "core")
        down_blocks = {key: after(block, active) for key, block in down_blocks.items()}
        down_weight = order_blocks(spread(down_blocks, "core"), ["core", "x"])
        last = last_layer(active, down_weight, middle, down_bias)
        last_given = to_give(last)
        down_x = send_half(
            gradient(active, d_out_low, core, got=after(down_core, last_given[0])), "x"
        )
        d_hidden, up_sums = d_hidden_layer(after(d_out_low, down_x[0]), down_weight, slope)
        up_core = [
            trade(gradient(normed2, d_hidden, 1 - core, side, 2), "core") for side in range(2)
        ]
        d_normed2 = d_normed(d_hidden, up_weight)
        d_middle = d_out + norm_backward(d_normed2, normal2, scale2, second_gain)
        d_branch = d_middle.astype(jnp.bfloat16)
        up_kept = [
            gradient(normed2, d_hidden, core, side, 2, after(up_core[side], d_branch))
            for side in range(2)
        ]
        up_one = send_half(up_kept[0], "ctx", 2)
        up_two = send_half(up_kept[1], "x")
        d_branch = after(d_branch, up_one[0], up_two[0])
        grad_out = to_local(matmul(attended.T, d_branch).astype(jnp.bfloat16), 0, far)
        out_core = send_half(grad_out, "core")
        d_attended = matmul(d_branch, out_weight.T).astype(jnp.bfloat16)
        outputs = give(last_given, d_attended).astype(jnp.bfloat16)
        out_x = send_half(add_half(out_core, d_attended), "x")
        down_far = send_far(add_half(down_x, d_attended), far)
        d_attended = after(d_attended, out_x[0], down_far[0])
        d_one = attention_backward(joined_one, d_attended, 0, log_one, bias)
        one_core = trade(gradient(normed1, d_one, 1 - core), "core")
        partial = d_normed(d_one, qkv_one)
        d_two = attention_backward(
            joined_two, after(d_attended, partial), half_width // PAIR, log_two, bias
        )
        two_core = trade(gradient(normed1, d_two, 1 - core), "core")
        qkv_one_x = send_half(gradient(normed1, d_one, core, got=after(one_core, d_two)), "x")
        up_one = send_half(add_half(up_one, d_two), "x")
        up_two = send_half(add_half(up_two, d_two), "ctx")
        out_y = send_half(add_half(out_x, d_two), "ctx")
        d_two_tied = after(d_two, qkv_one_x[0], up_one[0], up_two[0], out_y[0])
        d_normed1 = d_normed(d_two_tied, qkv_two, partial)
        d_last = d_middle + norm_backward(d_normed1, normal1, scale1, first_gain)
        d_last_given = to_give(d_last)
        qkv_two_y = send_half(
            gradient(normed1, d_two, core, got=after(two_core, d_last_given[0])), "ctx", 2
        )
        down_y = send_half(add_far(down_far, d_last_given[0]).astype(jnp.bfloat16), "ctx")
        up_one_far = send_far(add_half(up_one, qkv_two_y[0], down_y[0]), far)
        qkv_one_y = send_half(add_half(qkv_one_x, up_one_far[0]), "ctx")
        up_two_far = send_far(add_half(up_two, qkv_one_y[0]), far)
        out_far = send_far(add_half(out_y, up_two_far[0]), far)
        qkv_two_x = send_half(add_half(qkv_two_y, out_far[0]), "x")
        qkv_one_far = send_far(add_half(qkv_one_y, qkv_two_x[0]), far)
        qkv_two_far = send_far(add_half(qkv_two_x, qkv_one_far[0]), far)

        part = lambda vector: vector.reshape(devices, -1)
        core_sums = jnp.concatenate(
            [
                part(column_sums(array))
                for array in (
                    d_branch,
                    d_normed1 * normal1,
                    d_normed1,
                    d_normed2 * normal2,
                    d_normed2,
                    d_out_low,
                )
            ],
            axis=1,
        )
        joined_sums = [
            part(jnp.concatenate([column_sums(d_one[index]), column_sums(d_two[index])]))
            for index in (0, 2)
        ]
        joined_sums = jnp.concatenate(joined_sums, axis=1)
        up_sums = part(hidden_to_natural(up_sums[0], 0, far))
        small_sums = jnp.concatenate(
            [to_local(joined_sums, 0, far), core_sums, to_local(up_sums, 0, far)], axis=1
        )
        for axis in axes:
            small_sums = add_half(send_half(small_sums, axis))
        small_sums = add_far(send_far(small_sums, far))[0]

        sum_down = add_half(down_y).astype(jnp.float32)
        sum_up = jnp.concatenate([add_far(up_one_far), add_far(up_two_far)], axis=1)
        sum_out = add_far(out_far)
        sum_qkv = [
            add_far(arrays).reshape(shard_rows, 3, 1, half_width)
            for arrays in (qkv_one_far, qkv_two_far)
        ]
        sum_qkv = jnp.concatenate(sum_qkv, axis=2).reshape(shard_rows, 3 * width)
        input_grad = give(d_last_given, qkv_two_far[0])
        own = lambda index: small_sums[index * near_width : (index + 1) * near_width]
        back = lambda matrix: refold(to_natural(matrix, 1, far))
        return (
            outputs,
            input_grad,
            refold(sum_qkv),
            own(0),
            own(1),
            back(sum_out),
            own(2),
            own(3),
            own(4),
            own(5),
            own(6),
            refold(hidden_to_natural(sum_up, 1, far)),
            small_sums[8 * near_width :],
            back(sum_down),
            own(7),
        )

    return on_device


def solution(mesh):
    if mesh.shape["ctx"] == IMAGES and mesh.shape["dp"] % 4 == 0:
        far, axes = mesh.shape["dp"] // 4, ("z", "x", "core", "ctx")
        mesh = jax.sharding.Mesh(mesh.devices.reshape(far, 2, 2, IMAGES), axes)
        body = by_image(far)
    else:
        body, axes = on_device, ("dp", "ctx")
    matrix, vector = P(axes, None), P(axes)
    return jax.shard_map(
        body,
        mesh=mesh,
        in_specs=(matrix, matrix, vector, matrix, vector, vector, matrix)
        + (vector,) * 5
        + (matrix, vector, matrix, vector),
        out_specs=(matrix, matrix, matrix, vector, vector, matrix)
        + (vector,) * 5
        + (matrix, vector, matrix, vector),
        check_vma=False,
    )
```

```python
import functools
import math

import jax
import jax.numpy as jnp
from jax import lax
from jax.experimental import pallas as pl
from jax.experimental.pallas import tpu as pltpu
from jax.sharding import PartitionSpec as P

HD = 64


EPSILON = 1e-06


def layer_norm(value, gain, shift):
    center = value - jnp.mean(value, axis=-1, keepdims=True)
    variance = jnp.mean(center * center, axis=-1, keepdims=True)
    return center * lax.rsqrt(variance + EPSILON) * gain + shift


def gelu_exact(value):
    return jax.nn.gelu(value, approximate=False)


def matmul(left, right):
    return jnp.dot(left, right, preferred_element_type=jnp.float32)


def unfold(stored):
    return stored.reshape(stored.shape[0] // 8, stored.shape[1] * 8)


def refold(matrix):
    return matrix.reshape(matrix.shape[0] * 8, matrix.shape[1] // 8)


def on_device(
    inputs,
    cotangent,
    segment,
    w_qkv,
    b_query,
    b_value,
    w_out,
    b_out,
    norm1_gain,
    norm1_shift,
    norm2_gain,
    norm2_shift,
    w_up,
    b_up,
    w_down,
    b_down,
):
    gathered = (
        lax.all_gather(w_qkv, ("dp", "ctx"), axis=0, tiled=True),
        lax.all_gather(b_query, ("dp", "ctx"), axis=0, tiled=True),
        lax.all_gather(b_value, ("dp", "ctx"), axis=0, tiled=True),
        lax.all_gather(w_out, ("dp", "ctx"), axis=0, tiled=True),
        lax.all_gather(b_out, ("dp", "ctx"), axis=0, tiled=True),
        lax.all_gather(norm1_gain, ("dp", "ctx"), axis=0, tiled=True),
        lax.all_gather(norm1_shift, ("dp", "ctx"), axis=0, tiled=True),
        lax.all_gather(norm2_gain, ("dp", "ctx"), axis=0, tiled=True),
        lax.all_gather(norm2_shift, ("dp", "ctx"), axis=0, tiled=True),
        lax.all_gather(w_up, ("dp", "ctx"), axis=0, tiled=True),
        lax.all_gather(b_up, ("dp", "ctx"), axis=0, tiled=True),
        lax.all_gather(w_down, ("dp", "ctx"), axis=0, tiled=True),
        lax.all_gather(b_down, ("dp", "ctx"), axis=0, tiled=True),
    )
    (
        qkv_stored,
        query_bias,
        value_bias,
        out_stored,
        out_bias,
        gain_one,
        shift_one,
        gain_two,
        shift_two,
        up_stored,
        up_bias,
        down_stored,
        down_bias,
    ) = gathered
    qkv_weight = unfold(qkv_stored)
    out_weight = unfold(out_stored)
    up_weight = unfold(up_stored)
    down_weight = unfold(down_stored)
    first_gain = gain_one.astype(jnp.float32)
    first_shift = shift_one.astype(jnp.float32)
    second_gain = gain_two.astype(jnp.float32)
    second_shift = shift_two.astype(jnp.float32)
    row_count = inputs.shape[0]
    model_width = out_weight.shape[0]
    head_count = model_width // HD
    score_scale = 1.0 / math.sqrt(HD)
    values_in = inputs.astype(jnp.float32)
    normed1 = layer_norm(values_in, first_gain, first_shift).astype(jnp.bfloat16)
    joined = matmul(normed1, qkv_weight)
    queries = (joined[:, :model_width] + query_bias.astype(jnp.float32)).astype(jnp.bfloat16)
    key_rows = joined[:, model_width : 2 * model_width].astype(jnp.bfloat16)
    value_rows = (joined[:, 2 * model_width :] + value_bias.astype(jnp.float32)).astype(
        jnp.bfloat16
    )
    key_all, value_all, seg_all = (
        lax.all_gather(key_rows, "ctx", axis=0, tiled=True),
        lax.all_gather(value_rows, "ctx", axis=0, tiled=True),
        lax.all_gather(segment.astype(jnp.bfloat16), "ctx", axis=0, tiled=True),
    )
    key_count = key_all.shape[0]
    query_heads = queries.reshape(row_count, head_count, HD)
    key_heads = key_all.reshape(key_count, head_count, HD)
    value_heads = value_all.reshape(key_count, head_count, HD)
    own_seg = segment.astype(jnp.float32)
    group_seg = seg_all.astype(jnp.float32)
    same_seg = own_seg[:, None] == group_seg[None, :]

    def make_scores():
        raw = (
            jnp.einsum("qhd,khd->hqk", query_heads, key_heads, preferred_element_type=jnp.float32)
            * score_scale
        )
        return jnp.where(same_seg[None], raw, -1e30)

    scores = make_scores()
    row_max = jnp.max(scores, axis=-1, keepdims=True)
    expo = jnp.exp(scores - row_max)
    row_total = jnp.sum(expo, axis=-1, keepdims=True)
    probs_low = (expo / row_total).astype(jnp.bfloat16)
    log_total = row_max + jnp.log(row_total)
    mixed = jnp.einsum("hqk,khd->qhd", probs_low, value_heads, preferred_element_type=jnp.float32)
    attended = mixed.reshape(row_count, model_width).astype(jnp.bfloat16)
    middle = values_in + matmul(attended, out_weight) + out_bias.astype(jnp.float32)
    normed2 = layer_norm(middle, second_gain, second_shift).astype(jnp.bfloat16)
    hidden = matmul(normed2, up_weight) + up_bias.astype(jnp.float32)
    active = gelu_exact(hidden).astype(jnp.bfloat16)
    outputs = (middle + matmul(active, down_weight) + down_bias.astype(jnp.float32)).astype(
        jnp.bfloat16
    )
    back_qkv, back_out, back_up, back_down = (qkv_weight, out_weight, up_weight, down_weight)
    valid = (segment >= 0).astype(jnp.float32)[:, None]
    d_out = cotangent.astype(jnp.float32) * valid
    d_out_low = d_out.astype(jnp.bfloat16)
    grad_down = refold(matmul(active.T, d_out_low))
    grad_down_bias = jnp.sum(d_out_low.astype(jnp.float32), axis=0)
    d_active = matmul(d_out_low, back_down.T)
    gelu_value, gelu_pull = jax.vjp(gelu_exact, hidden)
    d_hidden = gelu_pull(d_active)[0].astype(jnp.bfloat16)
    grad_up = refold(matmul(normed2.T, d_hidden))
    grad_up_bias = jnp.sum(d_hidden.astype(jnp.float32), axis=0)
    d_normed2 = matmul(d_hidden, back_up.T)
    norm_value, norm_pull = jax.vjp(layer_norm, middle, second_gain, second_shift)
    d_middle_norm, grad_gain_two, grad_shift_two = norm_pull(d_normed2)
    d_middle = d_out + d_middle_norm
    d_branch = d_middle.astype(jnp.bfloat16)
    grad_out = refold(matmul(attended.T, d_branch))
    grad_out_bias = jnp.sum(d_branch.astype(jnp.float32), axis=0)
    d_attended_flat = matmul(d_branch, back_out.T).astype(jnp.bfloat16)
    d_attended = d_attended_flat.reshape(row_count, head_count, HD)
    scores = make_scores()
    probs = jnp.exp(scores - log_total)
    d_probs = jnp.einsum(
        "qhd,khd->hqk", d_attended, value_heads, preferred_element_type=jnp.float32
    )
    delta_rows = jnp.sum(probs * d_probs, axis=-1, keepdims=True)
    d_scores = (probs * (d_probs - delta_rows)).astype(jnp.bfloat16)
    d_query = (
        jnp.einsum("hqk,khd->qhd", d_scores, key_heads, preferred_element_type=jnp.float32)
        * score_scale
    ).reshape(row_count, model_width)
    probs_again = probs.astype(jnp.bfloat16)
    d_key_all = (
        jnp.einsum("hqk,qhd->khd", d_scores, query_heads, preferred_element_type=jnp.float32)
        * score_scale
    ).reshape(key_count, model_width)
    d_value_all = jnp.einsum(
        "hqk,qhd->khd", probs_again, d_attended, preferred_element_type=jnp.float32
    ).reshape(key_count, model_width)
    d_key, d_value = (
        lax.psum_scatter(
            d_key_all.astype(jnp.bfloat16), "ctx", scatter_dimension=0, tiled=True
        ).astype(jnp.float32),
        lax.psum_scatter(
            d_value_all.astype(jnp.bfloat16), "ctx", scatter_dimension=0, tiled=True
        ).astype(jnp.float32),
    )
    d_query_low = d_query.astype(jnp.bfloat16)
    d_value_low = d_value.astype(jnp.bfloat16)
    d_joined = jnp.concatenate([d_query_low, d_key.astype(jnp.bfloat16), d_value_low], axis=1)
    grad_qkv = refold(matmul(normed1.T, d_joined))
    grad_query_bias = jnp.sum(d_query_low.astype(jnp.float32), axis=0)
    grad_value_bias = jnp.sum(d_value_low.astype(jnp.float32), axis=0)
    d_normed1 = matmul(d_joined, back_qkv.T)
    first_value, first_pull = jax.vjp(layer_norm, values_in, first_gain, first_shift)
    d_input_norm, grad_gain_one, grad_shift_one = first_pull(d_normed1)
    input_grad = d_middle + d_input_norm
    partial_sums = (
        lax.psum_scatter(
            grad_qkv.astype(jnp.bfloat16), "dp", scatter_dimension=0, tiled=True
        ).astype(jnp.float32),
        lax.psum_scatter(
            grad_query_bias.astype(jnp.bfloat16), "dp", scatter_dimension=0, tiled=True
        ).astype(jnp.float32),
        lax.psum_scatter(
            grad_value_bias.astype(jnp.bfloat16), "dp", scatter_dimension=0, tiled=True
        ).astype(jnp.float32),
        lax.psum_scatter(
            grad_out.astype(jnp.bfloat16), "dp", scatter_dimension=0, tiled=True
        ).astype(jnp.float32),
        lax.psum_scatter(
            grad_out_bias.astype(jnp.bfloat16), "dp", scatter_dimension=0, tiled=True
        ).astype(jnp.float32),
        lax.psum_scatter(
            grad_gain_one.astype(jnp.bfloat16), "dp", scatter_dimension=0, tiled=True
        ).astype(jnp.float32),
        lax.psum_scatter(
            grad_shift_one.astype(jnp.bfloat16), "dp", scatter_dimension=0, tiled=True
        ).astype(jnp.float32),
        lax.psum_scatter(
            grad_gain_two.astype(jnp.bfloat16), "dp", scatter_dimension=0, tiled=True
        ).astype(jnp.float32),
        lax.psum_scatter(
            grad_shift_two.astype(jnp.bfloat16), "dp", scatter_dimension=0, tiled=True
        ).astype(jnp.float32),
        lax.psum_scatter(
            grad_up.astype(jnp.bfloat16), "dp", scatter_dimension=0, tiled=True
        ).astype(jnp.float32),
        lax.psum_scatter(
            grad_up_bias.astype(jnp.bfloat16), "dp", scatter_dimension=0, tiled=True
        ).astype(jnp.float32),
        lax.psum_scatter(
            grad_down.astype(jnp.bfloat16), "dp", scatter_dimension=0, tiled=True
        ).astype(jnp.float32),
        lax.psum_scatter(
            grad_down_bias.astype(jnp.bfloat16), "dp", scatter_dimension=0, tiled=True
        ).astype(jnp.float32),
    )
    all_sums = (
        lax.psum_scatter(
            partial_sums[0].astype(jnp.bfloat16), "ctx", scatter_dimension=0, tiled=True
        ).astype(jnp.float32),
        lax.psum_scatter(
            partial_sums[1].astype(jnp.bfloat16), "ctx", scatter_dimension=0, tiled=True
        ).astype(jnp.float32),
        lax.psum_scatter(
            partial_sums[2].astype(jnp.bfloat16), "ctx", scatter_dimension=0, tiled=True
        ).astype(jnp.float32),
        lax.psum_scatter(
            partial_sums[3].astype(jnp.bfloat16), "ctx", scatter_dimension=0, tiled=True
        ).astype(jnp.float32),
        lax.psum_scatter(
            partial_sums[4].astype(jnp.bfloat16), "ctx", scatter_dimension=0, tiled=True
        ).astype(jnp.float32),
        lax.psum_scatter(
            partial_sums[5].astype(jnp.bfloat16), "ctx", scatter_dimension=0, tiled=True
        ).astype(jnp.float32),
        lax.psum_scatter(
            partial_sums[6].astype(jnp.bfloat16), "ctx", scatter_dimension=0, tiled=True
        ).astype(jnp.float32),
        lax.psum_scatter(
            partial_sums[7].astype(jnp.bfloat16), "ctx", scatter_dimension=0, tiled=True
        ).astype(jnp.float32),
        lax.psum_scatter(
            partial_sums[8].astype(jnp.bfloat16), "ctx", scatter_dimension=0, tiled=True
        ).astype(jnp.float32),
        lax.psum_scatter(
            partial_sums[9].astype(jnp.bfloat16), "ctx", scatter_dimension=0, tiled=True
        ).astype(jnp.float32),
        lax.psum_scatter(
            partial_sums[10].astype(jnp.bfloat16), "ctx", scatter_dimension=0, tiled=True
        ).astype(jnp.float32),
        lax.psum_scatter(
            partial_sums[11].astype(jnp.bfloat16), "ctx", scatter_dimension=0, tiled=True
        ).astype(jnp.float32),
        lax.psum_scatter(
            partial_sums[12].astype(jnp.bfloat16), "ctx", scatter_dimension=0, tiled=True
        ).astype(jnp.float32),
    )
    (
        sum_qkv,
        sum_query_bias,
        sum_value_bias,
        sum_out,
        sum_out_bias,
        sum_gain_one,
        sum_shift_one,
        sum_gain_two,
        sum_shift_two,
        sum_up,
        sum_up_bias,
        sum_down,
        sum_down_bias,
    ) = all_sums
    return (
        outputs,
        input_grad,
        sum_qkv,
        sum_query_bias,
        sum_value_bias,
        sum_out,
        sum_out_bias,
        sum_gain_one,
        sum_shift_one,
        sum_gain_two,
        sum_shift_two,
        sum_up,
        sum_up_bias,
        sum_down,
        sum_down_bias,
    )


SEQ = 577
IMAGES = 2
PAIR = 2 * HD
CHUNK = 256
BLOCK = 512
HINT = pl.CostEstimate(flops=1, bytes_accessed=1, transcendentals=0)
ERFC = (
    0.09873409569263458,
    0.09871950000524521,
    0.09271052479743958,
    0.08134904503822327,
    0.056456614285707474,
    0.07422702759504318,
    -0.050631966441869736,
    0.11820460855960846,
    -0.09110676497220993,
    0.021337319165468216,
)
ERFC_STEP = 0.35


def round_up(count, unit):
    return -(-count // unit) * unit


def limit(mebibytes):
    return pltpu.CompilerParams(vmem_limit_bytes=mebibytes * 2**20)


def chunks_of(count):
    return [(start, min(CHUNK, count - start)) for start in range(0, count, CHUNK)]


def nt_dot(left, right):
    return lax.dot_general(
        left, right, (((1,), (1,)), ((), ())), preferred_element_type=jnp.float32
    )


def tn_dot(left, right):
    return lax.dot_general(
        left, right, (((0,), (0,)), ((), ())), preferred_element_type=jnp.float32
    )


def half_mask(rows):
    return lax.broadcasted_iota(jnp.int32, (rows, PAIR), 1) < HD


def forward_kernel(query_ref, key_ref, value_ref, bias_ref, *refs):
    attended_ref, log_ref = refs[-2:]
    rows = query_ref.shape[1]
    first = half_mask(rows)
    zero = jnp.zeros((rows, PAIR), jnp.bfloat16)
    key = key_ref[0]
    key_sides = (jnp.where(first, key, zero), jnp.where(first, zero, key))
    value_t = value_ref[0].astype(jnp.float32).T.astype(jnp.bfloat16)
    scale = jnp.bfloat16(1.0 / math.sqrt(HD))
    for start, size in chunks_of(rows):
        query = query_ref[0, start : start + size, :] * scale
        bias = bias_ref[:, start : start + size]
        outs = []
        for side in range(2):
            scores = nt_dot(key_sides[side], query) + bias
            top = jnp.max(scores, axis=0, keepdims=True)
            expo = jnp.exp(scores - top)
            total = jnp.sum(expo, axis=0, keepdims=True)
            probs_low = (expo * (1.0 / total)).astype(jnp.bfloat16)
            outs.append(matmul(value_t[side * HD : (side + 1) * HD, :], probs_low))
            log_ref[0, side : side + 1, start : start + size] = top + jnp.log(total)
        mixed = jnp.concatenate(outs, axis=0)
        attended_ref[start : start + size, :] = mixed.T.astype(jnp.bfloat16)


def backward_kernel(
    query_ref, key_ref, value_ref, d_ref, log_ref, bias_ref, joined_ref, dk_sum, dv_sum
):
    rows = query_ref.shape[1]
    first = half_mask(rows)
    zero = jnp.zeros((rows, PAIR), jnp.bfloat16)
    key = key_ref[0]
    value = value_ref[0]
    key_sides = (jnp.where(first, key, zero), jnp.where(first, zero, key))
    value_sides = (jnp.where(first, value, zero), jnp.where(first, zero, value))
    key_t = key.astype(jnp.float32).T.astype(jnp.bfloat16)
    scale = jnp.bfloat16(1.0 / math.sqrt(HD))
    for start, size in chunks_of(rows):
        query = query_ref[0, start : start + size, :] * scale
        d_rows = d_ref[start : start + size, :]
        bias = bias_ref[:, start : start + size]
        outs = []
        for side in range(2):
            scores = nt_dot(key_sides[side], query) + bias
            probs = jnp.exp(scores - log_ref[0, side : side + 1, start : start + size])
            d_probs = nt_dot(value_sides[side], d_rows)
            product = probs * d_probs
            delta = jnp.sum(product, axis=0, keepdims=True)
            d_scores = (product - probs * delta).astype(jnp.bfloat16)
            d_value = matmul(probs.astype(jnp.bfloat16), d_rows)
            d_key = matmul(d_scores, query)
            if start == 0:
                dv_sum[side] = d_value
                dk_sum[side] = d_key
            else:
                dv_sum[side] += d_value
                dk_sum[side] += d_key
            outs.append(matmul(key_t[side * HD : (side + 1) * HD, :], d_scores))
        d_query = jnp.concatenate(outs, axis=0) * (1.0 / math.sqrt(HD))
        joined_ref[0, start : start + size, :] = d_query.T.astype(jnp.bfloat16)
    joined_ref[1] = jnp.where(first, dk_sum[0], dk_sum[1]).astype(jnp.bfloat16)
    joined_ref[2] = jnp.where(first, dv_sum[0], dv_sum[1]).astype(jnp.bfloat16)


def pair_spec(rows, part):
    return pl.BlockSpec((1, rows, PAIR), lambda i: (part, 0, i))


def attention_forward(joined, bias, total, first_pair, base=None):
    rows, width = joined.shape[1:]
    pairs = width // PAIR
    extra = [] if base is None else [base]
    return pl.pallas_call(
        forward_kernel,
        grid=(pairs,),
        in_specs=[pair_spec(rows, part) for part in range(3)]
        + [pl.BlockSpec((rows, rows), lambda i: (0, 0))]
        + [pl.BlockSpec(memory_space=pl.ANY) for _ in extra],
        out_specs=[
            pl.BlockSpec((rows, PAIR), lambda i: (0, first_pair + i)),
            pl.BlockSpec((1, 2, rows), lambda i: (i, 0, 0)),
        ],
        out_shape=[
            jax.ShapeDtypeStruct((rows, total), jnp.bfloat16),
            jax.ShapeDtypeStruct((pairs, 2, rows), jnp.float32),
        ],
        input_output_aliases={4: 0} if extra else {},
        compiler_params=limit(32),
        cost_estimate=HINT,
        name="attention_forward",
    )(joined, joined, joined, bias, *extra)


def attention_backward(joined, d_attended, first_pair, log_total, bias):
    rows, width = joined.shape[1:]
    return pl.pallas_call(
        backward_kernel,
        grid=(width // PAIR,),
        in_specs=[pair_spec(rows, part) for part in range(3)]
        + [
            pl.BlockSpec((rows, PAIR), lambda i: (0, first_pair + i)),
            pl.BlockSpec((1, 2, rows), lambda i: (i, 0, 0)),
            pl.BlockSpec((rows, rows), lambda i: (0, 0)),
        ],
        out_specs=pl.BlockSpec((3, rows, PAIR), lambda i: (0, 0, i)),
        out_shape=jax.ShapeDtypeStruct((3, rows, width), jnp.bfloat16),
        scratch_shapes=[pltpu.VMEM((2, rows, PAIR), jnp.float32)] * 2,
        compiler_params=limit(32),
        cost_estimate=HINT,
        name="attention_backward",
    )(joined, joined, joined, d_attended, log_total, bias)


def whole_spec(shape):
    return pl.BlockSpec(shape, lambda *_: (0,) * len(shape))


def project_kernel(x_ref, weight_ref, bias_ref, out_ref):
    out_ref[0] = (matmul(x_ref[...], weight_ref[...]) + bias_ref[...]).astype(out_ref.dtype)


def project(x, weight, bias):
    rows, depth = x.shape
    width = weight.shape[1] // 3
    return pl.pallas_call(
        project_kernel,
        grid=(3,),
        in_specs=[
            whole_spec(x.shape),
            pl.BlockSpec((depth, width), lambda i: (0, i)),
            pl.BlockSpec((1, width), lambda i: (0, i)),
        ],
        out_specs=pl.BlockSpec((1, rows, width), lambda i: (i, 0, 0)),
        out_shape=jax.ShapeDtypeStruct((3, rows, width), jnp.bfloat16),
        compiler_params=limit(24),
        cost_estimate=HINT,
        name="project",
    )(x, weight, bias[None, :])


def hidden_kernel(x_ref, weight_ref, bias_ref, active_ref, slope_ref):
    hidden = matmul(x_ref[...], weight_ref[...]) + bias_ref[...]
    share = 1.0 / (1.0 + (ERFC_STEP * math.sqrt(0.5)) * jnp.abs(hidden))
    density = jnp.exp(-0.5 * hidden * hidden)
    tail = jnp.full_like(share, ERFC[-1])
    for factor in ERFC[-2::-1]:
        tail = tail * share + factor
    tail = tail * share * density
    phi = jnp.where(hidden < 0.0, tail, 1.0 - tail)
    active_ref[...] = (hidden * phi).astype(jnp.bfloat16)
    slope = phi + hidden * density * (1.0 / math.sqrt(2.0 * math.pi))
    slope_ref[...] = slope.astype(jnp.bfloat16)


def hidden_layer(x, weight, bias):
    rows, depth = x.shape
    width = weight.shape[1]
    block = pl.BlockSpec((rows, BLOCK), lambda i: (0, i))
    return pl.pallas_call(
        hidden_kernel,
        grid=(width // BLOCK,),
        in_specs=[
            whole_spec(x.shape),
            pl.BlockSpec((depth, BLOCK), lambda i: (0, i)),
            pl.BlockSpec((1, BLOCK), lambda i: (0, i)),
        ],
        out_specs=[block, block],
        out_shape=[jax.ShapeDtypeStruct((rows, width), jnp.bfloat16)] * 2,
        compiler_params=limit(32),
        cost_estimate=HINT,
        name="hidden_layer",
    )(x, weight, bias[None, :])


def last_kernel(active_ref, weight_ref, middle_ref, bias_ref, out_ref, total):
    step = pl.program_id(0)

    @pl.when(step == 0)
    def _():
        total[...] = middle_ref[...] + bias_ref[...]

    total[...] += matmul(active_ref[...], weight_ref[...])

    @pl.when(step == pl.num_programs(0) - 1)
    def _():
        out_ref[...] = total[...].astype(out_ref.dtype)


def last_layer(active, weight, middle, bias):
    rows, depth = active.shape
    width = weight.shape[1]
    return pl.pallas_call(
        last_kernel,
        grid=(depth // BLOCK,),
        in_specs=[
            pl.BlockSpec((rows, BLOCK), lambda i: (0, i)),
            pl.BlockSpec((BLOCK, width), lambda i: (i, 0)),
            whole_spec((rows, width)),
            whole_spec((1, width)),
        ],
        out_specs=whole_spec((rows, width)),
        out_shape=jax.ShapeDtypeStruct((rows, width), jnp.bfloat16),
        scratch_shapes=[pltpu.VMEM((rows, width), jnp.float32)],
        compiler_params=limit(52),
        cost_estimate=HINT,
        name="last_layer",
    )(active, weight, middle, bias[None, :])


def d_hidden_kernel(d_ref, weight_ref, slope_ref, out_ref, sum_ref):
    d_active = nt_dot(d_ref[...], weight_ref[...])
    d_hidden = (d_active * slope_ref[...].astype(jnp.float32)).astype(jnp.bfloat16)
    out_ref[...] = d_hidden
    sum_ref[...] = jnp.sum(d_hidden.astype(jnp.float32), axis=0, keepdims=True)


def d_hidden_layer(d_out, weight, slope):
    rows, depth = d_out.shape
    width = weight.shape[0]
    block = pl.BlockSpec((rows, BLOCK), lambda i: (0, i))
    return pl.pallas_call(
        d_hidden_kernel,
        grid=(width // BLOCK,),
        in_specs=[
            whole_spec(d_out.shape),
            pl.BlockSpec((BLOCK, depth), lambda i: (i, 0)),
            block,
        ],
        out_specs=[block, pl.BlockSpec((1, BLOCK), lambda i: (0, i))],
        out_shape=[
            jax.ShapeDtypeStruct((rows, width), jnp.bfloat16),
            jax.ShapeDtypeStruct((1, width), jnp.float32),
        ],
        compiler_params=limit(24),
        cost_estimate=HINT,
        name="d_hidden_layer",
    )(d_out, weight, slope)


def d_normed_kernel(d_ref, weight_ref, *refs):
    out_ref = refs[-1]
    d_rows = d_ref[0] if len(d_ref.shape) == 3 else d_ref[...]
    product = nt_dot(d_rows, weight_ref[...])
    step = pl.program_id(0)

    @pl.when(step == 0)
    def _():
        out_ref[...] = product + refs[0][...] if len(refs) == 2 else product

    @pl.when(step > 0)
    def _():
        out_ref[...] += product


def d_normed(d_rows, weight, base=None):
    rows, depth = d_rows.shape[-2], weight.shape[0]
    if d_rows.ndim == 3:
        d_spec = pl.BlockSpec((1, rows, BLOCK), lambda i: (i, 0, 0))
    else:
        d_spec = pl.BlockSpec((rows, BLOCK), lambda i: (0, i))
    extra = [] if base is None else [base]
    return pl.pallas_call(
        d_normed_kernel,
        grid=(weight.shape[1] // BLOCK,),
        in_specs=[d_spec, pl.BlockSpec((depth, BLOCK), lambda i: (0, i))]
        + [whole_spec((rows, depth)) for _ in extra],
        out_specs=whole_spec((rows, depth)),
        out_shape=jax.ShapeDtypeStruct((rows, depth), jnp.float32),
        compiler_params=limit(24),
        cost_estimate=HINT,
        name="d_normed",
    )(d_rows, weight, *extra)


def gradient_kernel(index_ref, x_ref, d_ref, *refs):
    out_ref = refs[-1]
    x = x_ref[...]
    width = d_ref.shape[-1]
    for part in range(out_ref.shape[1] // width):
        columns = slice(part * width, (part + 1) * width)
        product = tn_dot(x, d_ref[part] if len(d_ref.shape) == 3 else d_ref[...])
        if len(refs) == 2:
            product = product + refs[0][:, columns].astype(jnp.float32)
        out_ref[:, columns] = product.astype(out_ref.dtype)


def gradient(x, d_rows, half, column=0, columns=1, got=None):
    rows, depth = x.shape
    size = depth // 2
    blocks = size // CHUNK
    if d_rows.ndim == 3:
        d_spec = pl.BlockSpec(d_rows.shape, lambda i, index: (0, 0, 0))
        width = d_rows.shape[0] * d_rows.shape[2]
    else:
        width = d_rows.shape[1] // columns
        d_spec = pl.BlockSpec((rows, width), lambda i, index: (0, column))
    block = pl.BlockSpec((CHUNK, width), lambda i, index: (i, 0))
    extra = [] if got is None else [got]
    return pl.pallas_call(
        gradient_kernel,
        grid_spec=pltpu.PrefetchScalarGridSpec(
            num_scalar_prefetch=1,
            grid=(blocks,),
            in_specs=[
                pl.BlockSpec((rows, CHUNK), lambda i, index: (0, index[0] * blocks + i)),
                d_spec,
            ]
            + [block for _ in extra],
            out_specs=block,
        ),
        out_shape=jax.ShapeDtypeStruct((size, width), jnp.bfloat16),
        compiler_params=limit(32),
        cost_estimate=HINT,
        name="gradient",
    )(half.reshape(1).astype(jnp.int32), x, d_rows, *extra)


def standardize(value):
    center = value - jnp.mean(value, axis=-1, keepdims=True)
    variance = jnp.mean(center * center, axis=-1, keepdims=True)
    scale = lax.rsqrt(variance + EPSILON)
    return center * scale, scale


def norm_backward(d_normed_rows, normal, scale, gain):
    scaled = d_normed_rows * gain
    mean = jnp.mean(scaled, axis=-1, keepdims=True)
    along = jnp.mean(scaled * normal, axis=-1, keepdims=True)
    return (scaled - mean - normal * along) * scale


def reorder(array, axis, sizes, spots):
    shape = array.shape
    count = math.prod(sizes)
    cut = shape[:axis] + tuple(sizes) + (shape[axis] // count,) + shape[axis + 1 :]
    spots = list(range(axis)) + [axis + spot for spot in spots]
    return array.reshape(cut).transpose(spots + list(range(len(spots), len(cut)))).reshape(shape)


def to_local(array, axis, far):
    return reorder(array, axis, (far, 2, 2, 2), (2, 1, 3, 0))


def to_natural(array, axis, far):
    return reorder(array, axis, (2, 2, 2, far), (3, 1, 0, 2))


def hidden_to_local(array, axis, far):
    return reorder(array, axis, (far, 2, 2, 2), (2, 1, 0, 3))


def hidden_to_natural(array, axis, far):
    return reorder(array, axis, (2, 2, far, 2), (2, 1, 0, 3))


def assemble_kernel(routes, index_ref, *refs):
    count = len(routes)
    pieces, stages = refs[:count], refs[-count - 2 : -2]
    wholes, (arrived, left) = refs[count : -count - 2], refs[-2:]
    incoming = [
        pltpu.make_async_copy(piece, stage, arrived.at[number])
        for number, (piece, stage) in enumerate(zip(pieces, stages))
    ]
    for copy in incoming:
        copy.start()
    outgoing = []
    for number, route in enumerate(routes):
        incoming[number].wait()
        size = pieces[number].shape[0]
        start = pl.multiple_of(index_ref[number] * size, 16)
        for part, (source, width, whole, target) in enumerate(route):
            copy = pltpu.make_async_copy(
                stages[number].at[:, pl.ds(source, width)],
                wholes[whole].at[pl.ds(start, size), pl.ds(target, width)],
                left.at[part, number],
            )
            copy.start()
            outgoing.append(copy)
    for copy in outgoing:
        copy.wait()


def assemble(pieces, indices, outs, routes=None):
    if routes is None:
        routes = [[(0, piece.shape[1], 0, 0)] for piece in pieces]
    count = len(pieces)
    anywhere = pl.BlockSpec(memory_space=pl.ANY)
    kind = pieces[0].dtype
    return pl.pallas_call(
        functools.partial(assemble_kernel, routes),
        in_specs=[pl.BlockSpec(memory_space=pltpu.SMEM)] + [anywhere] * count,
        out_specs=[anywhere] * len(outs),
        out_shape=[jax.ShapeDtypeStruct(shape, kind) for shape in outs],
        scratch_shapes=[pltpu.VMEM(piece.shape, kind) for piece in pieces]
        + [
            pltpu.SemaphoreType.DMA((count,)),
            pltpu.SemaphoreType.DMA((max(len(route) for route in routes), count)),
        ],
        compiler_params=limit(16),
        cost_estimate=HINT,
        name="assemble",
    )(jnp.stack(indices).astype(jnp.int32), *pieces)


def trade(array, axis):
    return lax.ppermute(array, axis, [(0, 1), (1, 0)])


def after(array, *others):
    return lax.optimization_barrier((array, *others))[0]


def gather_far(shard, far, widths=None):
    place = lax.axis_index("z")
    pieces, indices = [shard], [place]
    for step in range(1, far):
        pieces.append(lax.ppermute(shard, "z", [(i, (i + step) % far) for i in range(far)]))
        indices.append((place - step) % far)
    rows, width = shard.shape
    widths = widths or [width]
    route, column = [], 0
    for number, one in enumerate(widths):
        route.append((column, one, number, 0))
        column += one
    return assemble(pieces, indices, [(far * rows, one) for one in widths], [route] * far)


def spread(blocks, axis):
    return blocks | {key | {axis}: trade(block, axis) for key, block in blocks.items()}


def tie_received(blocks, other):
    return {key: after(block, other) if key else block for key, block in blocks.items()}


def places(blocks, axes):
    indices = []
    for key in blocks:
        index = 0
        for axis in axes:
            place = lax.axis_index(axis)
            index = 2 * index + (1 - place if axis in key else place)
        indices.append(index)
    return indices


def order_blocks(blocks, axes):
    pieces = list(blocks.values())
    rows, width = pieces[0].shape
    return assemble(pieces, places(blocks, axes), [(len(pieces) * rows, width)])[0]


OWN = frozenset()


def send_half(matrix, axis, outer=1):
    rows, width = matrix.shape
    place = lax.axis_index(axis)
    blocks = matrix.reshape(outer, 2, rows // (2 * outer), width)
    kept = lax.dynamic_index_in_dim(blocks, place, 1, False).reshape(rows // 2, width)
    sent = lax.dynamic_index_in_dim(blocks, 1 - place, 1, False).reshape(rows // 2, width)
    return kept, trade(sent, axis)


def add_half(halves, *follow):
    kept, got = halves
    got = after(got, *follow) if follow else got
    return (kept.astype(jnp.float32) + got.astype(jnp.float32)).astype(kept.dtype)


def send_far(matrix, far):
    size = matrix.shape[0] // far
    place = lax.axis_index("z")
    arrays = [lax.dynamic_slice_in_dim(matrix, place * size, size)]
    for step in range(1, far):
        sent = lax.dynamic_slice_in_dim(matrix, ((place + step) % far) * size, size)
        arrays.append(lax.ppermute(sent, "z", [(i, (i + step) % far) for i in range(far)]))
    return arrays


def add_far(arrays, *follow):
    own, *got = arrays
    if follow:
        got = [after(array, *follow) for array in got]
    return sum(array.astype(jnp.float32) for array in [own, *got])


def column_sums(array):
    return jnp.sum(array.astype(jnp.float32), axis=0)


def by_image(far):
    def on_device(
        inputs,
        cotangent,
        segment,
        w_qkv,
        b_query,
        b_value,
        w_out,
        b_out,
        norm1_gain,
        norm1_shift,
        norm2_gain,
        norm2_shift,
        w_up,
        b_up,
        w_down,
        b_down,
    ):
        place, core = lax.axis_index("ctx"), lax.axis_index("core")
        swap = lambda array: trade(array, "ctx")
        slots, width = inputs.shape
        half_width = width // 2
        pads = 2 * slots - IMAGES * SEQ
        rows = round_up(SEQ + pads, 16)
        near_width = w_up.shape[0] // 8

        inputs_far = swap(inputs)
        segment_far = swap(segment)
        shard_rows = w_qkv.shape[0] // 8
        small = [b_query, b_value, b_out, norm1_gain, norm1_shift, norm2_gain, norm2_shift, b_down]
        small = jnp.concatenate([jnp.stack(small), b_up.reshape(-1, near_width)], axis=0)
        small_rows = small.shape[0]
        pad_small = lambda table: jnp.pad(
            table,
            [(0, 0)] * (table.ndim - 2)
            + [(0, shard_rows - small_rows), (0, 128 - near_width)],
        )
        small = pad_small(small)
        shard_qkv = unfold(w_qkv).reshape(shard_rows, 3, 2, half_width)
        halves = [shard_qkv[:, :, side].reshape(shard_rows, 3 * half_width) for side in range(2)]
        half_qkv = 3 * half_width
        far_one, far_two = gather_far(
            jnp.concatenate([halves[0], small, halves[1]], axis=1), far, [half_qkv + 128, half_qkv]
        )
        shard_up = jnp.concatenate(
            [to_local(unfold(w_out), 1, far), hidden_to_local(unfold(w_up), 1, far)], axis=1
        )
        up_width = w_up.shape[1] * 8
        up_cut = (width + up_width) // 2
        far_up = gather_far(after(shard_up, far_one), far, [up_cut, up_cut])
        far_one, far_two = after(far_one, inputs_far), after(far_two, inputs_far)
        one = spread(spread({OWN: far_one}, "x"), "ctx")
        two = spread(spread({OWN: far_two}, "ctx"), "x")
        all_one = list(one.values()) + list(two.values())
        shard_down = after(to_local(unfold(w_down), 1, far), far_up[0], *all_one)
        near_down = order_blocks(spread({OWN: shard_down}, "ctx"), ["ctx"])
        one_core, two_core = spread(one, "core"), spread(two, "core")
        axes = ["core", "x", "ctx"]
        routes = [[(0, half_qkv, 0, 0), (half_qkv, 128, 1, 0)]] * 8
        qkv_one, small_local = assemble(
            list(one_core.values()),
            places(one_core, axes),
            [(width, half_qkv), (width, 128)],
            routes,
        )
        qkv_two = order_blocks(two_core, axes)
        up_one = spread({OWN: after(far_up[0], *all_one)}, "x")
        up_two = spread({OWN: after(far_up[1], *all_one)}, "ctx")
        up_one = spread(tie_received(up_one, qkv_one), "ctx")
        up_two = spread(tie_received(up_two, qkv_one), "x")
        far_down = gather_far(near_down, far)[0]

        devices = 8 * far
        small_core = small_local.reshape(devices, shard_rows, 128)[:, :small_rows, :near_width]
        small_core = small_core.astype(jnp.float32)
        small_all = to_natural(small_core, 0, far)
        query_bias, value_bias = (small_all[:, index].reshape(-1) for index in range(2))
        out_bias, first_gain, first_shift, second_gain, second_shift, down_bias = (
            small_core[:, index].reshape(-1) for index in range(2, 8)
        )
        up_bias = hidden_to_local(small_all[:, 8:].reshape(-1), 0, far)

        slot = jnp.arange(slots)
        earlier = slot[:, None] < slot[None, :]

        def ranks(own, other, other_first):
            inside = jnp.sum((own[:, None] == own[None, :]) & earlier, axis=0)
            outside = jnp.sum(other[:, None] == own[None, :], axis=0)
            return inside + jnp.where(other_first, outside, 0)

        rank_near = ranks(segment, segment_far, place == 1)
        rank_far = ranks(segment_far, segment, place == 0)

        def positions(ids, rank, image):
            return jnp.where(ids == image, rank, jnp.where(ids < 0, SEQ + rank, -1))

        row = jnp.arange(rows)
        spot_near = positions(segment, rank_near, place)
        spot_far = positions(segment_far, rank_far, place)
        pick_near = (spot_near[None, :] == row[:, None]).astype(jnp.bfloat16)
        pick_far = (spot_far[None, :] == row[:, None]).astype(jnp.bfloat16)
        spot_other = jnp.where(segment == 1 - place, rank_near, -1)
        give_near = (spot_near[:, None] == row[None, :]).astype(jnp.bfloat16)
        give_far = (spot_other[:, None] == row[None, :]).astype(jnp.bfloat16)
        column = jnp.arange(width)
        to_core = (column[:, None] == to_local(column, 0, far)[None, :]).astype(jnp.bfloat16)

        def take(near, other):
            picked = matmul(pick_near, near) + matmul(pick_far, other)
            return matmul(picked.astype(jnp.bfloat16), to_core)

        def to_give(array):
            natural = nt_dot(array.astype(jnp.bfloat16), to_core).astype(jnp.bfloat16)
            return natural, swap(natural)

        def give(both, *follow):
            near, other = both
            other = after(other, *follow) if follow else other
            return matmul(give_near, near) + matmul(give_far, other)

        kind = (row >= SEQ).astype(jnp.int32) + (row >= SEQ + pads).astype(jnp.int32)
        bias = jnp.where(kind[:, None] == kind[None, :], 0.0, -1e30).astype(jnp.float32)

        values_in = take(inputs, inputs_far)
        normal1, scale1 = standardize(values_in)
        normed1 = (normal1 * first_gain + first_shift).astype(jnp.bfloat16)
        joined_bias = [
            jnp.concatenate(
                [query_bias[cut], jnp.zeros((half_width,), jnp.float32), value_bias[cut]]
            )
            for cut in (slice(0, half_width), slice(half_width, width))
        ]
        joined_one = project(normed1, qkv_one, joined_bias[0])
        attended, log_one = attention_forward(after(joined_one, near_down), bias, width, 0)
        joined_two = project(after(normed1, log_one), qkv_two, joined_bias[1])
        up_one, up_two = tie_received(up_one, log_one), tie_received(up_two, log_one)
        up_near = assemble(
            list(up_one.values()) + list(up_two.values()),
            places(up_one, ["x", "ctx"]) + places(up_two, ["x", "ctx"]),
            [(half_width, width + up_width)],
            [[(0, up_cut, 0, 0)]] * 4 + [[(0, up_cut, 0, up_cut)]] * 4,
        )[0]
        up_blocks = spread({OWN: up_near}, "core")
        attended, log_two = attention_forward(
            joined_two, bias, width, half_width // PAIR, attended
        )
        cotangent_far = swap(after(cotangent, up_near))
        down_blocks = spread({OWN: after(far_down, up_near)}, "x")
        out_rows, up_weight = assemble(
            list(up_blocks.values()),
            places(up_blocks, ["core"]),
            [(width, width), (width, up_width)],
            [[(0, width, 0, 0), (width, up_width, 1, 0)]] * 2,
        )
        out_weight = to_natural(out_rows, 0, far)
        middle = values_in + matmul(attended, out_weight) + out_bias
        normal2, scale2 = standardize(middle)
        normed2 = (normal2 * second_gain + second_shift).astype(jnp.bfloat16)
        active, slope = hidden_layer(normed2, up_weight, up_bias)

        live = (row < SEQ).astype(jnp.float32)[:, None]
        d_out = take(cotangent, cotangent_far) * live
        d_out_low = d_out.astype(jnp.bfloat16)
        down_core = trade(gradient(active, d_out_low, 1 - core), "core")
        down_blocks = {key: after(block, active) for key, block in down_blocks.items()}
        down_weight = order_blocks(spread(down_blocks, "core"), ["core", "x"])
        last = last_layer(active, down_weight, middle, down_bias)
        last_given = to_give(last)
        down_x = send_half(
            gradient(active, d_out_low, core, got=after(down_core, last_given[0])), "x"
        )
        d_hidden, up_sums = d_hidden_layer(after(d_out_low, down_x[0]), down_weight, slope)
        up_core = [
            trade(gradient(normed2, d_hidden, 1 - core, side, 2), "core") for side in range(2)
        ]
        d_normed2 = d_normed(d_hidden, up_weight)
        d_middle = d_out + norm_backward(d_normed2, normal2, scale2, second_gain)
        d_branch = d_middle.astype(jnp.bfloat16)
        up_kept = [
            gradient(normed2, d_hidden, core, side, 2, after(up_core[side], d_branch))
            for side in range(2)
        ]
        up_one = send_half(up_kept[0], "ctx", 2)
        up_two = send_half(up_kept[1], "x")
        d_branch = after(d_branch, up_one[0], up_two[0])
        grad_out = to_local(matmul(attended.T, d_branch).astype(jnp.bfloat16), 0, far)
        out_core = send_half(grad_out, "core")
        d_attended = matmul(d_branch, out_weight.T).astype(jnp.bfloat16)
        outputs = give(last_given, d_attended).astype(jnp.bfloat16)
        out_x = send_half(add_half(out_core, d_attended), "x")
        down_far = send_far(add_half(down_x, d_attended), far)
        d_attended = after(d_attended, out_x[0], down_far[0])
        d_one = attention_backward(joined_one, d_attended, 0, log_one, bias)
        one_core = trade(gradient(normed1, d_one, 1 - core), "core")
        partial = d_normed(d_one, qkv_one)
        up_one = send_half(add_half(up_one, partial), "x")
        up_two = send_half(add_half(up_two, partial), "ctx")
        out_y = send_half(add_half(out_x, partial), "ctx")
        d_attended = after(d_attended, partial, up_one[0], up_two[0], out_y[0])
        d_two = attention_backward(joined_two, d_attended, half_width // PAIR, log_two, bias)
        two_core = trade(gradient(normed1, d_two, 1 - core), "core")
        qkv_one_x = send_half(gradient(normed1, d_one, core, got=after(one_core, d_two)), "x")
        down_y = send_half(add_far(down_far, d_two).astype(jnp.bfloat16), "ctx")
        d_two_tied = after(d_two, qkv_one_x[0], down_y[0])
        d_normed1 = d_normed(d_two_tied, qkv_two, partial)
        d_last = d_middle + norm_backward(d_normed1, normal1, scale1, first_gain)
        d_last_given = to_give(d_last)
        qkv_two = gradient(normed1, d_two, core, got=after(two_core, d_last_given[0]))

        vectors = [
            column_sums(array)
            for array in (
                d_branch,
                d_normed1 * normal1,
                d_normed1,
                d_normed2 * normal2,
                d_normed2,
                d_out_low,
            )
        ]
        joined_vectors = [
            jnp.concatenate([column_sums(d_one[index]), column_sums(d_two[index])])
            for index in (0, 2)
        ]
        vectors = [to_local(vector, 0, far) for vector in joined_vectors] + vectors
        table = jnp.stack([vector.reshape(devices, near_width) for vector in vectors], axis=1)
        up_sums = to_local(hidden_to_natural(up_sums[0], 0, far), 0, far)
        table = jnp.concatenate([table, up_sums.reshape(devices, -1, near_width)], axis=1)
        table = pad_small(table).reshape(width, 128).astype(jnp.bfloat16)
        qkv_two_y = send_half(qkv_two, "ctx", 2)
        qkv_one_y = send_half(add_half(qkv_one_x, d_last_given[0]), "ctx")
        table = send_half(add_half(send_half(table, "core")), "ctx", 2)
        up_far = jnp.concatenate(
            [add_half(halves, qkv_two_y[0], qkv_one_y[0]) for halves in (up_one, up_two, out_y)],
            axis=1,
        )
        up_far = send_far(up_far, far)
        qkv_two = jnp.concatenate([add_half(qkv_two_y), add_half(table)], axis=1)
        qkv_two_x = send_half(qkv_two, "x")
        qkv_one_far = send_far(add_half(qkv_one_y), far)
        qkv_two_far = send_far(add_half(qkv_two_x), far)

        sum_down = add_half(down_y).astype(jnp.float32)
        sum_up = add_far(up_far)
        sum_up, sum_out = sum_up[:, :up_width], sum_up[:, up_width:]
        sum_one, sum_two = add_far(qkv_one_far), add_far(qkv_two_far)
        small_sums = sum_two[:small_rows, half_qkv : half_qkv + near_width]
        cut_qkv = lambda matrix: matrix[:, :half_qkv].reshape(shard_rows, 3, 1, half_width)
        sum_qkv = jnp.concatenate([cut_qkv(sum_one), cut_qkv(sum_two)], axis=2)
        sum_qkv = sum_qkv.reshape(shard_rows, 3 * width)
        input_grad = give(d_last_given)
        own = lambda index: small_sums[index]
        back = lambda matrix: refold(to_natural(matrix, 1, far))
        return (
            outputs,
            input_grad,
            refold(sum_qkv),
            own(0),
            own(1),
            back(sum_out),
            own(2),
            own(3),
            own(4),
            own(5),
            own(6),
            refold(hidden_to_natural(sum_up, 1, far)),
            small_sums[8:].reshape(-1),
            back(sum_down),
            own(7),
        )

    return on_device


def solution(mesh):
    if mesh.shape["ctx"] == IMAGES and mesh.shape["dp"] % 4 == 0:
        far, axes = mesh.shape["dp"] // 4, ("z", "x", "core", "ctx")
        mesh = jax.sharding.Mesh(mesh.devices.reshape(far, 2, 2, IMAGES), axes)
        body = by_image(far)
    else:
        body, axes = on_device, ("dp", "ctx")
    matrix, vector = P(axes, None), P(axes)
    return jax.shard_map(
        body,
        mesh=mesh,
        in_specs=(matrix, matrix, vector, matrix, vector, vector, matrix)
        + (vector,) * 5
        + (matrix, vector, matrix, vector),
        out_specs=(matrix, matrix, matrix, vector, vector, matrix)
        + (vector,) * 5
        + (matrix, vector, matrix, vector),
        check_vma=False,
    )
```

```python
import functools
import math

import jax
import jax.numpy as jnp
from jax import lax
from jax.experimental import pallas as pl
from jax.experimental.pallas import tpu as pltpu
from jax.sharding import PartitionSpec as P

HD = 64


EPSILON = 1e-06


def layer_norm(value, gain, shift):
    center = value - jnp.mean(value, axis=-1, keepdims=True)
    variance = jnp.mean(center * center, axis=-1, keepdims=True)
    return center * lax.rsqrt(variance + EPSILON) * gain + shift


def gelu_exact(value):
    return jax.nn.gelu(value, approximate=False)


def matmul(left, right):
    return jnp.dot(left, right, preferred_element_type=jnp.float32)


def unfold(stored):
    return stored.reshape(stored.shape[0] // 8, stored.shape[1] * 8)


def refold(matrix):
    return matrix.reshape(matrix.shape[0] * 8, matrix.shape[1] // 8)


def on_device(
    inputs,
    cotangent,
    segment,
    w_qkv,
    b_query,
    b_value,
    w_out,
    b_out,
    norm1_gain,
    norm1_shift,
    norm2_gain,
    norm2_shift,
    w_up,
    b_up,
    w_down,
    b_down,
):
    gathered = (
        lax.all_gather(w_qkv, ("dp", "ctx"), axis=0, tiled=True),
        lax.all_gather(b_query, ("dp", "ctx"), axis=0, tiled=True),
        lax.all_gather(b_value, ("dp", "ctx"), axis=0, tiled=True),
        lax.all_gather(w_out, ("dp", "ctx"), axis=0, tiled=True),
        lax.all_gather(b_out, ("dp", "ctx"), axis=0, tiled=True),
        lax.all_gather(norm1_gain, ("dp", "ctx"), axis=0, tiled=True),
        lax.all_gather(norm1_shift, ("dp", "ctx"), axis=0, tiled=True),
        lax.all_gather(norm2_gain, ("dp", "ctx"), axis=0, tiled=True),
        lax.all_gather(norm2_shift, ("dp", "ctx"), axis=0, tiled=True),
        lax.all_gather(w_up, ("dp", "ctx"), axis=0, tiled=True),
        lax.all_gather(b_up, ("dp", "ctx"), axis=0, tiled=True),
        lax.all_gather(w_down, ("dp", "ctx"), axis=0, tiled=True),
        lax.all_gather(b_down, ("dp", "ctx"), axis=0, tiled=True),
    )
    (
        qkv_stored,
        query_bias,
        value_bias,
        out_stored,
        out_bias,
        gain_one,
        shift_one,
        gain_two,
        shift_two,
        up_stored,
        up_bias,
        down_stored,
        down_bias,
    ) = gathered
    qkv_weight = unfold(qkv_stored)
    out_weight = unfold(out_stored)
    up_weight = unfold(up_stored)
    down_weight = unfold(down_stored)
    first_gain = gain_one.astype(jnp.float32)
    first_shift = shift_one.astype(jnp.float32)
    second_gain = gain_two.astype(jnp.float32)
    second_shift = shift_two.astype(jnp.float32)
    row_count = inputs.shape[0]
    model_width = out_weight.shape[0]
    head_count = model_width // HD
    score_scale = 1.0 / math.sqrt(HD)
    values_in = inputs.astype(jnp.float32)
    normed1 = layer_norm(values_in, first_gain, first_shift).astype(jnp.bfloat16)
    joined = matmul(normed1, qkv_weight)
    queries = (joined[:, :model_width] + query_bias.astype(jnp.float32)).astype(jnp.bfloat16)
    key_rows = joined[:, model_width : 2 * model_width].astype(jnp.bfloat16)
    value_rows = (joined[:, 2 * model_width :] + value_bias.astype(jnp.float32)).astype(
        jnp.bfloat16
    )
    key_all, value_all, seg_all = (
        lax.all_gather(key_rows, "ctx", axis=0, tiled=True),
        lax.all_gather(value_rows, "ctx", axis=0, tiled=True),
        lax.all_gather(segment.astype(jnp.bfloat16), "ctx", axis=0, tiled=True),
    )
    key_count = key_all.shape[0]
    query_heads = queries.reshape(row_count, head_count, HD)
    key_heads = key_all.reshape(key_count, head_count, HD)
    value_heads = value_all.reshape(key_count, head_count, HD)
    own_seg = segment.astype(jnp.float32)
    group_seg = seg_all.astype(jnp.float32)
    same_seg = own_seg[:, None] == group_seg[None, :]

    def make_scores():
        raw = (
            jnp.einsum("qhd,khd->hqk", query_heads, key_heads, preferred_element_type=jnp.float32)
            * score_scale
        )
        return jnp.where(same_seg[None], raw, -1e30)

    scores = make_scores()
    row_max = jnp.max(scores, axis=-1, keepdims=True)
    expo = jnp.exp(scores - row_max)
    row_total = jnp.sum(expo, axis=-1, keepdims=True)
    probs_low = (expo / row_total).astype(jnp.bfloat16)
    log_total = row_max + jnp.log(row_total)
    mixed = jnp.einsum("hqk,khd->qhd", probs_low, value_heads, preferred_element_type=jnp.float32)
    attended = mixed.reshape(row_count, model_width).astype(jnp.bfloat16)
    middle = values_in + matmul(attended, out_weight) + out_bias.astype(jnp.float32)
    normed2 = layer_norm(middle, second_gain, second_shift).astype(jnp.bfloat16)
    hidden = matmul(normed2, up_weight) + up_bias.astype(jnp.float32)
    active = gelu_exact(hidden).astype(jnp.bfloat16)
    outputs = (middle + matmul(active, down_weight) + down_bias.astype(jnp.float32)).astype(
        jnp.bfloat16
    )
    back_qkv, back_out, back_up, back_down = (qkv_weight, out_weight, up_weight, down_weight)
    valid = (segment >= 0).astype(jnp.float32)[:, None]
    d_out = cotangent.astype(jnp.float32) * valid
    d_out_low = d_out.astype(jnp.bfloat16)
    grad_down = refold(matmul(active.T, d_out_low))
    grad_down_bias = jnp.sum(d_out_low.astype(jnp.float32), axis=0)
    d_active = matmul(d_out_low, back_down.T)
    gelu_value, gelu_pull = jax.vjp(gelu_exact, hidden)
    d_hidden = gelu_pull(d_active)[0].astype(jnp.bfloat16)
    grad_up = refold(matmul(normed2.T, d_hidden))
    grad_up_bias = jnp.sum(d_hidden.astype(jnp.float32), axis=0)
    d_normed2 = matmul(d_hidden, back_up.T)
    norm_value, norm_pull = jax.vjp(layer_norm, middle, second_gain, second_shift)
    d_middle_norm, grad_gain_two, grad_shift_two = norm_pull(d_normed2)
    d_middle = d_out + d_middle_norm
    d_branch = d_middle.astype(jnp.bfloat16)
    grad_out = refold(matmul(attended.T, d_branch))
    grad_out_bias = jnp.sum(d_branch.astype(jnp.float32), axis=0)
    d_attended_flat = matmul(d_branch, back_out.T).astype(jnp.bfloat16)
    d_attended = d_attended_flat.reshape(row_count, head_count, HD)
    scores = make_scores()
    probs = jnp.exp(scores - log_total)
    d_probs = jnp.einsum(
        "qhd,khd->hqk", d_attended, value_heads, preferred_element_type=jnp.float32
    )
    delta_rows = jnp.sum(probs * d_probs, axis=-1, keepdims=True)
    d_scores = (probs * (d_probs - delta_rows)).astype(jnp.bfloat16)
    d_query = (
        jnp.einsum("hqk,khd->qhd", d_scores, key_heads, preferred_element_type=jnp.float32)
        * score_scale
    ).reshape(row_count, model_width)
    probs_again = probs.astype(jnp.bfloat16)
    d_key_all = (
        jnp.einsum("hqk,qhd->khd", d_scores, query_heads, preferred_element_type=jnp.float32)
        * score_scale
    ).reshape(key_count, model_width)
    d_value_all = jnp.einsum(
        "hqk,qhd->khd", probs_again, d_attended, preferred_element_type=jnp.float32
    ).reshape(key_count, model_width)
    d_key, d_value = (
        lax.psum_scatter(
            d_key_all.astype(jnp.bfloat16), "ctx", scatter_dimension=0, tiled=True
        ).astype(jnp.float32),
        lax.psum_scatter(
            d_value_all.astype(jnp.bfloat16), "ctx", scatter_dimension=0, tiled=True
        ).astype(jnp.float32),
    )
    d_query_low = d_query.astype(jnp.bfloat16)
    d_value_low = d_value.astype(jnp.bfloat16)
    d_joined = jnp.concatenate([d_query_low, d_key.astype(jnp.bfloat16), d_value_low], axis=1)
    grad_qkv = refold(matmul(normed1.T, d_joined))
    grad_query_bias = jnp.sum(d_query_low.astype(jnp.float32), axis=0)
    grad_value_bias = jnp.sum(d_value_low.astype(jnp.float32), axis=0)
    d_normed1 = matmul(d_joined, back_qkv.T)
    first_value, first_pull = jax.vjp(layer_norm, values_in, first_gain, first_shift)
    d_input_norm, grad_gain_one, grad_shift_one = first_pull(d_normed1)
    input_grad = d_middle + d_input_norm
    partial_sums = (
        lax.psum_scatter(
            grad_qkv.astype(jnp.bfloat16), "dp", scatter_dimension=0, tiled=True
        ).astype(jnp.float32),
        lax.psum_scatter(
            grad_query_bias.astype(jnp.bfloat16), "dp", scatter_dimension=0, tiled=True
        ).astype(jnp.float32),
        lax.psum_scatter(
            grad_value_bias.astype(jnp.bfloat16), "dp", scatter_dimension=0, tiled=True
        ).astype(jnp.float32),
        lax.psum_scatter(
            grad_out.astype(jnp.bfloat16), "dp", scatter_dimension=0, tiled=True
        ).astype(jnp.float32),
        lax.psum_scatter(
            grad_out_bias.astype(jnp.bfloat16), "dp", scatter_dimension=0, tiled=True
        ).astype(jnp.float32),
        lax.psum_scatter(
            grad_gain_one.astype(jnp.bfloat16), "dp", scatter_dimension=0, tiled=True
        ).astype(jnp.float32),
        lax.psum_scatter(
            grad_shift_one.astype(jnp.bfloat16), "dp", scatter_dimension=0, tiled=True
        ).astype(jnp.float32),
        lax.psum_scatter(
            grad_gain_two.astype(jnp.bfloat16), "dp", scatter_dimension=0, tiled=True
        ).astype(jnp.float32),
        lax.psum_scatter(
            grad_shift_two.astype(jnp.bfloat16), "dp", scatter_dimension=0, tiled=True
        ).astype(jnp.float32),
        lax.psum_scatter(
            grad_up.astype(jnp.bfloat16), "dp", scatter_dimension=0, tiled=True
        ).astype(jnp.float32),
        lax.psum_scatter(
            grad_up_bias.astype(jnp.bfloat16), "dp", scatter_dimension=0, tiled=True
        ).astype(jnp.float32),
        lax.psum_scatter(
            grad_down.astype(jnp.bfloat16), "dp", scatter_dimension=0, tiled=True
        ).astype(jnp.float32),
        lax.psum_scatter(
            grad_down_bias.astype(jnp.bfloat16), "dp", scatter_dimension=0, tiled=True
        ).astype(jnp.float32),
    )
    all_sums = (
        lax.psum_scatter(
            partial_sums[0].astype(jnp.bfloat16), "ctx", scatter_dimension=0, tiled=True
        ).astype(jnp.float32),
        lax.psum_scatter(
            partial_sums[1].astype(jnp.bfloat16), "ctx", scatter_dimension=0, tiled=True
        ).astype(jnp.float32),
        lax.psum_scatter(
            partial_sums[2].astype(jnp.bfloat16), "ctx", scatter_dimension=0, tiled=True
        ).astype(jnp.float32),
        lax.psum_scatter(
            partial_sums[3].astype(jnp.bfloat16), "ctx", scatter_dimension=0, tiled=True
        ).astype(jnp.float32),
        lax.psum_scatter(
            partial_sums[4].astype(jnp.bfloat16), "ctx", scatter_dimension=0, tiled=True
        ).astype(jnp.float32),
        lax.psum_scatter(
            partial_sums[5].astype(jnp.bfloat16), "ctx", scatter_dimension=0, tiled=True
        ).astype(jnp.float32),
        lax.psum_scatter(
            partial_sums[6].astype(jnp.bfloat16), "ctx", scatter_dimension=0, tiled=True
        ).astype(jnp.float32),
        lax.psum_scatter(
            partial_sums[7].astype(jnp.bfloat16), "ctx", scatter_dimension=0, tiled=True
        ).astype(jnp.float32),
        lax.psum_scatter(
            partial_sums[8].astype(jnp.bfloat16), "ctx", scatter_dimension=0, tiled=True
        ).astype(jnp.float32),
        lax.psum_scatter(
            partial_sums[9].astype(jnp.bfloat16), "ctx", scatter_dimension=0, tiled=True
        ).astype(jnp.float32),
        lax.psum_scatter(
            partial_sums[10].astype(jnp.bfloat16), "ctx", scatter_dimension=0, tiled=True
        ).astype(jnp.float32),
        lax.psum_scatter(
            partial_sums[11].astype(jnp.bfloat16), "ctx", scatter_dimension=0, tiled=True
        ).astype(jnp.float32),
        lax.psum_scatter(
            partial_sums[12].astype(jnp.bfloat16), "ctx", scatter_dimension=0, tiled=True
        ).astype(jnp.float32),
    )
    (
        sum_qkv,
        sum_query_bias,
        sum_value_bias,
        sum_out,
        sum_out_bias,
        sum_gain_one,
        sum_shift_one,
        sum_gain_two,
        sum_shift_two,
        sum_up,
        sum_up_bias,
        sum_down,
        sum_down_bias,
    ) = all_sums
    return (
        outputs,
        input_grad,
        sum_qkv,
        sum_query_bias,
        sum_value_bias,
        sum_out,
        sum_out_bias,
        sum_gain_one,
        sum_shift_one,
        sum_gain_two,
        sum_shift_two,
        sum_up,
        sum_up_bias,
        sum_down,
        sum_down_bias,
    )


SEQ = 577
IMAGES = 2
PAIR = 2 * HD
CHUNK = 256
BLOCK = 512
HINT = pl.CostEstimate(flops=1, bytes_accessed=1, transcendentals=0)
ERFC = (
    0.09873409569263458,
    0.09871950000524521,
    0.09271052479743958,
    0.08134904503822327,
    0.056456614285707474,
    0.07422702759504318,
    -0.050631966441869736,
    0.11820460855960846,
    -0.09110676497220993,
    0.021337319165468216,
)
ERFC_STEP = 0.35


def round_up(count, unit):
    return -(-count // unit) * unit


def limit(mebibytes):
    return pltpu.CompilerParams(vmem_limit_bytes=mebibytes * 2**20)


def chunks_of(count):
    return [(start, min(CHUNK, count - start)) for start in range(0, count, CHUNK)]


def nt_dot(left, right):
    return lax.dot_general(
        left, right, (((1,), (1,)), ((), ())), preferred_element_type=jnp.float32
    )


def tn_dot(left, right):
    return lax.dot_general(
        left, right, (((0,), (0,)), ((), ())), preferred_element_type=jnp.float32
    )


def half_mask(rows):
    return lax.broadcasted_iota(jnp.int32, (rows, PAIR), 1) < HD


def forward_kernel(query_ref, key_ref, value_ref, bias_ref, *refs):
    attended_ref, log_ref = refs[-2:]
    rows = query_ref.shape[1]
    first = half_mask(rows)
    zero = jnp.zeros((rows, PAIR), jnp.bfloat16)
    key = key_ref[0]
    key_sides = (jnp.where(first, key, zero), jnp.where(first, zero, key))
    value_t = value_ref[0].astype(jnp.float32).T.astype(jnp.bfloat16)
    scale = jnp.bfloat16(1.0 / math.sqrt(HD))
    for start, size in chunks_of(rows):
        query = query_ref[0, start : start + size, :] * scale
        bias = bias_ref[:, start : start + size]
        outs = []
        for side in range(2):
            scores = nt_dot(key_sides[side], query) + bias
            top = jnp.max(scores, axis=0, keepdims=True)
            expo = jnp.exp(scores - top)
            total = jnp.sum(expo, axis=0, keepdims=True)
            probs_low = (expo * (1.0 / total)).astype(jnp.bfloat16)
            outs.append(matmul(value_t[side * HD : (side + 1) * HD, :], probs_low))
            log_ref[0, side : side + 1, start : start + size] = top + jnp.log(total)
        mixed = jnp.concatenate(outs, axis=0)
        attended_ref[start : start + size, :] = mixed.T.astype(jnp.bfloat16)


def backward_kernel(
    query_ref, key_ref, value_ref, d_ref, log_ref, bias_ref, joined_ref, dk_sum, dv_sum
):
    rows = query_ref.shape[1]
    first = half_mask(rows)
    zero = jnp.zeros((rows, PAIR), jnp.bfloat16)
    key = key_ref[0]
    value = value_ref[0]
    key_sides = (jnp.where(first, key, zero), jnp.where(first, zero, key))
    value_sides = (jnp.where(first, value, zero), jnp.where(first, zero, value))
    key_t = key.astype(jnp.float32).T.astype(jnp.bfloat16)
    scale = jnp.bfloat16(1.0 / math.sqrt(HD))
    for start, size in chunks_of(rows):
        query = query_ref[0, start : start + size, :] * scale
        d_rows = d_ref[start : start + size, :]
        bias = bias_ref[:, start : start + size]
        outs = []
        for side in range(2):
            scores = nt_dot(key_sides[side], query) + bias
            probs = jnp.exp(scores - log_ref[0, side : side + 1, start : start + size])
            d_probs = nt_dot(value_sides[side], d_rows)
            product = probs * d_probs
            delta = jnp.sum(product, axis=0, keepdims=True)
            d_scores = (product - probs * delta).astype(jnp.bfloat16)
            d_value = matmul(probs.astype(jnp.bfloat16), d_rows)
            d_key = matmul(d_scores, query)
            if start == 0:
                dv_sum[side] = d_value
                dk_sum[side] = d_key
            else:
                dv_sum[side] += d_value
                dk_sum[side] += d_key
            outs.append(matmul(key_t[side * HD : (side + 1) * HD, :], d_scores))
        d_query = jnp.concatenate(outs, axis=0) * (1.0 / math.sqrt(HD))
        joined_ref[0, start : start + size, :] = d_query.T.astype(jnp.bfloat16)
    joined_ref[1] = jnp.where(first, dk_sum[0], dk_sum[1]).astype(jnp.bfloat16)
    joined_ref[2] = jnp.where(first, dv_sum[0], dv_sum[1]).astype(jnp.bfloat16)


def pair_spec(rows, part):
    return pl.BlockSpec((1, rows, PAIR), lambda i: (part, 0, i))


def attention_forward(joined, bias, total, first_pair, base=None):
    rows, width = joined.shape[1:]
    pairs = width // PAIR
    extra = [] if base is None else [base]
    return pl.pallas_call(
        forward_kernel,
        grid=(pairs,),
        in_specs=[pair_spec(rows, part) for part in range(3)]
        + [pl.BlockSpec((rows, rows), lambda i: (0, 0))]
        + [pl.BlockSpec(memory_space=pl.ANY) for _ in extra],
        out_specs=[
            pl.BlockSpec((rows, PAIR), lambda i: (0, first_pair + i)),
            pl.BlockSpec((1, 2, rows), lambda i: (i, 0, 0)),
        ],
        out_shape=[
            jax.ShapeDtypeStruct((rows, total), jnp.bfloat16),
            jax.ShapeDtypeStruct((pairs, 2, rows), jnp.float32),
        ],
        input_output_aliases={4: 0} if extra else {},
        compiler_params=limit(32),
        cost_estimate=HINT,
        name="attention_forward",
    )(joined, joined, joined, bias, *extra)


def attention_backward(joined, d_attended, first_pair, log_total, bias):
    rows, width = joined.shape[1:]
    return pl.pallas_call(
        backward_kernel,
        grid=(width // PAIR,),
        in_specs=[pair_spec(rows, part) for part in range(3)]
        + [
            pl.BlockSpec((rows, PAIR), lambda i: (0, first_pair + i)),
            pl.BlockSpec((1, 2, rows), lambda i: (i, 0, 0)),
            pl.BlockSpec((rows, rows), lambda i: (0, 0)),
        ],
        out_specs=pl.BlockSpec((3, rows, PAIR), lambda i: (0, 0, i)),
        out_shape=jax.ShapeDtypeStruct((3, rows, width), jnp.bfloat16),
        scratch_shapes=[pltpu.VMEM((2, rows, PAIR), jnp.float32)] * 2,
        compiler_params=limit(32),
        cost_estimate=HINT,
        name="attention_backward",
    )(joined, joined, joined, d_attended, log_total, bias)


def whole_spec(shape):
    return pl.BlockSpec(shape, lambda *_: (0,) * len(shape))


def project_kernel(x_ref, weight_ref, bias_ref, out_ref):
    out_ref[0] = (matmul(x_ref[...], weight_ref[...]) + bias_ref[...]).astype(out_ref.dtype)


def project(x, weight, bias):
    rows, depth = x.shape
    width = weight.shape[1] // 3
    return pl.pallas_call(
        project_kernel,
        grid=(3,),
        in_specs=[
            whole_spec(x.shape),
            pl.BlockSpec((depth, width), lambda i: (0, i)),
            pl.BlockSpec((1, width), lambda i: (0, i)),
        ],
        out_specs=pl.BlockSpec((1, rows, width), lambda i: (i, 0, 0)),
        out_shape=jax.ShapeDtypeStruct((3, rows, width), jnp.bfloat16),
        compiler_params=limit(24),
        cost_estimate=HINT,
        name="project",
    )(x, weight, bias[None, :])


def hidden_kernel(x_ref, weight_ref, bias_ref, active_ref, slope_ref):
    hidden = matmul(x_ref[...], weight_ref[...]) + bias_ref[...]
    share = 1.0 / (1.0 + (ERFC_STEP * math.sqrt(0.5)) * jnp.abs(hidden))
    density = jnp.exp(-0.5 * hidden * hidden)
    tail = jnp.full_like(share, ERFC[-1])
    for factor in ERFC[-2::-1]:
        tail = tail * share + factor
    tail = tail * share * density
    phi = jnp.where(hidden < 0.0, tail, 1.0 - tail)
    active_ref[...] = (hidden * phi).astype(jnp.bfloat16)
    slope = phi + hidden * density * (1.0 / math.sqrt(2.0 * math.pi))
    slope_ref[...] = slope.astype(jnp.bfloat16)


def hidden_layer(x, weight, bias):
    rows, depth = x.shape
    width = weight.shape[1]
    block = pl.BlockSpec((rows, BLOCK), lambda i: (0, i))
    return pl.pallas_call(
        hidden_kernel,
        grid=(width // BLOCK,),
        in_specs=[
            whole_spec(x.shape),
            pl.BlockSpec((depth, BLOCK), lambda i: (0, i)),
            pl.BlockSpec((1, BLOCK), lambda i: (0, i)),
        ],
        out_specs=[block, block],
        out_shape=[jax.ShapeDtypeStruct((rows, width), jnp.bfloat16)] * 2,
        compiler_params=limit(32),
        cost_estimate=HINT,
        name="hidden_layer",
    )(x, weight, bias[None, :])


def last_kernel(active_ref, weight_ref, middle_ref, bias_ref, out_ref, total):
    step = pl.program_id(0)

    @pl.when(step == 0)
    def _():
        total[...] = middle_ref[...] + bias_ref[...]

    total[...] += matmul(active_ref[...], weight_ref[...])

    @pl.when(step == pl.num_programs(0) - 1)
    def _():
        out_ref[...] = total[...].astype(out_ref.dtype)


def last_layer(active, weight, middle, bias):
    rows, depth = active.shape
    width = weight.shape[1]
    return pl.pallas_call(
        last_kernel,
        grid=(depth // BLOCK,),
        in_specs=[
            pl.BlockSpec((rows, BLOCK), lambda i: (0, i)),
            pl.BlockSpec((BLOCK, width), lambda i: (i, 0)),
            whole_spec((rows, width)),
            whole_spec((1, width)),
        ],
        out_specs=whole_spec((rows, width)),
        out_shape=jax.ShapeDtypeStruct((rows, width), jnp.bfloat16),
        scratch_shapes=[pltpu.VMEM((rows, width), jnp.float32)],
        compiler_params=limit(52),
        cost_estimate=HINT,
        name="last_layer",
    )(active, weight, middle, bias[None, :])


def d_hidden_kernel(d_ref, weight_ref, slope_ref, out_ref, sum_ref):
    d_active = nt_dot(d_ref[...], weight_ref[...])
    d_hidden = (d_active * slope_ref[...].astype(jnp.float32)).astype(jnp.bfloat16)
    out_ref[...] = d_hidden
    sum_ref[...] = jnp.sum(d_hidden.astype(jnp.float32), axis=0, keepdims=True)


def d_hidden_layer(d_out, weight, slope):
    rows, depth = d_out.shape
    width = weight.shape[0]
    block = pl.BlockSpec((rows, BLOCK), lambda i: (0, i))
    return pl.pallas_call(
        d_hidden_kernel,
        grid=(width // BLOCK,),
        in_specs=[
            whole_spec(d_out.shape),
            pl.BlockSpec((BLOCK, depth), lambda i: (i, 0)),
            block,
        ],
        out_specs=[block, pl.BlockSpec((1, BLOCK), lambda i: (0, i))],
        out_shape=[
            jax.ShapeDtypeStruct((rows, width), jnp.bfloat16),
            jax.ShapeDtypeStruct((1, width), jnp.float32),
        ],
        compiler_params=limit(24),
        cost_estimate=HINT,
        name="d_hidden_layer",
    )(d_out, weight, slope)


def d_normed_kernel(d_ref, weight_ref, *refs):
    out_ref = refs[-1]
    d_rows = d_ref[0] if len(d_ref.shape) == 3 else d_ref[...]
    product = nt_dot(d_rows, weight_ref[...])
    step = pl.program_id(0)

    @pl.when(step == 0)
    def _():
        out_ref[...] = product + refs[0][...] if len(refs) == 2 else product

    @pl.when(step > 0)
    def _():
        out_ref[...] += product


def d_normed(d_rows, weight, base=None):
    rows, depth = d_rows.shape[-2], weight.shape[0]
    if d_rows.ndim == 3:
        d_spec = pl.BlockSpec((1, rows, BLOCK), lambda i: (i, 0, 0))
    else:
        d_spec = pl.BlockSpec((rows, BLOCK), lambda i: (0, i))
    extra = [] if base is None else [base]
    return pl.pallas_call(
        d_normed_kernel,
        grid=(weight.shape[1] // BLOCK,),
        in_specs=[d_spec, pl.BlockSpec((depth, BLOCK), lambda i: (0, i))]
        + [whole_spec((rows, depth)) for _ in extra],
        out_specs=whole_spec((rows, depth)),
        out_shape=jax.ShapeDtypeStruct((rows, depth), jnp.float32),
        compiler_params=limit(24),
        cost_estimate=HINT,
        name="d_normed",
    )(d_rows, weight, *extra)


def norm_back_kernel(count, d_ref, weight_ref, *refs):
    base, (normal_ref, scale_ref, gain_ref, residual_ref) = refs[:count], refs[count : count + 4]
    *wide_refs, low_ref, sum_ref, total = refs[count + 4 :]
    d_rows = d_ref[0] if len(d_ref.shape) == 3 else d_ref[...]
    product = nt_dot(d_rows, weight_ref[...])
    step = pl.program_id(0)

    @pl.when(step == 0)
    def _():
        total[...] = product + base[0][...] if base else product

    @pl.when(step > 0)
    def _():
        total[...] += product

    @pl.when(step == pl.num_programs(0) - 1)
    def _():
        rows = total.shape[0]
        sums = [jnp.zeros((1, total.shape[1]), jnp.float32)] * 3
        for start, size in chunks_of(rows):
            part = slice(start, start + size)
            d_part, normal = total[part, :], normal_ref[part, :]
            along = d_part * normal
            scaled = d_part * gain_ref[...]
            mean = jnp.mean(scaled, axis=-1, keepdims=True)
            slope = jnp.mean(scaled * normal, axis=-1, keepdims=True)
            wide = (scaled - mean - normal * slope) * scale_ref[part, :]
            wide = wide + residual_ref[part, :].astype(jnp.float32)
            low = wide.astype(jnp.bfloat16)
            for wide_ref in wide_refs:
                wide_ref[part, :] = wide
            low_ref[part, :] = low
            for number, array in enumerate((along, d_part, low.astype(jnp.float32))):
                sums[number] = sums[number] + jnp.sum(array, axis=0, keepdims=True)
        for number, one in enumerate(sums):
            sum_ref[number : number + 1, :] = one


def norm_back(d_rows, weight, normal, scale, gain, residual, base=None, keep=False):
    rows, depth = d_rows.shape[-2], weight.shape[0]
    if d_rows.ndim == 3:
        d_spec = pl.BlockSpec((1, rows, BLOCK), lambda i: (i, 0, 0))
    else:
        d_spec = pl.BlockSpec((rows, BLOCK), lambda i: (0, i))
    extra = [] if base is None else [base]
    full = whole_spec((rows, depth))
    kinds = [jnp.float32] * keep + [jnp.bfloat16]
    return pl.pallas_call(
        functools.partial(norm_back_kernel, len(extra)),
        grid=(weight.shape[1] // BLOCK,),
        in_specs=[d_spec, pl.BlockSpec((depth, BLOCK), lambda i: (0, i))]
        + [full for _ in extra]
        + [full, whole_spec((rows, 1)), whole_spec((1, depth)), full],
        out_specs=[full for _ in kinds] + [whole_spec((8, depth))],
        out_shape=[jax.ShapeDtypeStruct((rows, depth), kind) for kind in kinds]
        + [jax.ShapeDtypeStruct((8, depth), jnp.float32)],
        scratch_shapes=[pltpu.VMEM((rows, depth), jnp.float32)],
        compiler_params=limit(40),
        cost_estimate=HINT,
        name="norm_back",
    )(d_rows, weight, *extra, normal, scale, gain[None, :], residual)


def gradient_kernel(index_ref, x_ref, d_ref, *refs):
    out_ref = refs[-1]
    x = x_ref[...]
    width = d_ref.shape[-1]
    for part in range(out_ref.shape[1] // width):
        columns = slice(part * width, (part + 1) * width)
        product = tn_dot(x, d_ref[part] if len(d_ref.shape) == 3 else d_ref[...])
        if len(refs) == 2:
            product = product + refs[0][:, columns].astype(jnp.float32)
        out_ref[:, columns] = product.astype(out_ref.dtype)


def gradient(x, d_rows, half, column=0, columns=1, got=None):
    rows, depth = x.shape
    size = depth // 2
    blocks = size // CHUNK
    if d_rows.ndim == 3:
        d_spec = pl.BlockSpec(d_rows.shape, lambda i, index: (0, 0, 0))
        width = d_rows.shape[0] * d_rows.shape[2]
    else:
        width = d_rows.shape[1] // columns
        d_spec = pl.BlockSpec((rows, width), lambda i, index: (0, column))
    block = pl.BlockSpec((CHUNK, width), lambda i, index: (i, 0))
    extra = [] if got is None else [got]
    return pl.pallas_call(
        gradient_kernel,
        grid_spec=pltpu.PrefetchScalarGridSpec(
            num_scalar_prefetch=1,
            grid=(blocks,),
            in_specs=[
                pl.BlockSpec((rows, CHUNK), lambda i, index: (0, index[0] * blocks + i)),
                d_spec,
            ]
            + [block for _ in extra],
            out_specs=block,
        ),
        out_shape=jax.ShapeDtypeStruct((size, width), jnp.bfloat16),
        compiler_params=limit(32),
        cost_estimate=HINT,
        name="gradient",
    )(half.reshape(1).astype(jnp.int32), x, d_rows, *extra)


def standardize(value):
    center = value - jnp.mean(value, axis=-1, keepdims=True)
    variance = jnp.mean(center * center, axis=-1, keepdims=True)
    scale = lax.rsqrt(variance + EPSILON)
    return center * scale, scale


def reorder(array, axis, sizes, spots):
    shape = array.shape
    count = math.prod(sizes)
    cut = shape[:axis] + tuple(sizes) + (shape[axis] // count,) + shape[axis + 1 :]
    spots = list(range(axis)) + [axis + spot for spot in spots]
    return array.reshape(cut).transpose(spots + list(range(len(spots), len(cut)))).reshape(shape)


def to_local(array, axis, far):
    return reorder(array, axis, (far, 2, 2, 2), (2, 1, 3, 0))


def to_natural(array, axis, far):
    return reorder(array, axis, (2, 2, 2, far), (3, 1, 0, 2))


def hidden_to_local(array, axis, far):
    return reorder(array, axis, (far, 2, 2, 2), (2, 1, 0, 3))


def hidden_to_natural(array, axis, far):
    return reorder(array, axis, (2, 2, far, 2), (2, 1, 0, 3))


def assemble_kernel(routes, index_ref, *refs):
    count = len(routes)
    pieces, stages = refs[:count], refs[-count - 2 : -2]
    wholes, (arrived, left) = refs[count : -count - 2], refs[-2:]
    incoming = [
        pltpu.make_async_copy(piece, stage, arrived.at[number])
        for number, (piece, stage) in enumerate(zip(pieces, stages))
    ]
    for copy in incoming:
        copy.start()
    outgoing = []
    for number, route in enumerate(routes):
        incoming[number].wait()
        size = pieces[number].shape[0]
        start = pl.multiple_of(index_ref[number] * size, 16)
        for part, (source, width, whole, target) in enumerate(route):
            copy = pltpu.make_async_copy(
                stages[number].at[:, pl.ds(source, width)],
                wholes[whole].at[pl.ds(start, size), pl.ds(target, width)],
                left.at[part, number],
            )
            copy.start()
            outgoing.append(copy)
    for copy in outgoing:
        copy.wait()


def assemble(pieces, indices, outs, routes=None):
    if routes is None:
        routes = [[(0, piece.shape[1], 0, 0)] for piece in pieces]
    count = len(pieces)
    anywhere = pl.BlockSpec(memory_space=pl.ANY)
    kind = pieces[0].dtype
    return pl.pallas_call(
        functools.partial(assemble_kernel, routes),
        in_specs=[pl.BlockSpec(memory_space=pltpu.SMEM)] + [anywhere] * count,
        out_specs=[anywhere] * len(outs),
        out_shape=[jax.ShapeDtypeStruct(shape, kind) for shape in outs],
        scratch_shapes=[pltpu.VMEM(piece.shape, kind) for piece in pieces]
        + [
            pltpu.SemaphoreType.DMA((count,)),
            pltpu.SemaphoreType.DMA((max(len(route) for route in routes), count)),
        ],
        compiler_params=limit(16),
        cost_estimate=HINT,
        name="assemble",
    )(jnp.stack(indices).astype(jnp.int32), *pieces)


def trade(array, axis):
    return lax.ppermute(array, axis, [(0, 1), (1, 0)])


def after(array, *others):
    return lax.optimization_barrier((array, *others))[0]


def gather_far(shard, far, widths=None):
    place = lax.axis_index("z")
    pieces, indices = [shard], [place]
    for step in range(1, far):
        pieces.append(lax.ppermute(shard, "z", [(i, (i + step) % far) for i in range(far)]))
        indices.append((place - step) % far)
    rows, width = shard.shape
    widths = widths or [width]
    route, column = [], 0
    for number, one in enumerate(widths):
        route.append((column, one, number, 0))
        column += one
    return assemble(pieces, indices, [(far * rows, one) for one in widths], [route] * far)


def spread(blocks, axis):
    return blocks | {key | {axis}: trade(block, axis) for key, block in blocks.items()}


def tie_received(blocks, other):
    return {key: after(block, other) if key else block for key, block in blocks.items()}


def places(blocks, axes):
    indices = []
    for key in blocks:
        index = 0
        for axis in axes:
            place = lax.axis_index(axis)
            index = 2 * index + (1 - place if axis in key else place)
        indices.append(index)
    return indices


def order_blocks(blocks, axes):
    pieces = list(blocks.values())
    rows, width = pieces[0].shape
    return assemble(pieces, places(blocks, axes), [(len(pieces) * rows, width)])[0]


OWN = frozenset()


def send_half(matrix, axis, outer=1):
    rows, width = matrix.shape
    place = lax.axis_index(axis)
    blocks = matrix.reshape(outer, 2, rows // (2 * outer), width)
    kept = lax.dynamic_index_in_dim(blocks, place, 1, False).reshape(rows // 2, width)
    sent = lax.dynamic_index_in_dim(blocks, 1 - place, 1, False).reshape(rows // 2, width)
    return kept, trade(sent, axis)


def add_half(halves, *follow):
    kept, got = halves
    got = after(got, *follow) if follow else got
    return (kept.astype(jnp.float32) + got.astype(jnp.float32)).astype(kept.dtype)


def send_far(matrix, far):
    size = matrix.shape[0] // far
    place = lax.axis_index("z")
    arrays = [lax.dynamic_slice_in_dim(matrix, place * size, size)]
    for step in range(1, far):
        sent = lax.dynamic_slice_in_dim(matrix, ((place + step) % far) * size, size)
        arrays.append(lax.ppermute(sent, "z", [(i, (i + step) % far) for i in range(far)]))
    return arrays


def add_far(arrays, *follow):
    own, *got = arrays
    if follow:
        got = [after(array, *follow) for array in got]
    return sum(array.astype(jnp.float32) for array in [own, *got])


def column_sums(array):
    return jnp.sum(array.astype(jnp.float32), axis=0)


def by_image(far):
    def on_device(
        inputs,
        cotangent,
        segment,
        w_qkv,
        b_query,
        b_value,
        w_out,
        b_out,
        norm1_gain,
        norm1_shift,
        norm2_gain,
        norm2_shift,
        w_up,
        b_up,
        w_down,
        b_down,
    ):
        place, core = lax.axis_index("ctx"), lax.axis_index("core")
        swap = lambda array: trade(array, "ctx")
        slots, width = inputs.shape
        half_width = width // 2
        pads = 2 * slots - IMAGES * SEQ
        rows = round_up(SEQ + pads, 16)
        near_width = w_up.shape[0] // 8

        inputs_far = swap(inputs)
        segment_far = swap(segment)
        shard_rows = w_qkv.shape[0] // 8
        small = [b_query, b_value, b_out, norm1_gain, norm1_shift, norm2_gain, norm2_shift, b_down]
        small = jnp.concatenate([jnp.stack(small), b_up.reshape(-1, near_width)], axis=0)
        small_rows = small.shape[0]
        pad_small = lambda table: jnp.pad(
            table,
            [(0, 0)] * (table.ndim - 2)
            + [(0, shard_rows - small_rows), (0, 128 - near_width)],
        )
        small = pad_small(small)
        shard_qkv = unfold(w_qkv).reshape(shard_rows, 3, 2, half_width)
        halves = [shard_qkv[:, :, side].reshape(shard_rows, 3 * half_width) for side in range(2)]
        half_qkv = 3 * half_width
        far_one, far_two = gather_far(
            jnp.concatenate([halves[0], small, halves[1]], axis=1), far, [half_qkv + 128, half_qkv]
        )
        shard_up = jnp.concatenate(
            [to_local(unfold(w_out), 1, far), hidden_to_local(unfold(w_up), 1, far)], axis=1
        )
        up_width = w_up.shape[1] * 8
        up_cut = (width + up_width) // 2
        one = spread({OWN: far_one}, "x")
        two = spread({OWN: after(far_two, inputs_far)}, "ctx")
        first = list(one.values()) + list(two.values())
        far_up = gather_far(after(shard_up, *first), far, [up_cut, up_cut])
        one, two = spread(one, "ctx"), spread(two, "x")
        all_one = list(one.values()) + list(two.values())
        shard_down = after(to_local(unfold(w_down), 1, far), far_up[0], *all_one)
        near_down = order_blocks(spread({OWN: shard_down}, "ctx"), ["ctx"])
        one_core, two_core = spread(one, "core"), spread(two, "core")
        axes = ["core", "x", "ctx"]
        routes = [[(0, half_qkv, 0, 0), (half_qkv, 128, 1, 0)]] * 8
        qkv_one, small_local = assemble(
            list(one_core.values()),
            places(one_core, axes),
            [(width, half_qkv), (width, 128)],
            routes,
        )
        qkv_two_weight = order_blocks(two_core, axes)
        up_one = spread({OWN: after(far_up[0], *all_one)}, "x")
        up_two = spread({OWN: after(far_up[1], *all_one)}, "ctx")
        up_one = spread(tie_received(up_one, qkv_two_weight), "ctx")
        up_two = spread(tie_received(up_two, qkv_two_weight), "x")
        far_down = gather_far(near_down, far)[0]

        devices = 8 * far
        small_core = small_local.reshape(devices, shard_rows, 128)[:, :small_rows, :near_width]
        small_core = small_core.astype(jnp.float32)
        small_all = to_natural(small_core, 0, far)
        query_bias, value_bias = (small_all[:, index].reshape(-1) for index in range(2))
        out_bias, first_gain, first_shift, second_gain, second_shift, down_bias = (
            small_core[:, index].reshape(-1) for index in range(2, 8)
        )
        up_bias = hidden_to_local(small_all[:, 8:].reshape(-1), 0, far)

        slot = jnp.arange(slots)
        earlier = slot[:, None] < slot[None, :]

        def ranks(own, other, other_first):
            inside = jnp.sum((own[:, None] == own[None, :]) & earlier, axis=0)
            outside = jnp.sum(other[:, None] == own[None, :], axis=0)
            return inside + jnp.where(other_first, outside, 0)

        rank_near = ranks(segment, segment_far, place == 1)
        rank_far = ranks(segment_far, segment, place == 0)

        def positions(ids, rank, image):
            return jnp.where(ids == image, rank, jnp.where(ids < 0, SEQ + rank, -1))

        row = jnp.arange(rows)
        spot_near = positions(segment, rank_near, place)
        spot_far = positions(segment_far, rank_far, place)
        pick_near = (spot_near[None, :] == row[:, None]).astype(jnp.bfloat16)
        pick_far = (spot_far[None, :] == row[:, None]).astype(jnp.bfloat16)
        spot_other = jnp.where(segment == 1 - place, rank_near, -1)
        give_near = (spot_near[:, None] == row[None, :]).astype(jnp.bfloat16)
        give_far = (spot_other[:, None] == row[None, :]).astype(jnp.bfloat16)
        column = jnp.arange(width)
        to_core = (column[:, None] == to_local(column, 0, far)[None, :]).astype(jnp.bfloat16)

        def take(near, other):
            picked = matmul(pick_near, near) + matmul(pick_far, other)
            return matmul(picked.astype(jnp.bfloat16), to_core)

        def to_give(array):
            natural = nt_dot(array.astype(jnp.bfloat16), to_core).astype(jnp.bfloat16)
            return natural, swap(natural)

        def give(both, *follow):
            near, other = both
            other = after(other, *follow) if follow else other
            return matmul(give_near, near) + matmul(give_far, other)

        kind = (row >= SEQ).astype(jnp.int32) + (row >= SEQ + pads).astype(jnp.int32)
        bias = jnp.where(kind[:, None] == kind[None, :], 0.0, -1e30).astype(jnp.float32)

        values_in = take(inputs, inputs_far)
        normal1, scale1 = standardize(values_in)
        normed1 = (normal1 * first_gain + first_shift).astype(jnp.bfloat16)
        joined_bias = [
            jnp.concatenate(
                [query_bias[cut], jnp.zeros((half_width,), jnp.float32), value_bias[cut]]
            )
            for cut in (slice(0, half_width), slice(half_width, width))
        ]
        joined_one = project(normed1, qkv_one, joined_bias[0])
        attended, log_one = attention_forward(after(joined_one, qkv_two_weight), bias, width, 0)
        joined_two = project(after(normed1, log_one), qkv_two_weight, joined_bias[1])
        up_one, up_two = tie_received(up_one, log_one), tie_received(up_two, log_one)
        up_near = assemble(
            list(up_one.values()) + list(up_two.values()),
            places(up_one, ["x", "ctx"]) + places(up_two, ["x", "ctx"]),
            [(half_width, width + up_width)],
            [[(0, up_cut, 0, 0)]] * 4 + [[(0, up_cut, 0, up_cut)]] * 4,
        )[0]
        up_blocks = spread({OWN: up_near}, "core")
        attended, log_two = attention_forward(
            after(joined_two, near_down), bias, width, half_width // PAIR, attended
        )
        cotangent_far = swap(after(cotangent, up_near))
        down_blocks = spread({OWN: after(far_down, up_near)}, "x")
        out_rows, up_weight = assemble(
            list(up_blocks.values()),
            places(up_blocks, ["core"]),
            [(width, width), (width, up_width)],
            [[(0, width, 0, 0), (width, up_width, 1, 0)]] * 2,
        )
        out_weight = to_natural(out_rows, 0, far)
        middle = values_in + matmul(attended, out_weight) + out_bias
        normal2, scale2 = standardize(middle)
        normed2 = (normal2 * second_gain + second_shift).astype(jnp.bfloat16)
        active, slope = hidden_layer(normed2, up_weight, up_bias)

        live = (row < SEQ).astype(jnp.float32)[:, None]
        d_out_low = (take(cotangent, cotangent_far) * live).astype(jnp.bfloat16)
        down_core = trade(gradient(active, d_out_low, 1 - core), "core")
        down_blocks = {key: after(block, active) for key, block in down_blocks.items()}
        down_weight = order_blocks(spread(down_blocks, "core"), ["core", "x"])
        last = last_layer(active, down_weight, middle, down_bias)
        last_given = to_give(last)
        down_x = send_half(
            gradient(active, d_out_low, core, got=after(down_core, last_given[0])), "x"
        )
        d_hidden, up_sums = d_hidden_layer(after(d_out_low, down_x[0]), down_weight, slope)
        up_core = [
            trade(gradient(normed2, d_hidden, 1 - core, side, 2), "core") for side in range(2)
        ]
        d_middle, d_branch, sums_two = norm_back(
            d_hidden, up_weight, normal2, scale2, second_gain, d_out_low, keep=True
        )
        up_kept = [
            gradient(normed2, d_hidden, core, side, 2, after(up_core[side], d_branch))
            for side in range(2)
        ]
        up_one = send_half(up_kept[0], "ctx", 2)
        up_two = send_half(up_kept[1], "x")
        d_branch = after(d_branch, up_one[0], up_two[0])
        grad_out = to_local(matmul(attended.T, d_branch).astype(jnp.bfloat16), 0, far)
        out_core = send_half(grad_out, "core")
        d_attended = matmul(d_branch, out_weight.T).astype(jnp.bfloat16)
        outputs = give(last_given, d_attended).astype(jnp.bfloat16)
        out_x = send_half(add_half(out_core, d_attended), "x")
        down_far = send_far(add_half(down_x, d_attended), far)
        d_attended = after(d_attended, out_x[0], down_far[0])
        d_one = attention_backward(joined_one, d_attended, 0, log_one, bias)
        one_core = trade(gradient(normed1, d_one, 1 - core), "core")
        partial = d_normed(d_one, qkv_one)
        up_one = send_half(add_half(up_one, partial), "x")
        up_two = send_half(add_half(up_two, partial), "ctx")
        out_y = send_half(add_half(out_x, partial), "ctx")
        d_attended = after(d_attended, partial, up_one[0], up_two[0], out_y[0])
        d_two = attention_backward(joined_two, d_attended, half_width // PAIR, log_two, bias)
        two_core = trade(gradient(normed1, d_two, 1 - core), "core")
        qkv_one_x = send_half(gradient(normed1, d_one, core, got=after(one_core, d_two)), "x")
        down_y = send_half(add_far(down_far, d_two).astype(jnp.bfloat16), "ctx")
        up_far = jnp.concatenate(
            [add_half(halves, d_two) for halves in (up_one, up_two, out_y)], axis=1
        )
        d_two_tied = after(d_two, qkv_one_x[0], down_y[0], up_far)
        d_last, sums_one = norm_back(
            d_two_tied, qkv_two_weight, normal1, scale1, first_gain, d_middle, base=partial
        )
        d_last_given = to_give(d_last)
        qkv_two = gradient(normed1, d_two, core, got=after(two_core, d_last_given[0]))

        vectors = [
            sums_two[2],
            sums_one[0],
            sums_one[1],
            sums_two[0],
            sums_two[1],
            column_sums(d_out_low),
        ]
        joined_vectors = [
            jnp.concatenate([column_sums(d_one[index]), column_sums(d_two[index])])
            for index in (0, 2)
        ]
        vectors = [to_local(vector, 0, far) for vector in joined_vectors] + vectors
        table = jnp.stack([vector.reshape(devices, near_width) for vector in vectors], axis=1)
        up_sums = to_local(hidden_to_natural(up_sums[0], 0, far), 0, far)
        table = jnp.concatenate([table, up_sums.reshape(devices, -1, near_width)], axis=1)
        table = pad_small(table).reshape(width, 128).astype(jnp.bfloat16)
        qkv_two_x = send_half(qkv_two, "x")
        qkv_one_y = send_half(add_half(qkv_one_x, d_last_given[0]), "ctx")
        table = send_half(add_half(send_half(table, "core")), "x")
        up_far = send_far(after(up_far, qkv_two_x[0], qkv_one_y[0]), far)
        qkv_two = jnp.concatenate([add_half(qkv_two_x), add_half(table)], axis=1)
        qkv_two_y = send_half(qkv_two, "ctx")
        qkv_one_far = send_far(add_half(qkv_one_y), far)
        qkv_two_far = send_far(add_half(qkv_two_y), far)

        sum_down = add_half(down_y, d_last_given[0]).astype(jnp.float32)
        sum_up = add_far(up_far)
        sum_up, sum_out = sum_up[:, :up_width], sum_up[:, up_width:]
        sum_one, sum_two = add_far(qkv_one_far), add_far(qkv_two_far)
        small_sums = sum_two[:small_rows, half_qkv : half_qkv + near_width]
        cut_qkv = lambda matrix: matrix[:, :half_qkv].reshape(shard_rows, 3, 1, half_width)
        sum_qkv = jnp.concatenate([cut_qkv(sum_one), cut_qkv(sum_two)], axis=2)
        sum_qkv = sum_qkv.reshape(shard_rows, 3 * width)
        input_grad = give(d_last_given)
        own = lambda index: small_sums[index]
        back = lambda matrix: refold(to_natural(matrix, 1, far))
        return (
            outputs,
            input_grad,
            refold(sum_qkv),
            own(0),
            own(1),
            back(sum_out),
            own(2),
            own(3),
            own(4),
            own(5),
            own(6),
            refold(hidden_to_natural(sum_up, 1, far)),
            small_sums[8:].reshape(-1),
            back(sum_down),
            own(7),
        )

    return on_device


def solution(mesh):
    if mesh.shape["ctx"] == IMAGES and mesh.shape["dp"] % 4 == 0:
        far, axes = mesh.shape["dp"] // 4, ("z", "x", "core", "ctx")
        mesh = jax.sharding.Mesh(mesh.devices.reshape(far, 2, 2, IMAGES), axes)
        body = by_image(far)
    else:
        body, axes = on_device, ("dp", "ctx")
    matrix, vector = P(axes, None), P(axes)
    return jax.shard_map(
        body,
        mesh=mesh,
        in_specs=(matrix, matrix, vector, matrix, vector, vector, matrix)
        + (vector,) * 5
        + (matrix, vector, matrix, vector),
        out_specs=(matrix, matrix, matrix, vector, vector, matrix)
        + (vector,) * 5
        + (matrix, vector, matrix, vector),
        check_vma=False,
    )
```

```python
import functools
import math

import jax
import jax.numpy as jnp
from jax import lax
from jax.experimental import pallas as pl
from jax.experimental.pallas import tpu as pltpu
from jax.sharding import PartitionSpec as P

HD = 64


EPSILON = 1e-06


def layer_norm(value, gain, shift):
    center = value - jnp.mean(value, axis=-1, keepdims=True)
    variance = jnp.mean(center * center, axis=-1, keepdims=True)
    return center * lax.rsqrt(variance + EPSILON) * gain + shift


def gelu_exact(value):
    return jax.nn.gelu(value, approximate=False)


def matmul(left, right):
    return jnp.dot(left, right, preferred_element_type=jnp.float32)


def unfold(stored):
    return stored.reshape(stored.shape[0] // 8, stored.shape[1] * 8)


def refold(matrix):
    return matrix.reshape(matrix.shape[0] * 8, matrix.shape[1] // 8)


def on_device(
    inputs,
    cotangent,
    segment,
    w_qkv,
    b_query,
    b_value,
    w_out,
    b_out,
    norm1_gain,
    norm1_shift,
    norm2_gain,
    norm2_shift,
    w_up,
    b_up,
    w_down,
    b_down,
):
    gathered = (
        lax.all_gather(w_qkv, ("dp", "ctx"), axis=0, tiled=True),
        lax.all_gather(b_query, ("dp", "ctx"), axis=0, tiled=True),
        lax.all_gather(b_value, ("dp", "ctx"), axis=0, tiled=True),
        lax.all_gather(w_out, ("dp", "ctx"), axis=0, tiled=True),
        lax.all_gather(b_out, ("dp", "ctx"), axis=0, tiled=True),
        lax.all_gather(norm1_gain, ("dp", "ctx"), axis=0, tiled=True),
        lax.all_gather(norm1_shift, ("dp", "ctx"), axis=0, tiled=True),
        lax.all_gather(norm2_gain, ("dp", "ctx"), axis=0, tiled=True),
        lax.all_gather(norm2_shift, ("dp", "ctx"), axis=0, tiled=True),
        lax.all_gather(w_up, ("dp", "ctx"), axis=0, tiled=True),
        lax.all_gather(b_up, ("dp", "ctx"), axis=0, tiled=True),
        lax.all_gather(w_down, ("dp", "ctx"), axis=0, tiled=True),
        lax.all_gather(b_down, ("dp", "ctx"), axis=0, tiled=True),
    )
    (
        qkv_stored,
        query_bias,
        value_bias,
        out_stored,
        out_bias,
        gain_one,
        shift_one,
        gain_two,
        shift_two,
        up_stored,
        up_bias,
        down_stored,
        down_bias,
    ) = gathered
    qkv_weight = unfold(qkv_stored)
    out_weight = unfold(out_stored)
    up_weight = unfold(up_stored)
    down_weight = unfold(down_stored)
    first_gain = gain_one.astype(jnp.float32)
    first_shift = shift_one.astype(jnp.float32)
    second_gain = gain_two.astype(jnp.float32)
    second_shift = shift_two.astype(jnp.float32)
    row_count = inputs.shape[0]
    model_width = out_weight.shape[0]
    head_count = model_width // HD
    score_scale = 1.0 / math.sqrt(HD)
    values_in = inputs.astype(jnp.float32)
    normed1 = layer_norm(values_in, first_gain, first_shift).astype(jnp.bfloat16)
    joined = matmul(normed1, qkv_weight)
    queries = (joined[:, :model_width] + query_bias.astype(jnp.float32)).astype(jnp.bfloat16)
    key_rows = joined[:, model_width : 2 * model_width].astype(jnp.bfloat16)
    value_rows = (joined[:, 2 * model_width :] + value_bias.astype(jnp.float32)).astype(
        jnp.bfloat16
    )
    key_all, value_all, seg_all = (
        lax.all_gather(key_rows, "ctx", axis=0, tiled=True),
        lax.all_gather(value_rows, "ctx", axis=0, tiled=True),
        lax.all_gather(segment.astype(jnp.bfloat16), "ctx", axis=0, tiled=True),
    )
    key_count = key_all.shape[0]
    query_heads = queries.reshape(row_count, head_count, HD)
    key_heads = key_all.reshape(key_count, head_count, HD)
    value_heads = value_all.reshape(key_count, head_count, HD)
    own_seg = segment.astype(jnp.float32)
    group_seg = seg_all.astype(jnp.float32)
    same_seg = own_seg[:, None] == group_seg[None, :]

    def make_scores():
        raw = (
            jnp.einsum("qhd,khd->hqk", query_heads, key_heads, preferred_element_type=jnp.float32)
            * score_scale
        )
        return jnp.where(same_seg[None], raw, -1e30)

    scores = make_scores()
    row_max = jnp.max(scores, axis=-1, keepdims=True)
    expo = jnp.exp(scores - row_max)
    row_total = jnp.sum(expo, axis=-1, keepdims=True)
    probs_low = (expo / row_total).astype(jnp.bfloat16)
    log_total = row_max + jnp.log(row_total)
    mixed = jnp.einsum("hqk,khd->qhd", probs_low, value_heads, preferred_element_type=jnp.float32)
    attended = mixed.reshape(row_count, model_width).astype(jnp.bfloat16)
    middle = values_in + matmul(attended, out_weight) + out_bias.astype(jnp.float32)
    normed2 = layer_norm(middle, second_gain, second_shift).astype(jnp.bfloat16)
    hidden = matmul(normed2, up_weight) + up_bias.astype(jnp.float32)
    active = gelu_exact(hidden).astype(jnp.bfloat16)
    outputs = (middle + matmul(active, down_weight) + down_bias.astype(jnp.float32)).astype(
        jnp.bfloat16
    )
    back_qkv, back_out, back_up, back_down = (qkv_weight, out_weight, up_weight, down_weight)
    valid = (segment >= 0).astype(jnp.float32)[:, None]
    d_out = cotangent.astype(jnp.float32) * valid
    d_out_low = d_out.astype(jnp.bfloat16)
    grad_down = refold(matmul(active.T, d_out_low))
    grad_down_bias = jnp.sum(d_out_low.astype(jnp.float32), axis=0)
    d_active = matmul(d_out_low, back_down.T)
    gelu_value, gelu_pull = jax.vjp(gelu_exact, hidden)
    d_hidden = gelu_pull(d_active)[0].astype(jnp.bfloat16)
    grad_up = refold(matmul(normed2.T, d_hidden))
    grad_up_bias = jnp.sum(d_hidden.astype(jnp.float32), axis=0)
    d_normed2 = matmul(d_hidden, back_up.T)
    norm_value, norm_pull = jax.vjp(layer_norm, middle, second_gain, second_shift)
    d_middle_norm, grad_gain_two, grad_shift_two = norm_pull(d_normed2)
    d_middle = d_out + d_middle_norm
    d_branch = d_middle.astype(jnp.bfloat16)
    grad_out = refold(matmul(attended.T, d_branch))
    grad_out_bias = jnp.sum(d_branch.astype(jnp.float32), axis=0)
    d_attended_flat = matmul(d_branch, back_out.T).astype(jnp.bfloat16)
    d_attended = d_attended_flat.reshape(row_count, head_count, HD)
    scores = make_scores()
    probs = jnp.exp(scores - log_total)
    d_probs = jnp.einsum(
        "qhd,khd->hqk", d_attended, value_heads, preferred_element_type=jnp.float32
    )
    delta_rows = jnp.sum(probs * d_probs, axis=-1, keepdims=True)
    d_scores = (probs * (d_probs - delta_rows)).astype(jnp.bfloat16)
    d_query = (
        jnp.einsum("hqk,khd->qhd", d_scores, key_heads, preferred_element_type=jnp.float32)
        * score_scale
    ).reshape(row_count, model_width)
    probs_again = probs.astype(jnp.bfloat16)
    d_key_all = (
        jnp.einsum("hqk,qhd->khd", d_scores, query_heads, preferred_element_type=jnp.float32)
        * score_scale
    ).reshape(key_count, model_width)
    d_value_all = jnp.einsum(
        "hqk,qhd->khd", probs_again, d_attended, preferred_element_type=jnp.float32
    ).reshape(key_count, model_width)
    d_key, d_value = (
        lax.psum_scatter(
            d_key_all.astype(jnp.bfloat16), "ctx", scatter_dimension=0, tiled=True
        ).astype(jnp.float32),
        lax.psum_scatter(
            d_value_all.astype(jnp.bfloat16), "ctx", scatter_dimension=0, tiled=True
        ).astype(jnp.float32),
    )
    d_query_low = d_query.astype(jnp.bfloat16)
    d_value_low = d_value.astype(jnp.bfloat16)
    d_joined = jnp.concatenate([d_query_low, d_key.astype(jnp.bfloat16), d_value_low], axis=1)
    grad_qkv = refold(matmul(normed1.T, d_joined))
    grad_query_bias = jnp.sum(d_query_low.astype(jnp.float32), axis=0)
    grad_value_bias = jnp.sum(d_value_low.astype(jnp.float32), axis=0)
    d_normed1 = matmul(d_joined, back_qkv.T)
    first_value, first_pull = jax.vjp(layer_norm, values_in, first_gain, first_shift)
    d_input_norm, grad_gain_one, grad_shift_one = first_pull(d_normed1)
    input_grad = d_middle + d_input_norm
    partial_sums = (
        lax.psum_scatter(
            grad_qkv.astype(jnp.bfloat16), "dp", scatter_dimension=0, tiled=True
        ).astype(jnp.float32),
        lax.psum_scatter(
            grad_query_bias.astype(jnp.bfloat16), "dp", scatter_dimension=0, tiled=True
        ).astype(jnp.float32),
        lax.psum_scatter(
            grad_value_bias.astype(jnp.bfloat16), "dp", scatter_dimension=0, tiled=True
        ).astype(jnp.float32),
        lax.psum_scatter(
            grad_out.astype(jnp.bfloat16), "dp", scatter_dimension=0, tiled=True
        ).astype(jnp.float32),
        lax.psum_scatter(
            grad_out_bias.astype(jnp.bfloat16), "dp", scatter_dimension=0, tiled=True
        ).astype(jnp.float32),
        lax.psum_scatter(
            grad_gain_one.astype(jnp.bfloat16), "dp", scatter_dimension=0, tiled=True
        ).astype(jnp.float32),
        lax.psum_scatter(
            grad_shift_one.astype(jnp.bfloat16), "dp", scatter_dimension=0, tiled=True
        ).astype(jnp.float32),
        lax.psum_scatter(
            grad_gain_two.astype(jnp.bfloat16), "dp", scatter_dimension=0, tiled=True
        ).astype(jnp.float32),
        lax.psum_scatter(
            grad_shift_two.astype(jnp.bfloat16), "dp", scatter_dimension=0, tiled=True
        ).astype(jnp.float32),
        lax.psum_scatter(
            grad_up.astype(jnp.bfloat16), "dp", scatter_dimension=0, tiled=True
        ).astype(jnp.float32),
        lax.psum_scatter(
            grad_up_bias.astype(jnp.bfloat16), "dp", scatter_dimension=0, tiled=True
        ).astype(jnp.float32),
        lax.psum_scatter(
            grad_down.astype(jnp.bfloat16), "dp", scatter_dimension=0, tiled=True
        ).astype(jnp.float32),
        lax.psum_scatter(
            grad_down_bias.astype(jnp.bfloat16), "dp", scatter_dimension=0, tiled=True
        ).astype(jnp.float32),
    )
    all_sums = (
        lax.psum_scatter(
            partial_sums[0].astype(jnp.bfloat16), "ctx", scatter_dimension=0, tiled=True
        ).astype(jnp.float32),
        lax.psum_scatter(
            partial_sums[1].astype(jnp.bfloat16), "ctx", scatter_dimension=0, tiled=True
        ).astype(jnp.float32),
        lax.psum_scatter(
            partial_sums[2].astype(jnp.bfloat16), "ctx", scatter_dimension=0, tiled=True
        ).astype(jnp.float32),
        lax.psum_scatter(
            partial_sums[3].astype(jnp.bfloat16), "ctx", scatter_dimension=0, tiled=True
        ).astype(jnp.float32),
        lax.psum_scatter(
            partial_sums[4].astype(jnp.bfloat16), "ctx", scatter_dimension=0, tiled=True
        ).astype(jnp.float32),
        lax.psum_scatter(
            partial_sums[5].astype(jnp.bfloat16), "ctx", scatter_dimension=0, tiled=True
        ).astype(jnp.float32),
        lax.psum_scatter(
            partial_sums[6].astype(jnp.bfloat16), "ctx", scatter_dimension=0, tiled=True
        ).astype(jnp.float32),
        lax.psum_scatter(
            partial_sums[7].astype(jnp.bfloat16), "ctx", scatter_dimension=0, tiled=True
        ).astype(jnp.float32),
        lax.psum_scatter(
            partial_sums[8].astype(jnp.bfloat16), "ctx", scatter_dimension=0, tiled=True
        ).astype(jnp.float32),
        lax.psum_scatter(
            partial_sums[9].astype(jnp.bfloat16), "ctx", scatter_dimension=0, tiled=True
        ).astype(jnp.float32),
        lax.psum_scatter(
            partial_sums[10].astype(jnp.bfloat16), "ctx", scatter_dimension=0, tiled=True
        ).astype(jnp.float32),
        lax.psum_scatter(
            partial_sums[11].astype(jnp.bfloat16), "ctx", scatter_dimension=0, tiled=True
        ).astype(jnp.float32),
        lax.psum_scatter(
            partial_sums[12].astype(jnp.bfloat16), "ctx", scatter_dimension=0, tiled=True
        ).astype(jnp.float32),
    )
    (
        sum_qkv,
        sum_query_bias,
        sum_value_bias,
        sum_out,
        sum_out_bias,
        sum_gain_one,
        sum_shift_one,
        sum_gain_two,
        sum_shift_two,
        sum_up,
        sum_up_bias,
        sum_down,
        sum_down_bias,
    ) = all_sums
    return (
        outputs,
        input_grad,
        sum_qkv,
        sum_query_bias,
        sum_value_bias,
        sum_out,
        sum_out_bias,
        sum_gain_one,
        sum_shift_one,
        sum_gain_two,
        sum_shift_two,
        sum_up,
        sum_up_bias,
        sum_down,
        sum_down_bias,
    )


SEQ = 577
IMAGES = 2
PAIR = 2 * HD
CHUNK = 256
BLOCK = 512
HINT = pl.CostEstimate(flops=1, bytes_accessed=1, transcendentals=0)
ERFC = (
    0.09873409569263458,
    0.09871950000524521,
    0.09271052479743958,
    0.08134904503822327,
    0.056456614285707474,
    0.07422702759504318,
    -0.050631966441869736,
    0.11820460855960846,
    -0.09110676497220993,
    0.021337319165468216,
)
ERFC_STEP = 0.35


def round_up(count, unit):
    return -(-count // unit) * unit


def limit(mebibytes):
    return pltpu.CompilerParams(vmem_limit_bytes=mebibytes * 2**20)


def chunks_of(count):
    return [(start, min(CHUNK, count - start)) for start in range(0, count, CHUNK)]


def nt_dot(left, right):
    return lax.dot_general(
        left, right, (((1,), (1,)), ((), ())), preferred_element_type=jnp.float32
    )


def tn_dot(left, right):
    return lax.dot_general(
        left, right, (((0,), (0,)), ((), ())), preferred_element_type=jnp.float32
    )


def half_mask(rows):
    return lax.broadcasted_iota(jnp.int32, (rows, PAIR), 1) < HD


def forward_kernel(query_ref, key_ref, value_ref, bias_ref, *refs):
    attended_ref, log_ref = refs[-2:]
    rows = query_ref.shape[1]
    first = half_mask(rows)
    zero = jnp.zeros((rows, PAIR), jnp.bfloat16)
    key = key_ref[0]
    key_sides = (jnp.where(first, key, zero), jnp.where(first, zero, key))
    value_t = value_ref[0].astype(jnp.float32).T.astype(jnp.bfloat16)
    scale = jnp.bfloat16(1.0 / math.sqrt(HD))
    for start, size in chunks_of(rows):
        query = query_ref[0, start : start + size, :] * scale
        bias = bias_ref[:, start : start + size]
        outs = []
        for side in range(2):
            scores = nt_dot(key_sides[side], query) + bias
            top = jnp.max(scores, axis=0, keepdims=True)
            expo = jnp.exp(scores - top)
            total = jnp.sum(expo, axis=0, keepdims=True)
            probs_low = (expo * (1.0 / total)).astype(jnp.bfloat16)
            outs.append(matmul(value_t[side * HD : (side + 1) * HD, :], probs_low))
            log_ref[0, side : side + 1, start : start + size] = top + jnp.log(total)
        mixed = jnp.concatenate(outs, axis=0)
        attended_ref[start : start + size, :] = mixed.T.astype(jnp.bfloat16)


def backward_kernel(
    query_ref, key_ref, value_ref, d_ref, log_ref, bias_ref, joined_ref, dk_sum, dv_sum
):
    rows = query_ref.shape[1]
    first = half_mask(rows)
    zero = jnp.zeros((rows, PAIR), jnp.bfloat16)
    key = key_ref[0]
    value = value_ref[0]
    key_sides = (jnp.where(first, key, zero), jnp.where(first, zero, key))
    value_sides = (jnp.where(first, value, zero), jnp.where(first, zero, value))
    key_t = key.astype(jnp.float32).T.astype(jnp.bfloat16)
    scale = jnp.bfloat16(1.0 / math.sqrt(HD))
    for start, size in chunks_of(rows):
        query = query_ref[0, start : start + size, :] * scale
        d_rows = d_ref[start : start + size, :]
        bias = bias_ref[:, start : start + size]
        outs = []
        for side in range(2):
            scores = nt_dot(key_sides[side], query) + bias
            probs = jnp.exp(scores - log_ref[0, side : side + 1, start : start + size])
            d_probs = nt_dot(value_sides[side], d_rows)
            product = probs * d_probs
            delta = jnp.sum(product, axis=0, keepdims=True)
            d_scores = (product - probs * delta).astype(jnp.bfloat16)
            d_value = matmul(probs.astype(jnp.bfloat16), d_rows)
            d_key = matmul(d_scores, query)
            if start == 0:
                dv_sum[side] = d_value
                dk_sum[side] = d_key
            else:
                dv_sum[side] += d_value
                dk_sum[side] += d_key
            outs.append(matmul(key_t[side * HD : (side + 1) * HD, :], d_scores))
        d_query = jnp.concatenate(outs, axis=0) * (1.0 / math.sqrt(HD))
        joined_ref[0, start : start + size, :] = d_query.T.astype(jnp.bfloat16)
    joined_ref[1] = jnp.where(first, dk_sum[0], dk_sum[1]).astype(jnp.bfloat16)
    joined_ref[2] = jnp.where(first, dv_sum[0], dv_sum[1]).astype(jnp.bfloat16)


def pair_spec(rows, part):
    return pl.BlockSpec((1, rows, PAIR), lambda i: (part, 0, i))


def attention_forward(joined, bias, total, first_pair, base=None):
    rows, width = joined.shape[1:]
    pairs = width // PAIR
    extra = [] if base is None else [base]
    return pl.pallas_call(
        forward_kernel,
        grid=(pairs,),
        in_specs=[pair_spec(rows, part) for part in range(3)]
        + [pl.BlockSpec((rows, rows), lambda i: (0, 0))]
        + [pl.BlockSpec(memory_space=pl.ANY) for _ in extra],
        out_specs=[
            pl.BlockSpec((rows, PAIR), lambda i: (0, first_pair + i)),
            pl.BlockSpec((1, 2, rows), lambda i: (i, 0, 0)),
        ],
        out_shape=[
            jax.ShapeDtypeStruct((rows, total), jnp.bfloat16),
            jax.ShapeDtypeStruct((pairs, 2, rows), jnp.float32),
        ],
        input_output_aliases={4: 0} if extra else {},
        compiler_params=limit(32),
        cost_estimate=HINT,
        name="attention_forward",
    )(joined, joined, joined, bias, *extra)


def attention_backward(joined, d_attended, first_pair, log_total, bias):
    rows, width = joined.shape[1:]
    return pl.pallas_call(
        backward_kernel,
        grid=(width // PAIR,),
        in_specs=[pair_spec(rows, part) for part in range(3)]
        + [
            pl.BlockSpec((rows, PAIR), lambda i: (0, first_pair + i)),
            pl.BlockSpec((1, 2, rows), lambda i: (i, 0, 0)),
            pl.BlockSpec((rows, rows), lambda i: (0, 0)),
        ],
        out_specs=pl.BlockSpec((3, rows, PAIR), lambda i: (0, 0, i)),
        out_shape=jax.ShapeDtypeStruct((3, rows, width), jnp.bfloat16),
        scratch_shapes=[pltpu.VMEM((2, rows, PAIR), jnp.float32)] * 2,
        compiler_params=limit(32),
        cost_estimate=HINT,
        name="attention_backward",
    )(joined, joined, joined, d_attended, log_total, bias)


def whole_spec(shape):
    return pl.BlockSpec(shape, lambda *_: (0,) * len(shape))


def project_kernel(x_ref, weight_ref, bias_ref, out_ref):
    out_ref[0] = (matmul(x_ref[...], weight_ref[...]) + bias_ref[...]).astype(out_ref.dtype)


def project(x, weight, bias):
    rows, depth = x.shape
    width = weight.shape[1] // 3
    return pl.pallas_call(
        project_kernel,
        grid=(3,),
        in_specs=[
            whole_spec(x.shape),
            pl.BlockSpec((depth, width), lambda i: (0, i)),
            pl.BlockSpec((1, width), lambda i: (0, i)),
        ],
        out_specs=pl.BlockSpec((1, rows, width), lambda i: (i, 0, 0)),
        out_shape=jax.ShapeDtypeStruct((3, rows, width), jnp.bfloat16),
        compiler_params=limit(24),
        cost_estimate=HINT,
        name="project",
    )(x, weight, bias[None, :])


def hidden_kernel(x_ref, weight_ref, bias_ref, active_ref, slope_ref):
    hidden = matmul(x_ref[...], weight_ref[...]) + bias_ref[...]
    share = 1.0 / (1.0 + (ERFC_STEP * math.sqrt(0.5)) * jnp.abs(hidden))
    density = jnp.exp(-0.5 * hidden * hidden)
    tail = jnp.full_like(share, ERFC[-1])
    for factor in ERFC[-2::-1]:
        tail = tail * share + factor
    tail = tail * share * density
    phi = jnp.where(hidden < 0.0, tail, 1.0 - tail)
    active_ref[...] = (hidden * phi).astype(jnp.bfloat16)
    slope = phi + hidden * density * (1.0 / math.sqrt(2.0 * math.pi))
    slope_ref[...] = slope.astype(jnp.bfloat16)


def hidden_layer(x, weight, bias):
    rows, depth = x.shape
    width = weight.shape[1]
    block = pl.BlockSpec((rows, BLOCK), lambda i: (0, i))
    return pl.pallas_call(
        hidden_kernel,
        grid=(width // BLOCK,),
        in_specs=[
            whole_spec(x.shape),
            pl.BlockSpec((depth, BLOCK), lambda i: (0, i)),
            pl.BlockSpec((1, BLOCK), lambda i: (0, i)),
        ],
        out_specs=[block, block],
        out_shape=[jax.ShapeDtypeStruct((rows, width), jnp.bfloat16)] * 2,
        compiler_params=limit(32),
        cost_estimate=HINT,
        name="hidden_layer",
    )(x, weight, bias[None, :])


def last_kernel(active_ref, weight_ref, middle_ref, bias_ref, out_ref, total):
    step = pl.program_id(0)

    @pl.when(step == 0)
    def _():
        total[...] = middle_ref[...] + bias_ref[...]

    total[...] += matmul(active_ref[...], weight_ref[...])

    @pl.when(step == pl.num_programs(0) - 1)
    def _():
        out_ref[...] = total[...].astype(out_ref.dtype)


def last_layer(active, weight, middle, bias):
    rows, depth = active.shape
    width = weight.shape[1]
    return pl.pallas_call(
        last_kernel,
        grid=(depth // BLOCK,),
        in_specs=[
            pl.BlockSpec((rows, BLOCK), lambda i: (0, i)),
            pl.BlockSpec((BLOCK, width), lambda i: (i, 0)),
            whole_spec((rows, width)),
            whole_spec((1, width)),
        ],
        out_specs=whole_spec((rows, width)),
        out_shape=jax.ShapeDtypeStruct((rows, width), jnp.bfloat16),
        scratch_shapes=[pltpu.VMEM((rows, width), jnp.float32)],
        compiler_params=limit(52),
        cost_estimate=HINT,
        name="last_layer",
    )(active, weight, middle, bias[None, :])


def d_hidden_kernel(d_ref, weight_ref, slope_ref, out_ref, sum_ref):
    d_active = nt_dot(d_ref[...], weight_ref[...])
    d_hidden = (d_active * slope_ref[...].astype(jnp.float32)).astype(jnp.bfloat16)
    out_ref[...] = d_hidden
    sum_ref[...] = jnp.sum(d_hidden.astype(jnp.float32), axis=0, keepdims=True)


def d_hidden_layer(d_out, weight, slope):
    rows, depth = d_out.shape
    width = weight.shape[0]
    block = pl.BlockSpec((rows, BLOCK), lambda i: (0, i))
    return pl.pallas_call(
        d_hidden_kernel,
        grid=(width // BLOCK,),
        in_specs=[
            whole_spec(d_out.shape),
            pl.BlockSpec((BLOCK, depth), lambda i: (i, 0)),
            block,
        ],
        out_specs=[block, pl.BlockSpec((1, BLOCK), lambda i: (0, i))],
        out_shape=[
            jax.ShapeDtypeStruct((rows, width), jnp.bfloat16),
            jax.ShapeDtypeStruct((1, width), jnp.float32),
        ],
        compiler_params=limit(24),
        cost_estimate=HINT,
        name="d_hidden_layer",
    )(d_out, weight, slope)


def d_normed_kernel(d_ref, weight_ref, *refs):
    out_ref = refs[-1]
    d_rows = d_ref[0] if len(d_ref.shape) == 3 else d_ref[...]
    product = nt_dot(d_rows, weight_ref[...])
    step = pl.program_id(0)

    @pl.when(step == 0)
    def _():
        out_ref[...] = product + refs[0][...] if len(refs) == 2 else product

    @pl.when(step > 0)
    def _():
        out_ref[...] += product


def d_normed(d_rows, weight, base=None):
    rows, depth = d_rows.shape[-2], weight.shape[0]
    if d_rows.ndim == 3:
        d_spec = pl.BlockSpec((1, rows, BLOCK), lambda i: (i, 0, 0))
    else:
        d_spec = pl.BlockSpec((rows, BLOCK), lambda i: (0, i))
    extra = [] if base is None else [base]
    return pl.pallas_call(
        d_normed_kernel,
        grid=(weight.shape[1] // BLOCK,),
        in_specs=[d_spec, pl.BlockSpec((depth, BLOCK), lambda i: (0, i))]
        + [whole_spec((rows, depth)) for _ in extra],
        out_specs=whole_spec((rows, depth)),
        out_shape=jax.ShapeDtypeStruct((rows, depth), jnp.float32),
        compiler_params=limit(24),
        cost_estimate=HINT,
        name="d_normed",
    )(d_rows, weight, *extra)


def norm_back_kernel(count, d_ref, weight_ref, *refs):
    base, (normal_ref, scale_ref, gain_ref, residual_ref) = refs[:count], refs[count : count + 4]
    *wide_refs, low_ref, sum_ref, total = refs[count + 4 :]
    d_rows = d_ref[0] if len(d_ref.shape) == 3 else d_ref[...]
    product = nt_dot(d_rows, weight_ref[...])
    step = pl.program_id(0)

    @pl.when(step == 0)
    def _():
        total[...] = product + base[0][...] if base else product

    @pl.when(step > 0)
    def _():
        total[...] += product

    @pl.when(step == pl.num_programs(0) - 1)
    def _():
        rows = total.shape[0]
        sums = [jnp.zeros((1, total.shape[1]), jnp.float32)] * 3
        for start, size in chunks_of(rows):
            part = slice(start, start + size)
            d_part, normal = total[part, :], normal_ref[part, :]
            along = d_part * normal
            scaled = d_part * gain_ref[...]
            mean = jnp.mean(scaled, axis=-1, keepdims=True)
            slope = jnp.mean(scaled * normal, axis=-1, keepdims=True)
            wide = (scaled - mean - normal * slope) * scale_ref[part, :]
            wide = wide + residual_ref[part, :].astype(jnp.float32)
            low = wide.astype(jnp.bfloat16)
            for wide_ref in wide_refs:
                wide_ref[part, :] = wide
            low_ref[part, :] = low
            for number, array in enumerate((along, d_part, low.astype(jnp.float32))):
                sums[number] = sums[number] + jnp.sum(array, axis=0, keepdims=True)
        for number, one in enumerate(sums):
            sum_ref[number : number + 1, :] = one


def norm_back(d_rows, weight, normal, scale, gain, residual, base=None, keep=False):
    rows, depth = d_rows.shape[-2], weight.shape[0]
    if d_rows.ndim == 3:
        d_spec = pl.BlockSpec((1, rows, BLOCK), lambda i: (i, 0, 0))
    else:
        d_spec = pl.BlockSpec((rows, BLOCK), lambda i: (0, i))
    extra = [] if base is None else [base]
    full = whole_spec((rows, depth))
    kinds = [jnp.float32] * keep + [jnp.bfloat16]
    return pl.pallas_call(
        functools.partial(norm_back_kernel, len(extra)),
        grid=(weight.shape[1] // BLOCK,),
        in_specs=[d_spec, pl.BlockSpec((depth, BLOCK), lambda i: (0, i))]
        + [full for _ in extra]
        + [full, whole_spec((rows, 1)), whole_spec((1, depth)), full],
        out_specs=[full for _ in kinds] + [whole_spec((8, depth))],
        out_shape=[jax.ShapeDtypeStruct((rows, depth), kind) for kind in kinds]
        + [jax.ShapeDtypeStruct((8, depth), jnp.float32)],
        scratch_shapes=[pltpu.VMEM((rows, depth), jnp.float32)],
        compiler_params=limit(40),
        cost_estimate=HINT,
        name="norm_back",
    )(d_rows, weight, *extra, normal, scale, gain[None, :], residual)


def gradient_kernel(index_ref, x_ref, d_ref, *refs):
    out_ref = refs[-1]
    x = x_ref[...]
    width = d_ref.shape[-1]
    for part in range(out_ref.shape[1] // width):
        columns = slice(part * width, (part + 1) * width)
        product = tn_dot(x, d_ref[part] if len(d_ref.shape) == 3 else d_ref[...])
        if len(refs) == 2:
            product = product + refs[0][:, columns].astype(jnp.float32)
        out_ref[:, columns] = product.astype(out_ref.dtype)


def gradient(x, d_rows, half, column=0, columns=1, got=None):
    rows, depth = x.shape
    size = depth // 2
    blocks = size // CHUNK
    if d_rows.ndim == 3:
        d_spec = pl.BlockSpec(d_rows.shape, lambda i, index: (0, 0, 0))
        width = d_rows.shape[0] * d_rows.shape[2]
    else:
        width = d_rows.shape[1] // columns
        d_spec = pl.BlockSpec((rows, width), lambda i, index: (0, column))
    block = pl.BlockSpec((CHUNK, width), lambda i, index: (i, 0))
    extra = [] if got is None else [got]
    return pl.pallas_call(
        gradient_kernel,
        grid_spec=pltpu.PrefetchScalarGridSpec(
            num_scalar_prefetch=1,
            grid=(blocks,),
            in_specs=[
                pl.BlockSpec((rows, CHUNK), lambda i, index: (0, index[0] * blocks + i)),
                d_spec,
            ]
            + [block for _ in extra],
            out_specs=block,
        ),
        out_shape=jax.ShapeDtypeStruct((size, width), jnp.bfloat16),
        compiler_params=limit(32),
        cost_estimate=HINT,
        name="gradient",
    )(half.reshape(1).astype(jnp.int32), x, d_rows, *extra)


def standardize(value):
    center = value - jnp.mean(value, axis=-1, keepdims=True)
    variance = jnp.mean(center * center, axis=-1, keepdims=True)
    scale = lax.rsqrt(variance + EPSILON)
    return center * scale, scale


def reorder(array, axis, sizes, spots):
    shape = array.shape
    count = math.prod(sizes)
    cut = shape[:axis] + tuple(sizes) + (shape[axis] // count,) + shape[axis + 1 :]
    spots = list(range(axis)) + [axis + spot for spot in spots]
    return array.reshape(cut).transpose(spots + list(range(len(spots), len(cut)))).reshape(shape)


def to_local(array, axis, far):
    return reorder(array, axis, (far, 2, 2, 2), (2, 1, 3, 0))


def to_natural(array, axis, far):
    return reorder(array, axis, (2, 2, 2, far), (3, 1, 0, 2))


def hidden_to_local(array, axis, far):
    return reorder(array, axis, (far, 2, 2, 2), (2, 1, 0, 3))


def hidden_to_natural(array, axis, far):
    return reorder(array, axis, (2, 2, far, 2), (2, 1, 0, 3))


def assemble_kernel(routes, index_ref, *refs):
    count = len(routes)
    pieces, stages = refs[:count], refs[-count - 2 : -2]
    wholes, (arrived, left) = refs[count : -count - 2], refs[-2:]
    incoming = [
        pltpu.make_async_copy(piece, stage, arrived.at[number])
        for number, (piece, stage) in enumerate(zip(pieces, stages))
    ]
    for copy in incoming:
        copy.start()
    outgoing = []
    for number, route in enumerate(routes):
        incoming[number].wait()
        size = pieces[number].shape[0]
        start = pl.multiple_of(index_ref[number] * size, 16)
        for part, (source, width, whole, target) in enumerate(route):
            copy = pltpu.make_async_copy(
                stages[number].at[:, pl.ds(source, width)],
                wholes[whole].at[pl.ds(start, size), pl.ds(target, width)],
                left.at[part, number],
            )
            copy.start()
            outgoing.append(copy)
    for copy in outgoing:
        copy.wait()


def assemble(pieces, indices, outs, routes=None):
    if routes is None:
        routes = [[(0, piece.shape[1], 0, 0)] for piece in pieces]
    count = len(pieces)
    anywhere = pl.BlockSpec(memory_space=pl.ANY)
    kind = pieces[0].dtype
    return pl.pallas_call(
        functools.partial(assemble_kernel, routes),
        in_specs=[pl.BlockSpec(memory_space=pltpu.SMEM)] + [anywhere] * count,
        out_specs=[anywhere] * len(outs),
        out_shape=[jax.ShapeDtypeStruct(shape, kind) for shape in outs],
        scratch_shapes=[pltpu.VMEM(piece.shape, kind) for piece in pieces]
        + [
            pltpu.SemaphoreType.DMA((count,)),
            pltpu.SemaphoreType.DMA((max(len(route) for route in routes), count)),
        ],
        compiler_params=limit(16),
        cost_estimate=HINT,
        name="assemble",
    )(jnp.stack(indices).astype(jnp.int32), *pieces)


def trade(array, axis):
    return lax.ppermute(array, axis, [(0, 1), (1, 0)])


def after(array, *others):
    return lax.optimization_barrier((array, *others))[0]


def gather_far(shard, far, widths=None, follow=()):
    place = lax.axis_index("z")
    pieces, indices = [shard], [place]
    for step in range(1, far):
        got = lax.ppermute(shard, "z", [(i, (i + step) % far) for i in range(far)])
        pieces.append(after(got, *follow) if follow else got)
        indices.append((place - step) % far)
    rows, width = shard.shape
    widths = widths or [width]
    route, column = [], 0
    for number, one in enumerate(widths):
        route.append((column, one, number, 0))
        column += one
    return assemble(pieces, indices, [(far * rows, one) for one in widths], [route] * far)


def spread(blocks, axis):
    return blocks | {key | {axis}: trade(block, axis) for key, block in blocks.items()}


def tie_received(blocks, other):
    return {key: after(block, other) if key else block for key, block in blocks.items()}


def places(blocks, axes):
    indices = []
    for key in blocks:
        index = 0
        for axis in axes:
            place = lax.axis_index(axis)
            index = 2 * index + (1 - place if axis in key else place)
        indices.append(index)
    return indices


def order_blocks(blocks, axes):
    pieces = list(blocks.values())
    rows, width = pieces[0].shape
    return assemble(pieces, places(blocks, axes), [(len(pieces) * rows, width)])[0]


OWN = frozenset()


def send_half(matrix, axis, outer=1):
    rows, width = matrix.shape
    place = lax.axis_index(axis)
    blocks = matrix.reshape(outer, 2, rows // (2 * outer), width)
    kept = lax.dynamic_index_in_dim(blocks, place, 1, False).reshape(rows // 2, width)
    sent = lax.dynamic_index_in_dim(blocks, 1 - place, 1, False).reshape(rows // 2, width)
    return kept, trade(sent, axis)


def add_half(halves, *follow):
    kept, got = halves
    got = after(got, *follow) if follow else got
    return (kept.astype(jnp.float32) + got.astype(jnp.float32)).astype(kept.dtype)


def send_far(matrix, far):
    size = matrix.shape[0] // far
    place = lax.axis_index("z")
    arrays = [lax.dynamic_slice_in_dim(matrix, place * size, size)]
    for step in range(1, far):
        sent = lax.dynamic_slice_in_dim(matrix, ((place + step) % far) * size, size)
        arrays.append(lax.ppermute(sent, "z", [(i, (i + step) % far) for i in range(far)]))
    return arrays


def add_far(arrays, *follow):
    own, *got = arrays
    if follow:
        got = [after(array, *follow) for array in got]
    return sum(array.astype(jnp.float32) for array in [own, *got])


def column_sums(array):
    return jnp.sum(array.astype(jnp.float32), axis=0)


def by_image(far):
    def on_device(
        inputs,
        cotangent,
        segment,
        w_qkv,
        b_query,
        b_value,
        w_out,
        b_out,
        norm1_gain,
        norm1_shift,
        norm2_gain,
        norm2_shift,
        w_up,
        b_up,
        w_down,
        b_down,
    ):
        place, core = lax.axis_index("ctx"), lax.axis_index("core")
        swap = lambda array: trade(array, "ctx")
        slots, width = inputs.shape
        half_width = width // 2
        pads = 2 * slots - IMAGES * SEQ
        rows = round_up(SEQ + pads, 16)
        near_width = w_up.shape[0] // 8

        inputs_far = swap(inputs)
        segment_far = swap(segment)
        shard_rows = w_qkv.shape[0] // 8
        small = [b_query, b_value, b_out, norm1_gain, norm1_shift, norm2_gain, norm2_shift, b_down]
        small = jnp.concatenate([jnp.stack(small), b_up.reshape(-1, near_width)], axis=0)
        small_rows = small.shape[0]
        pad_small = lambda table: jnp.pad(
            table,
            [(0, 0)] * (table.ndim - 2)
            + [(0, shard_rows - small_rows), (0, 128 - near_width)],
        )
        small = pad_small(small)
        shard_qkv = unfold(w_qkv).reshape(shard_rows, 3, 2, half_width)
        halves = [shard_qkv[:, :, side].reshape(shard_rows, 3 * half_width) for side in range(2)]
        half_qkv = 3 * half_width
        far_one, far_two = gather_far(
            jnp.concatenate([halves[0], small, halves[1]], axis=1), far, [half_qkv + 128, half_qkv]
        )
        shard_up = jnp.concatenate(
            [to_local(unfold(w_out), 1, far), hidden_to_local(unfold(w_up), 1, far)], axis=1
        )
        up_width = w_up.shape[1] * 8
        up_cut = (width + up_width) // 2
        one = spread({OWN: far_one}, "x")
        two = spread({OWN: after(far_two, inputs_far)}, "ctx")
        first = list(one.values()) + list(two.values())
        one, two = spread(one, "ctx"), spread(two, "x")
        all_one = list(one.values()) + list(two.values())
        shard_down = after(to_local(unfold(w_down), 1, far), *first)
        near_down = order_blocks(spread({OWN: shard_down}, "ctx"), ["ctx"])
        far_up = gather_far(
            after(shard_up, *all_one), far, [up_cut, up_cut], [near_down]
        )
        one_core, two_core = spread(one, "core"), spread(two, "core")
        axes = ["core", "x", "ctx"]
        routes = [[(0, half_qkv, 0, 0), (half_qkv, 128, 1, 0)]] * 8
        qkv_one, small_local = assemble(
            list(one_core.values()),
            places(one_core, axes),
            [(width, half_qkv), (width, 128)],
            routes,
        )
        qkv_two_weight = order_blocks(two_core, axes)
        up_one = spread({OWN: after(far_up[0], *all_one)}, "x")
        up_two = spread({OWN: after(far_up[1], *all_one)}, "ctx")
        up_one = spread(tie_received(up_one, qkv_two_weight), "ctx")
        up_two = spread(tie_received(up_two, qkv_two_weight), "x")
        far_down = gather_far(after(near_down, far_up[0]), far)[0]

        devices = 8 * far
        small_core = small_local.reshape(devices, shard_rows, 128)[:, :small_rows, :near_width]
        small_core = small_core.astype(jnp.float32)
        small_all = to_natural(small_core, 0, far)
        query_bias, value_bias = (small_all[:, index].reshape(-1) for index in range(2))
        out_bias, first_gain, first_shift, second_gain, second_shift, down_bias = (
            small_core[:, index].reshape(-1) for index in range(2, 8)
        )
        up_bias = hidden_to_local(small_all[:, 8:].reshape(-1), 0, far)

        slot = jnp.arange(slots)
        earlier = slot[:, None] < slot[None, :]

        def ranks(own, other, other_first):
            inside = jnp.sum((own[:, None] == own[None, :]) & earlier, axis=0)
            outside = jnp.sum(other[:, None] == own[None, :], axis=0)
            return inside + jnp.where(other_first, outside, 0)

        rank_near = ranks(segment, segment_far, place == 1)
        rank_far = ranks(segment_far, segment, place == 0)

        def positions(ids, rank, image):
            return jnp.where(ids == image, rank, jnp.where(ids < 0, SEQ + rank, -1))

        row = jnp.arange(rows)
        spot_near = positions(segment, rank_near, place)
        spot_far = positions(segment_far, rank_far, place)
        pick_near = (spot_near[None, :] == row[:, None]).astype(jnp.bfloat16)
        pick_far = (spot_far[None, :] == row[:, None]).astype(jnp.bfloat16)
        spot_other = jnp.where(segment == 1 - place, rank_near, -1)
        give_near = (spot_near[:, None] == row[None, :]).astype(jnp.bfloat16)
        give_far = (spot_other[:, None] == row[None, :]).astype(jnp.bfloat16)
        column = jnp.arange(width)
        to_core = (column[:, None] == to_local(column, 0, far)[None, :]).astype(jnp.bfloat16)

        def take(near, other):
            picked = matmul(pick_near, near) + matmul(pick_far, other)
            return matmul(picked.astype(jnp.bfloat16), to_core)

        def to_give(array):
            natural = nt_dot(array.astype(jnp.bfloat16), to_core).astype(jnp.bfloat16)
            return natural, swap(natural)

        def give(both, *follow):
            near, other = both
            other = after(other, *follow) if follow else other
            return matmul(give_near, near) + matmul(give_far, other)

        kind = (row >= SEQ).astype(jnp.int32) + (row >= SEQ + pads).astype(jnp.int32)
        bias = jnp.where(kind[:, None] == kind[None, :], 0.0, -1e30).astype(jnp.float32)

        values_in = take(inputs, inputs_far)
        normal1, scale1 = standardize(values_in)
        normed1 = (normal1 * first_gain + first_shift).astype(jnp.bfloat16)
        joined_bias = [
            jnp.concatenate(
                [query_bias[cut], jnp.zeros((half_width,), jnp.float32), value_bias[cut]]
            )
            for cut in (slice(0, half_width), slice(half_width, width))
        ]
        joined_one = project(normed1, qkv_one, joined_bias[0])
        attended, log_one = attention_forward(
            after(joined_one, qkv_two_weight), bias, width, 0
        )
        joined_two = project(after(normed1, log_one), qkv_two_weight, joined_bias[1])
        up_one, up_two = tie_received(up_one, log_one), tie_received(up_two, log_one)
        up_near = assemble(
            list(up_one.values()) + list(up_two.values()),
            places(up_one, ["x", "ctx"]) + places(up_two, ["x", "ctx"]),
            [(half_width, width + up_width)],
            [[(0, up_cut, 0, 0)]] * 4 + [[(0, up_cut, 0, up_cut)]] * 4,
        )[0]
        up_blocks = spread({OWN: up_near}, "core")
        attended, log_two = attention_forward(
            joined_two, bias, width, half_width // PAIR, attended
        )
        cotangent_far = swap(after(cotangent, up_near))
        down_blocks = spread({OWN: after(far_down, up_near)}, "x")
        out_rows, up_weight = assemble(
            list(up_blocks.values()),
            places(up_blocks, ["core"]),
            [(width, width), (width, up_width)],
            [[(0, width, 0, 0), (width, up_width, 1, 0)]] * 2,
        )
        out_weight = to_natural(out_rows, 0, far)
        middle = values_in + matmul(attended, out_weight) + out_bias
        normal2, scale2 = standardize(middle)
        normed2 = (normal2 * second_gain + second_shift).astype(jnp.bfloat16)
        active, slope = hidden_layer(normed2, up_weight, up_bias)

        live = (row < SEQ).astype(jnp.float32)[:, None]
        d_out_low = (take(cotangent, cotangent_far) * live).astype(jnp.bfloat16)
        down_core = trade(gradient(active, d_out_low, 1 - core), "core")
        down_blocks = {key: after(block, active) for key, block in down_blocks.items()}
        down_weight = order_blocks(spread(down_blocks, "core"), ["core", "x"])
        last = last_layer(active, down_weight, middle, down_bias)
        last_given = to_give(last)
        down_x = send_half(
            gradient(active, d_out_low, core, got=after(down_core, last_given[0])), "x"
        )
        d_hidden, up_sums = d_hidden_layer(after(d_out_low, down_x[0]), down_weight, slope)
        up_core = [
            trade(gradient(normed2, d_hidden, 1 - core, side, 2), "core") for side in range(2)
        ]
        d_middle, d_branch, sums_two = norm_back(
            d_hidden, up_weight, normal2, scale2, second_gain, d_out_low, keep=True
        )
        up_kept = [
            gradient(normed2, d_hidden, core, side, 2, after(up_core[side], d_branch))
            for side in range(2)
        ]
        up_one = send_half(up_kept[0], "ctx", 2)
        up_two = send_half(up_kept[1], "x")
        d_branch = after(d_branch, up_one[0], up_two[0])
        grad_out = to_local(matmul(attended.T, d_branch).astype(jnp.bfloat16), 0, far)
        out_core = send_half(grad_out, "core")
        d_attended = matmul(d_branch, out_weight.T).astype(jnp.bfloat16)
        outputs = give(last_given, d_attended).astype(jnp.bfloat16)
        out_x = send_half(add_half(out_core, d_attended), "x")
        down_far = send_far(add_half(down_x, d_attended), far)
        d_attended = after(d_attended, out_x[0], down_far[0])
        d_one = attention_backward(joined_one, d_attended, 0, log_one, bias)
        one_core = trade(gradient(normed1, d_one, 1 - core), "core")
        partial = d_normed(d_one, qkv_one)
        up_one = send_half(add_half(up_one, partial), "x")
        up_two = send_half(add_half(up_two, partial), "ctx")
        d_attended = after(d_attended, partial, up_one[0], up_two[0])
        d_two = attention_backward(joined_two, d_attended, half_width // PAIR, log_two, bias)
        two_core = trade(gradient(normed1, d_two, 1 - core), "core")
        qkv_one_x = send_half(gradient(normed1, d_one, core, got=after(one_core, d_two)), "x")
        down_y = send_half(add_far(down_far, d_two).astype(jnp.bfloat16), "ctx")
        out_y = send_half(add_half(out_x, d_two), "ctx")
        up_halves = [add_half(halves, d_two) for halves in (up_one, up_two)]
        d_two_tied = after(d_two, qkv_one_x[0], down_y[0], out_y[0], *up_halves)
        d_last, sums_one = norm_back(
            d_two_tied, qkv_two_weight, normal1, scale1, first_gain, d_middle, base=partial
        )
        d_last_given = to_give(d_last)
        qkv_two = gradient(normed1, d_two, core, got=after(two_core, d_last))

        vectors = [
            sums_two[2],
            sums_one[0],
            sums_one[1],
            sums_two[0],
            sums_two[1],
            column_sums(d_out_low),
        ]
        joined_vectors = [
            jnp.concatenate([column_sums(d_one[index]), column_sums(d_two[index])])
            for index in (0, 2)
        ]
        vectors = [to_local(vector, 0, far) for vector in joined_vectors] + vectors
        table = jnp.stack([vector.reshape(devices, near_width) for vector in vectors], axis=1)
        up_sums = to_local(hidden_to_natural(up_sums[0], 0, far), 0, far)
        table = jnp.concatenate([table, up_sums.reshape(devices, -1, near_width)], axis=1)
        table = pad_small(table).reshape(width, 128).astype(jnp.bfloat16)
        qkv_two_x = send_half(qkv_two, "x")
        up_far = jnp.concatenate([*up_halves, add_half(out_y, d_last)], axis=1)
        up_far = send_far(up_far, far)
        qkv_one_y = send_half(
            add_half(qkv_one_x, d_last_given[0], qkv_two_x[0], up_far[0]), "ctx"
        )
        table = send_half(add_half(send_half(table, "core")), "x")
        qkv_two = jnp.concatenate([add_half(qkv_two_x), add_half(table)], axis=1)
        qkv_two_y = send_half(qkv_two, "ctx")
        qkv_one_far = send_far(add_half(qkv_one_y), far)
        qkv_two_far = send_far(add_half(qkv_two_y), far)

        sum_down = add_half(down_y, d_last_given[0]).astype(jnp.float32)
        sum_up = add_far(up_far, qkv_one_y[0])
        sum_up, sum_out = sum_up[:, :up_width], sum_up[:, up_width:]
        sum_one, sum_two = add_far(qkv_one_far), add_far(qkv_two_far)
        small_sums = sum_two[:small_rows, half_qkv : half_qkv + near_width]
        cut_qkv = lambda matrix: matrix[:, :half_qkv].reshape(shard_rows, 3, 1, half_width)
        sum_qkv = jnp.concatenate([cut_qkv(sum_one), cut_qkv(sum_two)], axis=2)
        sum_qkv = sum_qkv.reshape(shard_rows, 3 * width)
        input_grad = give(d_last_given)
        own = lambda index: small_sums[index]
        back = lambda matrix: refold(to_natural(matrix, 1, far))
        return (
            outputs,
            input_grad,
            refold(sum_qkv),
            own(0),
            own(1),
            back(sum_out),
            own(2),
            own(3),
            own(4),
            own(5),
            own(6),
            refold(hidden_to_natural(sum_up, 1, far)),
            small_sums[8:].reshape(-1),
            back(sum_down),
            own(7),
        )

    return on_device


def solution(mesh):
    if mesh.shape["ctx"] == IMAGES and mesh.shape["dp"] % 4 == 0:
        far, axes = mesh.shape["dp"] // 4, ("z", "x", "core", "ctx")
        mesh = jax.sharding.Mesh(mesh.devices.reshape(far, 2, 2, IMAGES), axes)
        body = by_image(far)
    else:
        body, axes = on_device, ("dp", "ctx")
    matrix, vector = P(axes, None), P(axes)
    return jax.shard_map(
        body,
        mesh=mesh,
        in_specs=(matrix, matrix, vector, matrix, vector, vector, matrix)
        + (vector,) * 5
        + (matrix, vector, matrix, vector),
        out_specs=(matrix, matrix, matrix, vector, vector, matrix)
        + (vector,) * 5
        + (matrix, vector, matrix, vector),
        check_vma=False,
    )
```

```python
import functools
import math

import jax
import jax.numpy as jnp
from jax import lax
from jax.experimental import pallas as pl
from jax.experimental.pallas import tpu as pltpu
from jax.sharding import PartitionSpec as P

HD = 64


EPSILON = 1e-06


def layer_norm(value, gain, shift):
    center = value - jnp.mean(value, axis=-1, keepdims=True)
    variance = jnp.mean(center * center, axis=-1, keepdims=True)
    return center * lax.rsqrt(variance + EPSILON) * gain + shift


def gelu_exact(value):
    return jax.nn.gelu(value, approximate=False)


def matmul(left, right):
    return jnp.dot(left, right, preferred_element_type=jnp.float32)


def unfold(stored):
    return stored.reshape(stored.shape[0] // 8, stored.shape[1] * 8)


def refold(matrix):
    return matrix.reshape(matrix.shape[0] * 8, matrix.shape[1] // 8)


def on_device(
    inputs,
    cotangent,
    segment,
    w_qkv,
    b_query,
    b_value,
    w_out,
    b_out,
    norm1_gain,
    norm1_shift,
    norm2_gain,
    norm2_shift,
    w_up,
    b_up,
    w_down,
    b_down,
):
    gathered = (
        lax.all_gather(w_qkv, ("dp", "ctx"), axis=0, tiled=True),
        lax.all_gather(b_query, ("dp", "ctx"), axis=0, tiled=True),
        lax.all_gather(b_value, ("dp", "ctx"), axis=0, tiled=True),
        lax.all_gather(w_out, ("dp", "ctx"), axis=0, tiled=True),
        lax.all_gather(b_out, ("dp", "ctx"), axis=0, tiled=True),
        lax.all_gather(norm1_gain, ("dp", "ctx"), axis=0, tiled=True),
        lax.all_gather(norm1_shift, ("dp", "ctx"), axis=0, tiled=True),
        lax.all_gather(norm2_gain, ("dp", "ctx"), axis=0, tiled=True),
        lax.all_gather(norm2_shift, ("dp", "ctx"), axis=0, tiled=True),
        lax.all_gather(w_up, ("dp", "ctx"), axis=0, tiled=True),
        lax.all_gather(b_up, ("dp", "ctx"), axis=0, tiled=True),
        lax.all_gather(w_down, ("dp", "ctx"), axis=0, tiled=True),
        lax.all_gather(b_down, ("dp", "ctx"), axis=0, tiled=True),
    )
    (
        qkv_stored,
        query_bias,
        value_bias,
        out_stored,
        out_bias,
        gain_one,
        shift_one,
        gain_two,
        shift_two,
        up_stored,
        up_bias,
        down_stored,
        down_bias,
    ) = gathered
    qkv_weight = unfold(qkv_stored)
    out_weight = unfold(out_stored)
    up_weight = unfold(up_stored)
    down_weight = unfold(down_stored)
    first_gain = gain_one.astype(jnp.float32)
    first_shift = shift_one.astype(jnp.float32)
    second_gain = gain_two.astype(jnp.float32)
    second_shift = shift_two.astype(jnp.float32)
    row_count = inputs.shape[0]
    model_width = out_weight.shape[0]
    head_count = model_width // HD
    score_scale = 1.0 / math.sqrt(HD)
    values_in = inputs.astype(jnp.float32)
    normed1 = layer_norm(values_in, first_gain, first_shift).astype(jnp.bfloat16)
    joined = matmul(normed1, qkv_weight)
    queries = (joined[:, :model_width] + query_bias.astype(jnp.float32)).astype(jnp.bfloat16)
    key_rows = joined[:, model_width : 2 * model_width].astype(jnp.bfloat16)
    value_rows = (joined[:, 2 * model_width :] + value_bias.astype(jnp.float32)).astype(
        jnp.bfloat16
    )
    key_all, value_all, seg_all = (
        lax.all_gather(key_rows, "ctx", axis=0, tiled=True),
        lax.all_gather(value_rows, "ctx", axis=0, tiled=True),
        lax.all_gather(segment.astype(jnp.bfloat16), "ctx", axis=0, tiled=True),
    )
    key_count = key_all.shape[0]
    query_heads = queries.reshape(row_count, head_count, HD)
    key_heads = key_all.reshape(key_count, head_count, HD)
    value_heads = value_all.reshape(key_count, head_count, HD)
    own_seg = segment.astype(jnp.float32)
    group_seg = seg_all.astype(jnp.float32)
    same_seg = own_seg[:, None] == group_seg[None, :]

    def make_scores():
        raw = (
            jnp.einsum("qhd,khd->hqk", query_heads, key_heads, preferred_element_type=jnp.float32)
            * score_scale
        )
        return jnp.where(same_seg[None], raw, -1e30)

    scores = make_scores()
    row_max = jnp.max(scores, axis=-1, keepdims=True)
    expo = jnp.exp(scores - row_max)
    row_total = jnp.sum(expo, axis=-1, keepdims=True)
    probs_low = (expo / row_total).astype(jnp.bfloat16)
    log_total = row_max + jnp.log(row_total)
    mixed = jnp.einsum("hqk,khd->qhd", probs_low, value_heads, preferred_element_type=jnp.float32)
    attended = mixed.reshape(row_count, model_width).astype(jnp.bfloat16)
    middle = values_in + matmul(attended, out_weight) + out_bias.astype(jnp.float32)
    normed2 = layer_norm(middle, second_gain, second_shift).astype(jnp.bfloat16)
    hidden = matmul(normed2, up_weight) + up_bias.astype(jnp.float32)
    active = gelu_exact(hidden).astype(jnp.bfloat16)
    outputs = (middle + matmul(active, down_weight) + down_bias.astype(jnp.float32)).astype(
        jnp.bfloat16
    )
    back_qkv, back_out, back_up, back_down = (qkv_weight, out_weight, up_weight, down_weight)
    valid = (segment >= 0).astype(jnp.float32)[:, None]
    d_out = cotangent.astype(jnp.float32) * valid
    d_out_low = d_out.astype(jnp.bfloat16)
    grad_down = refold(matmul(active.T, d_out_low))
    grad_down_bias = jnp.sum(d_out_low.astype(jnp.float32), axis=0)
    d_active = matmul(d_out_low, back_down.T)
    gelu_value, gelu_pull = jax.vjp(gelu_exact, hidden)
    d_hidden = gelu_pull(d_active)[0].astype(jnp.bfloat16)
    grad_up = refold(matmul(normed2.T, d_hidden))
    grad_up_bias = jnp.sum(d_hidden.astype(jnp.float32), axis=0)
    d_normed2 = matmul(d_hidden, back_up.T)
    norm_value, norm_pull = jax.vjp(layer_norm, middle, second_gain, second_shift)
    d_middle_norm, grad_gain_two, grad_shift_two = norm_pull(d_normed2)
    d_middle = d_out + d_middle_norm
    d_branch = d_middle.astype(jnp.bfloat16)
    grad_out = refold(matmul(attended.T, d_branch))
    grad_out_bias = jnp.sum(d_branch.astype(jnp.float32), axis=0)
    d_attended_flat = matmul(d_branch, back_out.T).astype(jnp.bfloat16)
    d_attended = d_attended_flat.reshape(row_count, head_count, HD)
    scores = make_scores()
    probs = jnp.exp(scores - log_total)
    d_probs = jnp.einsum(
        "qhd,khd->hqk", d_attended, value_heads, preferred_element_type=jnp.float32
    )
    delta_rows = jnp.sum(probs * d_probs, axis=-1, keepdims=True)
    d_scores = (probs * (d_probs - delta_rows)).astype(jnp.bfloat16)
    d_query = (
        jnp.einsum("hqk,khd->qhd", d_scores, key_heads, preferred_element_type=jnp.float32)
        * score_scale
    ).reshape(row_count, model_width)
    probs_again = probs.astype(jnp.bfloat16)
    d_key_all = (
        jnp.einsum("hqk,qhd->khd", d_scores, query_heads, preferred_element_type=jnp.float32)
        * score_scale
    ).reshape(key_count, model_width)
    d_value_all = jnp.einsum(
        "hqk,qhd->khd", probs_again, d_attended, preferred_element_type=jnp.float32
    ).reshape(key_count, model_width)
    d_key, d_value = (
        lax.psum_scatter(
            d_key_all.astype(jnp.bfloat16), "ctx", scatter_dimension=0, tiled=True
        ).astype(jnp.float32),
        lax.psum_scatter(
            d_value_all.astype(jnp.bfloat16), "ctx", scatter_dimension=0, tiled=True
        ).astype(jnp.float32),
    )
    d_query_low = d_query.astype(jnp.bfloat16)
    d_value_low = d_value.astype(jnp.bfloat16)
    d_joined = jnp.concatenate([d_query_low, d_key.astype(jnp.bfloat16), d_value_low], axis=1)
    grad_qkv = refold(matmul(normed1.T, d_joined))
    grad_query_bias = jnp.sum(d_query_low.astype(jnp.float32), axis=0)
    grad_value_bias = jnp.sum(d_value_low.astype(jnp.float32), axis=0)
    d_normed1 = matmul(d_joined, back_qkv.T)
    first_value, first_pull = jax.vjp(layer_norm, values_in, first_gain, first_shift)
    d_input_norm, grad_gain_one, grad_shift_one = first_pull(d_normed1)
    input_grad = d_middle + d_input_norm
    partial_sums = (
        lax.psum_scatter(
            grad_qkv.astype(jnp.bfloat16), "dp", scatter_dimension=0, tiled=True
        ).astype(jnp.float32),
        lax.psum_scatter(
            grad_query_bias.astype(jnp.bfloat16), "dp", scatter_dimension=0, tiled=True
        ).astype(jnp.float32),
        lax.psum_scatter(
            grad_value_bias.astype(jnp.bfloat16), "dp", scatter_dimension=0, tiled=True
        ).astype(jnp.float32),
        lax.psum_scatter(
            grad_out.astype(jnp.bfloat16), "dp", scatter_dimension=0, tiled=True
        ).astype(jnp.float32),
        lax.psum_scatter(
            grad_out_bias.astype(jnp.bfloat16), "dp", scatter_dimension=0, tiled=True
        ).astype(jnp.float32),
        lax.psum_scatter(
            grad_gain_one.astype(jnp.bfloat16), "dp", scatter_dimension=0, tiled=True
        ).astype(jnp.float32),
        lax.psum_scatter(
            grad_shift_one.astype(jnp.bfloat16), "dp", scatter_dimension=0, tiled=True
        ).astype(jnp.float32),
        lax.psum_scatter(
            grad_gain_two.astype(jnp.bfloat16), "dp", scatter_dimension=0, tiled=True
        ).astype(jnp.float32),
        lax.psum_scatter(
            grad_shift_two.astype(jnp.bfloat16), "dp", scatter_dimension=0, tiled=True
        ).astype(jnp.float32),
        lax.psum_scatter(
            grad_up.astype(jnp.bfloat16), "dp", scatter_dimension=0, tiled=True
        ).astype(jnp.float32),
        lax.psum_scatter(
            grad_up_bias.astype(jnp.bfloat16), "dp", scatter_dimension=0, tiled=True
        ).astype(jnp.float32),
        lax.psum_scatter(
            grad_down.astype(jnp.bfloat16), "dp", scatter_dimension=0, tiled=True
        ).astype(jnp.float32),
        lax.psum_scatter(
            grad_down_bias.astype(jnp.bfloat16), "dp", scatter_dimension=0, tiled=True
        ).astype(jnp.float32),
    )
    all_sums = (
        lax.psum_scatter(
            partial_sums[0].astype(jnp.bfloat16), "ctx", scatter_dimension=0, tiled=True
        ).astype(jnp.float32),
        lax.psum_scatter(
            partial_sums[1].astype(jnp.bfloat16), "ctx", scatter_dimension=0, tiled=True
        ).astype(jnp.float32),
        lax.psum_scatter(
            partial_sums[2].astype(jnp.bfloat16), "ctx", scatter_dimension=0, tiled=True
        ).astype(jnp.float32),
        lax.psum_scatter(
            partial_sums[3].astype(jnp.bfloat16), "ctx", scatter_dimension=0, tiled=True
        ).astype(jnp.float32),
        lax.psum_scatter(
            partial_sums[4].astype(jnp.bfloat16), "ctx", scatter_dimension=0, tiled=True
        ).astype(jnp.float32),
        lax.psum_scatter(
            partial_sums[5].astype(jnp.bfloat16), "ctx", scatter_dimension=0, tiled=True
        ).astype(jnp.float32),
        lax.psum_scatter(
            partial_sums[6].astype(jnp.bfloat16), "ctx", scatter_dimension=0, tiled=True
        ).astype(jnp.float32),
        lax.psum_scatter(
            partial_sums[7].astype(jnp.bfloat16), "ctx", scatter_dimension=0, tiled=True
        ).astype(jnp.float32),
        lax.psum_scatter(
            partial_sums[8].astype(jnp.bfloat16), "ctx", scatter_dimension=0, tiled=True
        ).astype(jnp.float32),
        lax.psum_scatter(
            partial_sums[9].astype(jnp.bfloat16), "ctx", scatter_dimension=0, tiled=True
        ).astype(jnp.float32),
        lax.psum_scatter(
            partial_sums[10].astype(jnp.bfloat16), "ctx", scatter_dimension=0, tiled=True
        ).astype(jnp.float32),
        lax.psum_scatter(
            partial_sums[11].astype(jnp.bfloat16), "ctx", scatter_dimension=0, tiled=True
        ).astype(jnp.float32),
        lax.psum_scatter(
            partial_sums[12].astype(jnp.bfloat16), "ctx", scatter_dimension=0, tiled=True
        ).astype(jnp.float32),
    )
    (
        sum_qkv,
        sum_query_bias,
        sum_value_bias,
        sum_out,
        sum_out_bias,
        sum_gain_one,
        sum_shift_one,
        sum_gain_two,
        sum_shift_two,
        sum_up,
        sum_up_bias,
        sum_down,
        sum_down_bias,
    ) = all_sums
    return (
        outputs,
        input_grad,
        sum_qkv,
        sum_query_bias,
        sum_value_bias,
        sum_out,
        sum_out_bias,
        sum_gain_one,
        sum_shift_one,
        sum_gain_two,
        sum_shift_two,
        sum_up,
        sum_up_bias,
        sum_down,
        sum_down_bias,
    )


SEQ = 577
IMAGES = 2
PAIR = 2 * HD
CHUNK = 256
BLOCK = 512
HINT = pl.CostEstimate(flops=1, bytes_accessed=1, transcendentals=0)
ERFC = (
    0.09873409569263458,
    0.09871950000524521,
    0.09271052479743958,
    0.08134904503822327,
    0.056456614285707474,
    0.07422702759504318,
    -0.050631966441869736,
    0.11820460855960846,
    -0.09110676497220993,
    0.021337319165468216,
)
ERFC_STEP = 0.35


def round_up(count, unit):
    return -(-count // unit) * unit


def limit(mebibytes):
    return pltpu.CompilerParams(vmem_limit_bytes=mebibytes * 2**20)


def chunks_of(count):
    return [(start, min(CHUNK, count - start)) for start in range(0, count, CHUNK)]


def nt_dot(left, right):
    return lax.dot_general(
        left, right, (((1,), (1,)), ((), ())), preferred_element_type=jnp.float32
    )


def tn_dot(left, right):
    return lax.dot_general(
        left, right, (((0,), (0,)), ((), ())), preferred_element_type=jnp.float32
    )


def half_mask(rows):
    return lax.broadcasted_iota(jnp.int32, (rows, PAIR), 1) < HD


def forward_kernel(query_ref, key_ref, value_ref, bias_ref, *refs):
    attended_ref, log_ref = refs[-2:]
    rows = query_ref.shape[1]
    first = half_mask(rows)
    zero = jnp.zeros((rows, PAIR), jnp.bfloat16)
    key = key_ref[0]
    key_sides = (jnp.where(first, key, zero), jnp.where(first, zero, key))
    value_t = value_ref[0].astype(jnp.float32).T.astype(jnp.bfloat16)
    scale = jnp.bfloat16(1.0 / math.sqrt(HD))
    for start, size in chunks_of(rows):
        query = query_ref[0, start : start + size, :] * scale
        bias = bias_ref[:, start : start + size]
        outs = []
        for side in range(2):
            scores = nt_dot(key_sides[side], query) + bias
            top = jnp.max(scores, axis=0, keepdims=True)
            expo = jnp.exp(scores - top)
            total = jnp.sum(expo, axis=0, keepdims=True)
            probs_low = (expo * (1.0 / total)).astype(jnp.bfloat16)
            outs.append(matmul(value_t[side * HD : (side + 1) * HD, :], probs_low))
            log_ref[0, side : side + 1, start : start + size] = top + jnp.log(total)
        mixed = jnp.concatenate(outs, axis=0)
        attended_ref[start : start + size, :] = mixed.T.astype(jnp.bfloat16)


def backward_kernel(
    query_ref, key_ref, value_ref, d_ref, log_ref, bias_ref, joined_ref, dk_sum, dv_sum
):
    rows = query_ref.shape[1]
    first = half_mask(rows)
    zero = jnp.zeros((rows, PAIR), jnp.bfloat16)
    key = key_ref[0]
    value = value_ref[0]
    key_sides = (jnp.where(first, key, zero), jnp.where(first, zero, key))
    value_sides = (jnp.where(first, value, zero), jnp.where(first, zero, value))
    key_t = key.astype(jnp.float32).T.astype(jnp.bfloat16)
    scale = jnp.bfloat16(1.0 / math.sqrt(HD))
    for start, size in chunks_of(rows):
        query = query_ref[0, start : start + size, :] * scale
        d_rows = d_ref[start : start + size, :]
        bias = bias_ref[:, start : start + size]
        outs = []
        for side in range(2):
            scores = nt_dot(key_sides[side], query) + bias
            probs = jnp.exp(scores - log_ref[0, side : side + 1, start : start + size])
            d_probs = nt_dot(value_sides[side], d_rows)
            product = probs * d_probs
            delta = jnp.sum(product, axis=0, keepdims=True)
            d_scores = (product - probs * delta).astype(jnp.bfloat16)
            d_value = matmul(probs.astype(jnp.bfloat16), d_rows)
            d_key = matmul(d_scores, query)
            if start == 0:
                dv_sum[side] = d_value
                dk_sum[side] = d_key
            else:
                dv_sum[side] += d_value
                dk_sum[side] += d_key
            outs.append(matmul(key_t[side * HD : (side + 1) * HD, :], d_scores))
        d_query = jnp.concatenate(outs, axis=0) * (1.0 / math.sqrt(HD))
        joined_ref[0, start : start + size, :] = d_query.T.astype(jnp.bfloat16)
    joined_ref[1] = jnp.where(first, dk_sum[0], dk_sum[1]).astype(jnp.bfloat16)
    joined_ref[2] = jnp.where(first, dv_sum[0], dv_sum[1]).astype(jnp.bfloat16)


def pair_spec(rows, part):
    return pl.BlockSpec((1, rows, PAIR), lambda i: (part, 0, i))


def attention_forward(joined, bias, total, first_pair, base=None):
    rows, width = joined.shape[1:]
    pairs = width // PAIR
    extra = [] if base is None else [base]
    return pl.pallas_call(
        forward_kernel,
        grid=(pairs,),
        in_specs=[pair_spec(rows, part) for part in range(3)]
        + [pl.BlockSpec((rows, rows), lambda i: (0, 0))]
        + [pl.BlockSpec(memory_space=pl.ANY) for _ in extra],
        out_specs=[
            pl.BlockSpec((rows, PAIR), lambda i: (0, first_pair + i)),
            pl.BlockSpec((1, 2, rows), lambda i: (i, 0, 0)),
        ],
        out_shape=[
            jax.ShapeDtypeStruct((rows, total), jnp.bfloat16),
            jax.ShapeDtypeStruct((pairs, 2, rows), jnp.float32),
        ],
        input_output_aliases={4: 0} if extra else {},
        compiler_params=limit(32),
        cost_estimate=HINT,
        name="attention_forward",
    )(joined, joined, joined, bias, *extra)


def attention_backward(joined, d_attended, first_pair, log_total, bias):
    rows, width = joined.shape[1:]
    return pl.pallas_call(
        backward_kernel,
        grid=(width // PAIR,),
        in_specs=[pair_spec(rows, part) for part in range(3)]
        + [
            pl.BlockSpec((rows, PAIR), lambda i: (0, first_pair + i)),
            pl.BlockSpec((1, 2, rows), lambda i: (i, 0, 0)),
            pl.BlockSpec((rows, rows), lambda i: (0, 0)),
        ],
        out_specs=pl.BlockSpec((3, rows, PAIR), lambda i: (0, 0, i)),
        out_shape=jax.ShapeDtypeStruct((3, rows, width), jnp.bfloat16),
        scratch_shapes=[pltpu.VMEM((2, rows, PAIR), jnp.float32)] * 2,
        compiler_params=limit(32),
        cost_estimate=HINT,
        name="attention_backward",
    )(joined, joined, joined, d_attended, log_total, bias)


def whole_spec(shape):
    return pl.BlockSpec(shape, lambda *_: (0,) * len(shape))


def project_kernel(x_ref, weight_ref, bias_ref, out_ref):
    out_ref[0] = (matmul(x_ref[...], weight_ref[...]) + bias_ref[...]).astype(out_ref.dtype)


def project(x, weight, bias):
    rows, depth = x.shape
    width = weight.shape[1] // 3
    return pl.pallas_call(
        project_kernel,
        grid=(3,),
        in_specs=[
            whole_spec(x.shape),
            pl.BlockSpec((depth, width), lambda i: (0, i)),
            pl.BlockSpec((1, width), lambda i: (0, i)),
        ],
        out_specs=pl.BlockSpec((1, rows, width), lambda i: (i, 0, 0)),
        out_shape=jax.ShapeDtypeStruct((3, rows, width), jnp.bfloat16),
        compiler_params=limit(24),
        cost_estimate=HINT,
        name="project",
    )(x, weight, bias[None, :])


def hidden_kernel(x_ref, weight_ref, bias_ref, active_ref, slope_ref):
    hidden = matmul(x_ref[...], weight_ref[...]) + bias_ref[...]
    share = 1.0 / (1.0 + (ERFC_STEP * math.sqrt(0.5)) * jnp.abs(hidden))
    density = jnp.exp(-0.5 * hidden * hidden)
    tail = jnp.full_like(share, ERFC[-1])
    for factor in ERFC[-2::-1]:
        tail = tail * share + factor
    tail = tail * share * density
    phi = jnp.where(hidden < 0.0, tail, 1.0 - tail)
    active_ref[...] = (hidden * phi).astype(jnp.bfloat16)
    slope = phi + hidden * density * (1.0 / math.sqrt(2.0 * math.pi))
    slope_ref[...] = slope.astype(jnp.bfloat16)


def hidden_layer(x, weight, bias):
    rows, depth = x.shape
    width = weight.shape[1]
    block = pl.BlockSpec((rows, BLOCK), lambda i: (0, i))
    return pl.pallas_call(
        hidden_kernel,
        grid=(width // BLOCK,),
        in_specs=[
            whole_spec(x.shape),
            pl.BlockSpec((depth, BLOCK), lambda i: (0, i)),
            pl.BlockSpec((1, BLOCK), lambda i: (0, i)),
        ],
        out_specs=[block, block],
        out_shape=[jax.ShapeDtypeStruct((rows, width), jnp.bfloat16)] * 2,
        compiler_params=limit(32),
        cost_estimate=HINT,
        name="hidden_layer",
    )(x, weight, bias[None, :])


def last_kernel(active_ref, weight_ref, middle_ref, bias_ref, out_ref, total):
    step = pl.program_id(0)

    @pl.when(step == 0)
    def _():
        total[...] = middle_ref[...] + bias_ref[...]

    total[...] += matmul(active_ref[...], weight_ref[...])

    @pl.when(step == pl.num_programs(0) - 1)
    def _():
        out_ref[...] = total[...].astype(out_ref.dtype)


def last_layer(active, weight, middle, bias):
    rows, depth = active.shape
    width = weight.shape[1]
    return pl.pallas_call(
        last_kernel,
        grid=(depth // BLOCK,),
        in_specs=[
            pl.BlockSpec((rows, BLOCK), lambda i: (0, i)),
            pl.BlockSpec((BLOCK, width), lambda i: (i, 0)),
            whole_spec((rows, width)),
            whole_spec((1, width)),
        ],
        out_specs=whole_spec((rows, width)),
        out_shape=jax.ShapeDtypeStruct((rows, width), jnp.bfloat16),
        scratch_shapes=[pltpu.VMEM((rows, width), jnp.float32)],
        compiler_params=limit(52),
        cost_estimate=HINT,
        name="last_layer",
    )(active, weight, middle, bias[None, :])


def d_hidden_kernel(d_ref, weight_ref, slope_ref, out_ref, sum_ref):
    d_active = nt_dot(d_ref[...], weight_ref[...])
    d_hidden = (d_active * slope_ref[...].astype(jnp.float32)).astype(jnp.bfloat16)
    out_ref[...] = d_hidden
    sum_ref[...] = jnp.sum(d_hidden.astype(jnp.float32), axis=0, keepdims=True)


def d_hidden_layer(d_out, weight, slope):
    rows, depth = d_out.shape
    width = weight.shape[0]
    block = pl.BlockSpec((rows, BLOCK), lambda i: (0, i))
    return pl.pallas_call(
        d_hidden_kernel,
        grid=(width // BLOCK,),
        in_specs=[
            whole_spec(d_out.shape),
            pl.BlockSpec((BLOCK, depth), lambda i: (i, 0)),
            block,
        ],
        out_specs=[block, pl.BlockSpec((1, BLOCK), lambda i: (0, i))],
        out_shape=[
            jax.ShapeDtypeStruct((rows, width), jnp.bfloat16),
            jax.ShapeDtypeStruct((1, width), jnp.float32),
        ],
        compiler_params=limit(24),
        cost_estimate=HINT,
        name="d_hidden_layer",
    )(d_out, weight, slope)


def d_normed_kernel(d_ref, weight_ref, *refs):
    out_ref = refs[-1]
    d_rows = d_ref[0] if len(d_ref.shape) == 3 else d_ref[...]
    product = nt_dot(d_rows, weight_ref[...])
    step = pl.program_id(0)

    @pl.when(step == 0)
    def _():
        out_ref[...] = product + refs[0][...] if len(refs) == 2 else product

    @pl.when(step > 0)
    def _():
        out_ref[...] += product


def d_normed(d_rows, weight, base=None):
    rows, depth = d_rows.shape[-2], weight.shape[0]
    if d_rows.ndim == 3:
        d_spec = pl.BlockSpec((1, rows, BLOCK), lambda i: (i, 0, 0))
    else:
        d_spec = pl.BlockSpec((rows, BLOCK), lambda i: (0, i))
    extra = [] if base is None else [base]
    return pl.pallas_call(
        d_normed_kernel,
        grid=(weight.shape[1] // BLOCK,),
        in_specs=[d_spec, pl.BlockSpec((depth, BLOCK), lambda i: (0, i))]
        + [whole_spec((rows, depth)) for _ in extra],
        out_specs=whole_spec((rows, depth)),
        out_shape=jax.ShapeDtypeStruct((rows, depth), jnp.float32),
        compiler_params=limit(24),
        cost_estimate=HINT,
        name="d_normed",
    )(d_rows, weight, *extra)


def norm_back_kernel(count, d_ref, weight_ref, *refs):
    base, (normal_ref, scale_ref, gain_ref, residual_ref) = refs[:count], refs[count : count + 4]
    *wide_refs, low_ref, sum_ref, total = refs[count + 4 :]
    d_rows = d_ref[0] if len(d_ref.shape) == 3 else d_ref[...]
    product = nt_dot(d_rows, weight_ref[...])
    step = pl.program_id(0)

    @pl.when(step == 0)
    def _():
        total[...] = product + base[0][...] if base else product

    @pl.when(step > 0)
    def _():
        total[...] += product

    @pl.when(step == pl.num_programs(0) - 1)
    def _():
        rows = total.shape[0]
        sums = [jnp.zeros((1, total.shape[1]), jnp.float32)] * 3
        for start, size in chunks_of(rows):
            part = slice(start, start + size)
            d_part, normal = total[part, :], normal_ref[part, :]
            along = d_part * normal
            scaled = d_part * gain_ref[...]
            mean = jnp.mean(scaled, axis=-1, keepdims=True)
            slope = jnp.mean(scaled * normal, axis=-1, keepdims=True)
            wide = (scaled - mean - normal * slope) * scale_ref[part, :]
            wide = wide + residual_ref[part, :].astype(jnp.float32)
            low = wide.astype(jnp.bfloat16)
            for wide_ref in wide_refs:
                wide_ref[part, :] = wide
            low_ref[part, :] = low
            for number, array in enumerate((along, d_part, low.astype(jnp.float32))):
                sums[number] = sums[number] + jnp.sum(array, axis=0, keepdims=True)
        for number, one in enumerate(sums):
            sum_ref[number : number + 1, :] = one


def norm_back(d_rows, weight, normal, scale, gain, residual, base=None, keep=False):
    rows, depth = d_rows.shape[-2], weight.shape[0]
    if d_rows.ndim == 3:
        d_spec = pl.BlockSpec((1, rows, BLOCK), lambda i: (i, 0, 0))
    else:
        d_spec = pl.BlockSpec((rows, BLOCK), lambda i: (0, i))
    extra = [] if base is None else [base]
    full = whole_spec((rows, depth))
    kinds = [jnp.float32] * keep + [jnp.bfloat16]
    return pl.pallas_call(
        functools.partial(norm_back_kernel, len(extra)),
        grid=(weight.shape[1] // BLOCK,),
        in_specs=[d_spec, pl.BlockSpec((depth, BLOCK), lambda i: (0, i))]
        + [full for _ in extra]
        + [full, whole_spec((rows, 1)), whole_spec((1, depth)), full],
        out_specs=[full for _ in kinds] + [whole_spec((8, depth))],
        out_shape=[jax.ShapeDtypeStruct((rows, depth), kind) for kind in kinds]
        + [jax.ShapeDtypeStruct((8, depth), jnp.float32)],
        scratch_shapes=[pltpu.VMEM((rows, depth), jnp.float32)],
        compiler_params=limit(40),
        cost_estimate=HINT,
        name="norm_back",
    )(d_rows, weight, *extra, normal, scale, gain[None, :], residual)


def gradient_kernel(index_ref, x_ref, d_ref, *refs):
    out_ref = refs[-1]
    x = x_ref[...]
    width = d_ref.shape[-1]
    for part in range(out_ref.shape[1] // width):
        columns = slice(part * width, (part + 1) * width)
        product = tn_dot(x, d_ref[part] if len(d_ref.shape) == 3 else d_ref[...])
        if len(refs) == 2:
            product = product + refs[0][:, columns].astype(jnp.float32)
        out_ref[:, columns] = product.astype(out_ref.dtype)


def gradient(x, d_rows, half, column=0, columns=1, got=None, runs=1):
    rows, depth = x.shape
    size = depth // 2
    blocks = size // CHUNK
    run = blocks // runs
    if d_rows.ndim == 3:
        d_spec = pl.BlockSpec(d_rows.shape, lambda i, index: (0, 0, 0))
        width = d_rows.shape[0] * d_rows.shape[2]
    else:
        width = d_rows.shape[1] // columns
        d_spec = pl.BlockSpec((rows, width), lambda i, index: (0, column))
    block = pl.BlockSpec((CHUNK, width), lambda i, index: (i, 0))
    extra = [] if got is None else [got]
    return pl.pallas_call(
        gradient_kernel,
        grid_spec=pltpu.PrefetchScalarGridSpec(
            num_scalar_prefetch=1,
            grid=(blocks,),
            in_specs=[
                pl.BlockSpec(
                    (rows, CHUNK),
                    lambda i, index: (0, (2 * (i // run) + index[0]) * run + i % run),
                ),
                d_spec,
            ]
            + [block for _ in extra],
            out_specs=block,
        ),
        out_shape=jax.ShapeDtypeStruct((size, width), jnp.bfloat16),
        compiler_params=limit(32),
        cost_estimate=HINT,
        name="gradient",
    )(half.reshape(1).astype(jnp.int32), x, d_rows, *extra)


def standardize(value):
    center = value - jnp.mean(value, axis=-1, keepdims=True)
    variance = jnp.mean(center * center, axis=-1, keepdims=True)
    scale = lax.rsqrt(variance + EPSILON)
    return center * scale, scale


def reorder(array, axis, sizes, spots):
    shape = array.shape
    count = math.prod(sizes)
    cut = shape[:axis] + tuple(sizes) + (shape[axis] // count,) + shape[axis + 1 :]
    spots = list(range(axis)) + [axis + spot for spot in spots]
    return array.reshape(cut).transpose(spots + list(range(len(spots), len(cut)))).reshape(shape)


def to_local(array, axis, far):
    return reorder(array, axis, (far, 2, 2, 2), (2, 1, 3, 0))


def to_natural(array, axis, far):
    return reorder(array, axis, (2, 2, 2, far), (3, 1, 0, 2))


def assemble_kernel(routes, index_ref, *refs):
    count = len(routes)
    pieces, stages = refs[:count], refs[-count - 2 : -2]
    wholes, (arrived, left) = refs[count : -count - 2], refs[-2:]
    incoming = [
        pltpu.make_async_copy(piece, stage, arrived.at[number])
        for number, (piece, stage) in enumerate(zip(pieces, stages))
    ]
    for copy in incoming:
        copy.start()
    outgoing = []
    for number, route in enumerate(routes):
        incoming[number].wait()
        size = pieces[number].shape[0]
        start = pl.multiple_of(index_ref[number] * size, 16)
        for part, (source, width, whole, target) in enumerate(route):
            copy = pltpu.make_async_copy(
                stages[number].at[:, pl.ds(source, width)],
                wholes[whole].at[pl.ds(start, size), pl.ds(target, width)],
                left.at[part, number],
            )
            copy.start()
            outgoing.append(copy)
    for copy in outgoing:
        copy.wait()


def assemble(pieces, indices, outs, routes=None):
    if routes is None:
        routes = [[(0, piece.shape[1], 0, 0)] for piece in pieces]
    count = len(pieces)
    anywhere = pl.BlockSpec(memory_space=pl.ANY)
    kind = pieces[0].dtype
    return pl.pallas_call(
        functools.partial(assemble_kernel, routes),
        in_specs=[pl.BlockSpec(memory_space=pltpu.SMEM)] + [anywhere] * count,
        out_specs=[anywhere] * len(outs),
        out_shape=[jax.ShapeDtypeStruct(shape, kind) for shape in outs],
        scratch_shapes=[pltpu.VMEM(piece.shape, kind) for piece in pieces]
        + [
            pltpu.SemaphoreType.DMA((count,)),
            pltpu.SemaphoreType.DMA((max(len(route) for route in routes), count)),
        ],
        compiler_params=limit(16),
        cost_estimate=HINT,
        name="assemble",
    )(jnp.stack(indices).astype(jnp.int32), *pieces)


def trade(array, axis):
    return lax.ppermute(array, axis, [(0, 1), (1, 0)])


def after(array, *others):
    return lax.optimization_barrier((array, *others))[0]


def gather_far(shard, far, widths=None, follow=()):
    place = lax.axis_index("z")
    pieces, indices = [shard], [place]
    for step in range(1, far):
        got = lax.ppermute(shard, "z", [(i, (i + step) % far) for i in range(far)])
        pieces.append(after(got, *follow) if follow else got)
        indices.append((place - step) % far)
    rows, width = shard.shape
    widths = widths or [width]
    route, column = [], 0
    for number, one in enumerate(widths):
        route.append((column, one, number, 0))
        column += one
    return assemble(pieces, indices, [(far * rows, one) for one in widths], [route] * far)


def spread(blocks, axis):
    return blocks | {key | {axis}: trade(block, axis) for key, block in blocks.items()}


def tie_received(blocks, other):
    return {key: after(block, other) if key else block for key, block in blocks.items()}


def places(blocks, axes):
    indices = []
    for key in blocks:
        index = 0
        for axis in axes:
            place = lax.axis_index(axis)
            index = 2 * index + (1 - place if axis in key else place)
        indices.append(index)
    return indices


def order_blocks(blocks, axes):
    pieces = list(blocks.values())
    rows, width = pieces[0].shape
    return assemble(pieces, places(blocks, axes), [(len(pieces) * rows, width)])[0]


OWN = frozenset()


def send_half(matrix, axis, outer=1):
    rows, width = matrix.shape
    place = lax.axis_index(axis)
    blocks = matrix.reshape(outer, 2, rows // (2 * outer), width)
    kept = lax.dynamic_index_in_dim(blocks, place, 1, False).reshape(rows // 2, width)
    sent = lax.dynamic_index_in_dim(blocks, 1 - place, 1, False).reshape(rows // 2, width)
    return kept, trade(sent, axis)


def add_half(halves, *follow):
    kept, got = halves
    got = after(got, *follow) if follow else got
    return (kept.astype(jnp.float32) + got.astype(jnp.float32)).astype(kept.dtype)


def send_far(matrix, far):
    size = matrix.shape[0] // far
    place = lax.axis_index("z")
    arrays = [lax.dynamic_slice_in_dim(matrix, place * size, size)]
    for step in range(1, far):
        sent = lax.dynamic_slice_in_dim(matrix, ((place + step) % far) * size, size)
        arrays.append(lax.ppermute(sent, "z", [(i, (i + step) % far) for i in range(far)]))
    return arrays


def add_far(arrays, *follow):
    own, *got = arrays
    if follow:
        got = [after(array, *follow) for array in got]
    return sum(array.astype(jnp.float32) for array in [own, *got])


def column_sums(array):
    return jnp.sum(array.astype(jnp.float32), axis=0)


def by_image(far):
    def on_device(
        inputs,
        cotangent,
        segment,
        w_qkv,
        b_query,
        b_value,
        w_out,
        b_out,
        norm1_gain,
        norm1_shift,
        norm2_gain,
        norm2_shift,
        w_up,
        b_up,
        w_down,
        b_down,
    ):
        place, core = lax.axis_index("ctx"), lax.axis_index("core")
        swap = lambda array: trade(array, "ctx")
        slots, width = inputs.shape
        half_width = width // 2
        pads = 2 * slots - IMAGES * SEQ
        rows = round_up(SEQ + pads, 16)
        near_width = w_up.shape[0] // 8

        inputs_far = swap(inputs)
        segment_far = swap(segment)
        shard_rows = w_qkv.shape[0] // 8
        small = [b_query, b_value, b_out, norm1_gain, norm1_shift, norm2_gain, norm2_shift, b_down]
        small = jnp.concatenate([jnp.stack(small), b_up.reshape(-1, near_width)], axis=0)
        small_rows = small.shape[0]
        pad_small = lambda table: jnp.pad(
            table,
            [(0, 0)] * (table.ndim - 2)
            + [(0, shard_rows - small_rows), (0, 128 - near_width)],
        )
        small = pad_small(small)
        shard_qkv = unfold(w_qkv).reshape(shard_rows, 3, 2, half_width)
        halves = [shard_qkv[:, :, side].reshape(shard_rows, 3 * half_width) for side in range(2)]
        half_qkv = 3 * half_width
        far_one, far_two = gather_far(
            jnp.concatenate([halves[0], small, halves[1]], axis=1), far, [half_qkv + 128, half_qkv]
        )
        shard_up = jnp.concatenate(
            [to_local(unfold(w_out), 1, far), unfold(w_up)], axis=1
        )
        up_width = w_up.shape[1] * 8
        up_cut = (width + up_width) // 2
        one = spread({OWN: far_one}, "x")
        two = spread({OWN: after(far_two, inputs_far)}, "ctx")
        first = list(one.values()) + list(two.values())
        one, two = spread(one, "ctx"), spread(two, "x")
        all_one = list(one.values()) + list(two.values())
        one_core, two_core = spread(one, "core"), spread(two, "core")
        all_core = list(one_core.values()) + list(two_core.values())
        far_up = gather_far(after(shard_up, *all_core), far, [up_cut, up_cut])
        down_weight = lax.all_gather(
            after(to_local(unfold(w_down), 1, far), *all_one),
            ("z", "x", "core", "ctx"),
            axis=0,
            tiled=True,
        )
        axes = ["core", "x", "ctx"]
        routes = [[(0, half_qkv, 0, 0), (half_qkv, 128, 1, 0)]] * 8
        qkv_one, small_local = assemble(
            list(one_core.values()),
            places(one_core, axes),
            [(width, half_qkv), (width, 128)],
            routes,
        )
        qkv_two_weight = order_blocks(two_core, axes)
        up_one = spread({OWN: after(far_up[0], *all_one)}, "x")
        up_two = spread({OWN: after(far_up[1], *all_one)}, "ctx")
        up_one = spread(tie_received(up_one, qkv_two_weight), "ctx")
        up_two = spread(tie_received(up_two, qkv_two_weight), "x")

        devices = 8 * far
        small_core = small_local.reshape(devices, shard_rows, 128)[:, :small_rows, :near_width]
        small_core = small_core.astype(jnp.float32)
        small_all = to_natural(small_core, 0, far)
        query_bias, value_bias = (small_all[:, index].reshape(-1) for index in range(2))
        out_bias, first_gain, first_shift, second_gain, second_shift, down_bias = (
            small_core[:, index].reshape(-1) for index in range(2, 8)
        )
        up_bias = small_all[:, 8:].reshape(-1)

        slot = jnp.arange(slots)
        earlier = slot[:, None] < slot[None, :]

        def ranks(own, other, other_first):
            inside = jnp.sum((own[:, None] == own[None, :]) & earlier, axis=0)
            outside = jnp.sum(other[:, None] == own[None, :], axis=0)
            return inside + jnp.where(other_first, outside, 0)

        rank_near = ranks(segment, segment_far, place == 1)
        rank_far = ranks(segment_far, segment, place == 0)

        def positions(ids, rank, image):
            return jnp.where(ids == image, rank, jnp.where(ids < 0, SEQ + rank, -1))

        row = jnp.arange(rows)
        spot_near = positions(segment, rank_near, place)
        spot_far = positions(segment_far, rank_far, place)
        pick_near = (spot_near[None, :] == row[:, None]).astype(jnp.bfloat16)
        pick_far = (spot_far[None, :] == row[:, None]).astype(jnp.bfloat16)
        spot_other = jnp.where(segment == 1 - place, rank_near, -1)
        give_near = (spot_near[:, None] == row[None, :]).astype(jnp.bfloat16)
        give_far = (spot_other[:, None] == row[None, :]).astype(jnp.bfloat16)
        column = jnp.arange(width)
        to_core = (column[:, None] == to_local(column, 0, far)[None, :]).astype(jnp.bfloat16)

        def take(near, other):
            picked = matmul(pick_near, near) + matmul(pick_far, other)
            return matmul(picked.astype(jnp.bfloat16), to_core)

        def to_give(array):
            natural = nt_dot(array.astype(jnp.bfloat16), to_core).astype(jnp.bfloat16)
            return natural, swap(natural)

        def give(both, *follow):
            near, other = both
            other = after(other, *follow) if follow else other
            return matmul(give_near, near) + matmul(give_far, other)

        kind = (row >= SEQ).astype(jnp.int32) + (row >= SEQ + pads).astype(jnp.int32)
        bias = jnp.where(kind[:, None] == kind[None, :], 0.0, -1e30).astype(jnp.float32)

        values_in = take(inputs, inputs_far)
        normal1, scale1 = standardize(values_in)
        normed1 = (normal1 * first_gain + first_shift).astype(jnp.bfloat16)
        joined_bias = [
            jnp.concatenate(
                [query_bias[cut], jnp.zeros((half_width,), jnp.float32), value_bias[cut]]
            )
            for cut in (slice(0, half_width), slice(half_width, width))
        ]
        joined_one = project(normed1, qkv_one, joined_bias[0])
        attended, log_one = attention_forward(
            after(joined_one, qkv_two_weight), bias, width, 0
        )
        joined_two = project(after(normed1, log_one), qkv_two_weight, joined_bias[1])
        attended, log_two = attention_forward(
            joined_two, bias, width, half_width // PAIR, attended
        )
        up_one, up_two = tie_received(up_one, log_two), tie_received(up_two, log_two)
        up_near = assemble(
            list(up_one.values()) + list(up_two.values()),
            places(up_one, ["x", "ctx"]) + places(up_two, ["x", "ctx"]),
            [(half_width, width + up_width)],
            [[(0, up_cut, 0, 0)]] * 4 + [[(0, up_cut, 0, up_cut)]] * 4,
        )[0]
        up_blocks = spread({OWN: up_near}, "core")
        cotangent_far = swap(after(cotangent, up_near))
        out_rows, up_weight = assemble(
            list(up_blocks.values()),
            places(up_blocks, ["core"]),
            [(width, width), (width, up_width)],
            [[(0, width, 0, 0), (width, up_width, 1, 0)]] * 2,
        )
        out_weight = to_natural(out_rows, 0, far)
        middle = values_in + matmul(attended, out_weight) + out_bias
        normal2, scale2 = standardize(middle)
        normed2 = (normal2 * second_gain + second_shift).astype(jnp.bfloat16)
        active, slope = hidden_layer(normed2, up_weight, up_bias)

        live = (row < SEQ).astype(jnp.float32)[:, None]
        d_out_low = (take(cotangent, cotangent_far) * live).astype(jnp.bfloat16)
        down_core = trade(gradient(active, d_out_low, 1 - core, runs=2 * far), "core")
        last = last_layer(active, down_weight, middle, down_bias)
        last_given = to_give(last)
        down_x = send_half(
            gradient(
                active, d_out_low, core, got=after(down_core, last_given[0]), runs=2 * far
            ),
            "x",
            far,
        )
        d_hidden, up_sums = d_hidden_layer(after(d_out_low, down_x[0]), down_weight, slope)
        up_core = [
            trade(gradient(normed2, d_hidden, 1 - core, side, 2), "core") for side in range(2)
        ]
        d_middle, d_branch, sums_two = norm_back(
            d_hidden, up_weight, normal2, scale2, second_gain, d_out_low, keep=True
        )
        up_kept = [
            gradient(normed2, d_hidden, core, side, 2, after(up_core[side], d_branch))
            for side in range(2)
        ]
        up_one = send_half(up_kept[0], "ctx", 2)
        up_two = send_half(up_kept[1], "x")
        d_branch = after(d_branch, up_one[0], up_two[0])
        grad_out = to_local(matmul(attended.T, d_branch).astype(jnp.bfloat16), 0, far)
        out_core = send_half(grad_out, "core")
        d_attended = matmul(d_branch, out_weight.T).astype(jnp.bfloat16)
        outputs = give(last_given, d_attended).astype(jnp.bfloat16)
        out_x = send_half(add_half(out_core, d_attended), "x")
        down_far = send_far(add_half(down_x, d_attended), far)
        d_attended = after(d_attended, out_x[0], down_far[0])
        d_one = attention_backward(joined_one, d_attended, 0, log_one, bias)
        one_core = trade(gradient(normed1, d_one, 1 - core), "core")
        partial = d_normed(d_one, qkv_one)
        up_one = send_half(add_half(up_one, partial), "x")
        up_two = send_half(add_half(up_two, partial), "ctx")
        d_attended = after(d_attended, partial, up_one[0], up_two[0])
        d_two = attention_backward(joined_two, d_attended, half_width // PAIR, log_two, bias)
        two_core = trade(gradient(normed1, d_two, 1 - core), "core")
        qkv_one_x = send_half(gradient(normed1, d_one, core, got=after(one_core, d_two)), "x")
        down_y = send_half(add_far(down_far, d_two).astype(jnp.bfloat16), "ctx")
        out_y = send_half(add_half(out_x, d_two), "ctx")
        up_halves = [add_half(halves, d_two) for halves in (up_one, up_two)]
        d_two_tied = after(d_two, qkv_one_x[0], down_y[0], out_y[0], *up_halves)
        d_last, sums_one = norm_back(
            d_two_tied, qkv_two_weight, normal1, scale1, first_gain, d_middle, base=partial
        )
        d_last_given = to_give(d_last)
        qkv_two = gradient(normed1, d_two, core, got=after(two_core, d_last))

        vectors = [
            sums_two[2],
            sums_one[0],
            sums_one[1],
            sums_two[0],
            sums_two[1],
            column_sums(d_out_low),
        ]
        joined_vectors = [
            jnp.concatenate([column_sums(d_one[index]), column_sums(d_two[index])])
            for index in (0, 2)
        ]
        vectors = [to_local(vector, 0, far) for vector in joined_vectors] + vectors
        table = jnp.stack([vector.reshape(devices, near_width) for vector in vectors], axis=1)
        up_sums = to_local(up_sums[0], 0, far)
        table = jnp.concatenate([table, up_sums.reshape(devices, -1, near_width)], axis=1)
        table = pad_small(table).reshape(width, 128).astype(jnp.bfloat16)
        table = add_half(send_half(table, "core"))
        qkv_two_x = send_half(jnp.concatenate([qkv_two, table], axis=1), "x")
        up_far = jnp.concatenate([*up_halves, add_half(out_y, d_last)], axis=1)
        up_far = send_far(up_far, far)
        qkv_one_y = send_half(
            add_half(qkv_one_x, d_last_given[0], qkv_two_x[0], up_far[0]), "ctx"
        )
        qkv_two_y = send_half(add_half(qkv_two_x), "ctx")
        qkv_one_far = send_far(add_half(qkv_one_y), far)
        qkv_two_far = send_far(add_half(qkv_two_y), far)

        sum_down = add_half(down_y, d_last_given[0]).astype(jnp.float32)
        sum_up = add_far(up_far, qkv_one_y[0])
        sum_up, sum_out = sum_up[:, :up_width], sum_up[:, up_width:]
        sum_one, sum_two = add_far(qkv_one_far), add_far(qkv_two_far)
        small_sums = sum_two[:small_rows, half_qkv : half_qkv + near_width]
        cut_qkv = lambda matrix: matrix[:, :half_qkv].reshape(shard_rows, 3, 1, half_width)
        sum_qkv = jnp.concatenate([cut_qkv(sum_one), cut_qkv(sum_two)], axis=2)
        sum_qkv = sum_qkv.reshape(shard_rows, 3 * width)
        input_grad = give(d_last_given)
        own = lambda index: small_sums[index]
        back = lambda matrix: refold(to_natural(matrix, 1, far))
        return (
            outputs,
            input_grad,
            refold(sum_qkv),
            own(0),
            own(1),
            back(sum_out),
            own(2),
            own(3),
            own(4),
            own(5),
            own(6),
            refold(sum_up),
            small_sums[8:].reshape(-1),
            back(sum_down),
            own(7),
        )

    return on_device


def solution(mesh):
    if mesh.shape["ctx"] == IMAGES and mesh.shape["dp"] % 4 == 0:
        far, axes = mesh.shape["dp"] // 4, ("z", "x", "core", "ctx")
        mesh = jax.sharding.Mesh(mesh.devices.reshape(far, 2, 2, IMAGES), axes)
        body = by_image(far)
    else:
        body, axes = on_device, ("dp", "ctx")
    matrix, vector = P(axes, None), P(axes)
    return jax.shard_map(
        body,
        mesh=mesh,
        in_specs=(matrix, matrix, vector, matrix, vector, vector, matrix)
        + (vector,) * 5
        + (matrix, vector, matrix, vector),
        out_specs=(matrix, matrix, matrix, vector, vector, matrix)
        + (vector,) * 5
        + (matrix, vector, matrix, vector),
        check_vma=False,
    )
```
